32 devices in a mesh: species: 2 (over x), dp: 16 (over z, y, core).
Axes of the slice: x: 2, y: 2, z: 4, core: 2. Of those that a mesh axis runs over, the one named last changes fastest.
Arguments:
- tokens: bfloat16 [32, 1024, 768], P(('species', 'dp')), may hold values from -6 to 6
- cotangent: bfloat16 [32, 1024, 768], P(('species', 'dp')), may hold values from -6 to 6
- lengths: int32 [32], P(('species', 'dp')), may hold values from 128 to 1024, as said below
- species_ids: int32 [32], P(('species', 'dp')), may hold values from 0 to 1
- species_table: bfloat16 [2, 768], replicated, may hold values from -3 to 3
- ln1_gain: bfloat16 [768], replicated, may hold values from 0.5 to 1.5
- ln1_bias: bfloat16 [768], replicated, may hold values from -2 to 2
- w_qkv: bfloat16 [768, 2304], replicated, may hold values from -0.21875 to 0.21875
- q_bias: bfloat16 [768], replicated, may hold values from -3 to 3
- v_bias: bfloat16 [768], replicated, may hold values from -3 to 3
- w_out: bfloat16 [768, 768], replicated, may hold values from -0.875 to 0.875
- out_bias: bfloat16 [768], replicated, may hold values from -3 to 3
- ln2_gain: bfloat16 [768], replicated, may hold values from 0.5 to 1.5
- ln2_bias: bfloat16 [768], replicated, may hold values from -2 to 2
- w_up: bfloat16 [768, 3072], replicated, may hold values from -0.21875 to 0.21875
- up_bias: bfloat16 [3072], replicated, may hold values from -3 to 3
- w_down: bfloat16 [3072, 768], replicated, may hold values from -0.109375 to 0.109375
- down_bias: bfloat16 [768], replicated, may hold values from -3 to 3
Outputs:
- mixed: bfloat16 [32, 1024, 768], P(('species', 'dp'))
- grad_tokens: bfloat16 [32, 1024, 768], P(('species', 'dp'))
- grad_species_table: float32 [2, 768], P(None, 'dp')
- grad_ln1_gain: float32 [768], P('dp')
- grad_ln1_bias: float32 [768], P('dp')
- grad_w_qkv: float32 [768, 2304], P('dp')
- grad_q_bias: float32 [768], P('dp')
- grad_v_bias: float32 [768], P('dp')
- grad_w_out: float32 [768, 768], P('dp')
- grad_out_bias: float32 [768], P('dp')
- grad_ln2_gain: float32 [768], P('dp')
- grad_ln2_bias: float32 [768], P('dp')
- grad_w_up: float32 [768, 3072], P('dp')
- grad_up_bias: float32 [3072], P('dp')
- grad_w_down: float32 [3072, 768], P('dp')
- grad_down_bias: float32 [768], P('dp')
The draws below stay inside these ranges and needn't reach their ends.
Inputs may be any that keep to these rules, and one draw needn't show every extreme that they name: `lengths`: some cell has exactly 1024 real genes and some exactly 128. `species_ids`: A cell's label does not depend on its stream; each stream may hold cells of either label.
All inputs are finite; a program needn't handle non-finite values.
Results may differ from the reference program's by a relative error of at most 0.012.
Values sent between devices are 32-bit elements; how exact they have to be, the bound alone decides.
No kernel may reach another device: no remote copies, remote signals or barrier semaphores. Data moves between devices by JAX's collectives and lax.ppermute only.
A program may use at most 384 MiB of HBM per device.

```python
import jax
import jax.numpy as jnp
from jax import lax

D = 768
HEADS = 12
HD = 64
FF = 3072
SEQ = 1024
CELLS = 32


def draw_lengths(key, part):
    key = jax.random.fold_in(key, 7)
    length_key, pick_key = jax.random.split(key)
    half_count = CELLS // 2
    position = jnp.arange(CELLS) % half_count
    upper_bound = SEQ // 4 + position * (SEQ - SEQ // 4) // max(half_count - 1, 1) + 1
    lengths_drawn = jax.random.randint(length_key, (CELLS,), SEQ // 8, upper_bound)
    shuffled = jax.random.permutation(pick_key, CELLS)
    lengths_drawn = jnp.where(jnp.arange(CELLS) == shuffled[0], SEQ, lengths_drawn)
    lengths_drawn = jnp.where(jnp.arange(CELLS) == shuffled[1], SEQ // 8, lengths_drawn)
    return lengths_drawn.astype(jnp.int32)


def plant(array, key, least, top_value):
    longest = array.shape.index(max(array.shape))
    spots = []
    for shift in (0, 1):
        where = [jax.random.randint(jax.random.fold_in(key, axis), (), 0, length) for axis, length in enumerate(array.shape)]
        where[longest] = (where[longest] + shift) % array.shape[longest]
        spots.append(tuple(where))
    return array.at[spots[0]].set(least).at[spots[1]].set(top_value)


def shard_levels(own_key, dims, cuts, smallest, largest):
    level, own = 1.0, jax.random.fold_in(own_key, 6)
    for axis_at, parts in cuts:
        heights = jnp.exp(jax.random.uniform(jax.random.fold_in(own, axis_at), (parts,), jnp.float32, smallest / len(cuts), largest / len(cuts)))
        level = level * jnp.repeat(heights, dims[axis_at] // parts).reshape([-1 if axis == axis_at else 1 for axis in range(len(dims))])
    return level


def bell_draw(rng, shape, width, bound, cuts=(), held_as=jnp.bfloat16):
    array = jax.random.normal(rng, shape, jnp.float32) * width
    if len(cuts) > 0:
        array = shard_levels(rng, shape, cuts, -0.22, 0.18) * array
    return jnp.clip(array, min=-bound, max=bound).astype(held_as)


def setup_inputs(seed: int = 0) -> dict:
    key_of = jax.random.split(jax.random.key(seed), 19)
    return {
        "tokens": bell_draw(key_of[0], (CELLS, SEQ, D), 1.0, 6.0, ((0, 32),)),
        "cotangent": bell_draw(key_of[1], (CELLS, SEQ, D), 1.0, 6.0, ((0, 32),)),
        "lengths": draw_lengths(jax.random.fold_in(key_of[18], 71), 0),
        "species_ids": plant(jax.random.randint(key_of[3], (CELLS,), 0, 2), jax.random.fold_in(key_of[3], 1), 0, 1).astype(jnp.int32),
        "species_table": bell_draw(key_of[4], (2, D), 0.5, 3.0),
        "ln1_gain": jnp.clip(1.0 + 0.1 * jax.random.normal(key_of[5], (D,), jnp.float32), 0.5, 1.5).astype(jnp.bfloat16),
        "ln1_bias": bell_draw(key_of[6], (D,), 0.3, 2.0),
        "w_qkv": bell_draw(key_of[7], (D, 3 * D), D ** -0.5, 0.21875),
        "q_bias": bell_draw(key_of[8], (D,), 0.5, 3.0),
        "v_bias": bell_draw(key_of[9], (D,), 0.5, 3.0),
        "w_out": bell_draw(key_of[10], (D, D), (D // 16) ** -0.5, 0.875),
        "out_bias": bell_draw(key_of[11], (D,), 0.5, 3.0),
        "ln2_gain": jnp.clip(1.0 + 0.1 * jax.random.normal(key_of[12], (D,), jnp.float32), 0.5, 1.5).astype(jnp.bfloat16),
        "ln2_bias": bell_draw(key_of[13], (D,), 0.3, 2.0),
        "w_up": bell_draw(key_of[14], (D, FF), D ** -0.5, 0.21875),
        "up_bias": bell_draw(key_of[15], (FF,), 0.5, 3.0),
        "w_down": bell_draw(key_of[16], (FF, D), FF ** -0.5, 0.109375),
        "down_bias": bell_draw(key_of[17], (D,), 0.5, 3.0),
    }


@jax.custom_vjp
def low(v):
    return lax.optimization_barrier(v.astype(jnp.bfloat16)).astype(jnp.float32)

@jax.custom_vjp
def low_back(v):
    return v

def low_keep(v):
    return (low(v), None)

def low_pass(kept, grad):
    return (grad,)

def back_keep(v):
    return (v, None)

def back_low(kept, grad):
    return (low(grad),)
low.defvjp(low_keep, low_pass)
low_back.defvjp(back_keep, back_low)

def matmul(left, right):
    return jnp.dot(left, right, precision=lax.Precision.HIGHEST)

def layer_norm(hidden, gain, offset):
    row_mean = lax.optimization_barrier(jnp.mean(hidden, axis=-1, keepdims=True))
    centred = hidden - row_mean
    variance = lax.optimization_barrier(jnp.mean(centred * centred, axis=-1, keepdims=True))
    return centred * lax.rsqrt(variance + 1e-05) * gain + offset

def attend_rows(query_rows, key_heads, value_heads, key_valid):
    scores = jnp.einsum('qhd,khd->hqk', query_rows, key_heads, precision=lax.Precision.HIGHEST) * HD ** (-0.5)
    scores = low_back(scores)
    scores = jnp.where(key_valid[None, None, :], scores, -1e+30)
    row_max = lax.optimization_barrier(jnp.max(scores, axis=-1, keepdims=True))
    exponent = jnp.exp(scores - row_max)
    soft_probs = exponent / lax.optimization_barrier(jnp.sum(exponent, axis=-1, keepdims=True))
    probs_low = low(soft_probs)
    return jnp.einsum('hqk,khd->qhd', probs_low, value_heads, precision=lax.Precision.HIGHEST)

def forward(tokens_row, onehot, key_valid, params):
    species_rows, gain_one, offset_one, w_qkv, q_bias, v_bias, w_out, out_bias, gain_two, offset_two, w_up, up_bias, w_down, down_bias = params
    stream_in = tokens_row + lax.optimization_barrier(jnp.sum(onehot[:, None] * species_rows, axis=0))
    normed_one = low(layer_norm(stream_in, gain_one, offset_one))
    projected = matmul(normed_one, w_qkv)
    queries = low(low_back(projected[:, :D] + q_bias)).reshape(SEQ, HEADS, HD)
    keys_all = low(low_back(projected[:, D:2 * D])).reshape(SEQ, HEADS, HD)
    values_all = low(low_back(projected[:, 2 * D:] + v_bias)).reshape(SEQ, HEADS, HD)
    block_rows = min(512, SEQ)
    query_blocks = queries.reshape(SEQ // block_rows, block_rows, HEADS, HD)
    attended = lax.map(jax.checkpoint(lambda query_rows: attend_rows(query_rows, keys_all, values_all, key_valid)), query_blocks)
    attended = low(low_back(attended.reshape(SEQ, D)))
    branch = low_back(matmul(attended, w_out) + out_bias)
    middle = stream_in + branch
    normed_two = low(layer_norm(middle, gain_two, offset_two))
    hidden_up = low_back(matmul(normed_two, w_up) + up_bias)
    activated = low(jax.nn.gelu(hidden_up, approximate=True))
    feed = low_back(matmul(activated, w_down) + down_bias)
    return middle + feed

def reference(tokens, cotangent, lengths, species_ids, species_table, ln1_gain, ln1_bias, w_qkv, q_bias, v_bias, w_out, out_bias, ln2_gain, ln2_bias, w_up, up_bias, w_down, down_bias):
    params = tuple((item.astype(jnp.float32) for item in (species_table, ln1_gain, ln1_bias, w_qkv, q_bias, v_bias, w_out, out_bias, ln2_gain, ln2_bias, w_up, up_bias, w_down, down_bias)))
    stream_counts = lax.optimization_barrier(jnp.sum(lengths.reshape(2, CELLS // 2).astype(jnp.float32), axis=1))
    stream_of = (jnp.arange(CELLS) // (CELLS // 2)).astype(jnp.int32)
    cell_weights = lengths.astype(jnp.float32) / (2.0 * stream_counts[stream_of])
    positions = jnp.arange(SEQ).astype(jnp.int32)

    def one_cell(accumulated, inputs):
        tokens_cell, cot_cell, length_cell, species_cell, weight_cell = inputs
        key_valid = positions < length_cell
        onehot = (jnp.arange(2).astype(jnp.int32) == species_cell).astype(jnp.float32)
        layer_out, pullback = jax.vjp(lambda tokens_row, all_params: forward(tokens_row, onehot, key_valid, all_params), tokens_cell.astype(jnp.float32), params)
        cot_masked = cot_cell.astype(jnp.float32) * key_valid[:, None].astype(jnp.float32)
        grad_in, grad_params = pullback(cot_masked)
        accumulated = jax.tree.map(lambda running, part: running + weight_cell * part, accumulated, grad_params)
        return (accumulated, (layer_out.astype(jnp.bfloat16), grad_in.astype(jnp.bfloat16)))
    zero_grads = jax.tree.map(jnp.zeros_like, params)
    summed, (mixed, grad_tokens) = lax.scan(one_cell, zero_grads, (tokens, cotangent, lengths, species_ids, cell_weights))
    return (mixed, grad_tokens, summed[0], summed[1], summed[2], summed[3], summed[4], summed[5], summed[6], summed[7], summed[8], summed[9], summed[10], summed[11], summed[12], summed[13])
```

```python
from functools import partial

import jax
import jax.numpy as jnp
from jax import lax
from jax.experimental import pallas as pl
from jax.experimental.pallas import tpu as pltpu
from jax.sharding import PartitionSpec as P

HEADS = 12
F32 = jnp.float32
BF = jnp.bfloat16
LOG2E = 1.4426950408889634
MIB = 1 << 20
LANES = 128


def nt(a, b):
    return lax.dot_general(a, b, (((1,), (1,)), ((), ())), preferred_element_type=F32)


def nn(a, b):
    return lax.dot_general(a, b, (((1,), (0,)), ((), ())), preferred_element_type=F32)


def call(body, name, grid, ins, outs, shapes, scratch=(), prefetch=0, mib=56, flops=0, nbytes=0):
    return pl.pallas_call(
        body,
        grid_spec=pltpu.PrefetchScalarGridSpec(
            num_scalar_prefetch=prefetch,
            grid=grid,
            in_specs=ins,
            out_specs=outs,
            scratch_shapes=list(scratch),
        ),
        out_shape=shapes,
        compiler_params=pltpu.CompilerParams(vmem_limit_bytes=mib * MIB),
        cost_estimate=pl.CostEstimate(flops=flops, bytes_accessed=nbytes, transcendentals=0),
        name=name,
    )


def const(*shape):
    return pl.BlockSpec(shape, lambda *a: (0,) * len(shape))


def sds(*shape, dt=F32):
    return jax.ShapeDtypeStruct(shape, dt)


def normed(x):
    c = x - jnp.mean(x, axis=-1, keepdims=True)
    r = lax.rsqrt(jnp.mean(c * c, axis=-1, keepdims=True) + 1e-5)
    return c * r, r


def norm_back(g, n, r, gain):
    e = g * gain
    return r * (e - jnp.mean(e, axis=-1, keepdims=True) - n * jnp.mean(e * n, axis=-1, keepdims=True))


def colsum(x):
    return jnp.sum(x, axis=0, keepdims=True)


def rows_of(rb, n):
    return pl.BlockSpec((rb, n), lambda i, *_: (i, 0))


def cols_of(n, rb):
    return pl.BlockSpec((n, rb), lambda i, *_: (0, i))


def qkv_body(tok, sp, g, b, w, bias, qkv, n1t):
    n, _ = normed(tok[...].astype(F32) + sp[...])
    nb = (n * g[...] + b[...]).astype(BF)
    n1t[...] = nb.T
    qkv[...] = (nn(nb, w[...]) + bias[...]).astype(BF)


def qkv_proj(tok, sp, g, b, w, bias, rb=256):
    S, D = tok.shape
    N = w.shape[1]
    return call(
        qkv_body, "qkv_proj", (S // rb,),
        [rows_of(rb, D), const(1, D), const(1, D), const(1, D), const(D, N), const(1, N)],
        [rows_of(rb, N), cols_of(D, rb)],
        [sds(S, N, dt=BF), sds(D, S, dt=BF)],
        flops=2 * S * D * N, nbytes=12 * MIB,
    )(tok, sp, g, b, w, bias)


def split2(x):
    hi = x.astype(BF)
    return hi, (x - hi.astype(F32)).astype(BF)


def split3(x):
    a = x.astype(BF).astype(F32)
    r = x - a
    b = r.astype(BF).astype(F32)
    return a, b, r - b


def attn_fwd_body(ln, q_ref, k_ref, v_ref, o_ref, of_ref, nl_ref, *, scale, qb, hd):
    S = q_ref.shape[0]
    lane = lax.broadcasted_iota(jnp.int32, (1, LANES), 1)
    row = lax.broadcasted_iota(jnp.int32, (S, 1), 0)
    mask = jnp.where(row < ln[0], 0.0, -1e30).astype(F32)
    kk = k_ref[...]
    kf = kk.astype(F32)
    vf = v_ref[...].astype(F32)
    hi, lo = split2(q_ref[...].astype(F32) * (scale * LOG2E))
    hi = hi.astype(F32)
    lo = lo.astype(F32)
    qa, ka, va = [], [], []
    for h in range(2):
        own = (lane // hd) == h
        aux = lane == (1 - h) * hd
        k2 = jnp.where(own, kf, jnp.where(aux, mask, 0.0)).astype(BF)
        ka.append(jnp.concatenate([kk, k2], axis=1))
        q1 = jnp.where(own, hi, 0.0).astype(BF)
        q2 = jnp.where(own, lo, jnp.where(aux, 1.0, 0.0)).astype(BF)
        qa.append(jnp.concatenate([q1, q2], axis=1))
        va.append(jnp.where(own, vf, 1.0).astype(BF))
    for b in range(S // qb):
        sl = slice(b * qb, (b + 1) * qb)
        outs, nls = [], []
        for h in range(2):
            s = nt(qa[h][sl], ka[h])
            m = jnp.max(s, axis=1, keepdims=True)
            p = jnp.exp2(s - m).astype(BF)
            o = nn(p, va[h])
            outs.append(o / pltpu.roll(o, hd, 1))
            nls.append(-(m + jnp.log2(o)))
        o = jnp.where(lane < hd, outs[0], outs[1])
        of_ref[sl, :] = o
        o_ref[sl, :] = o.astype(BF)
        nl_ref[sl, :] = jnp.where(lane < hd, nls[1], nls[0])


def attn_fwd(ln, qkv, scale, hd, qb=512):
    S, D = qkv.shape[0], qkv.shape[1] // 3
    n = D // LANES
    qb = min(qb, S)
    cb = lambda off: pl.BlockSpec((S, LANES), lambda p, l: (0, off + p))
    return call(
        partial(attn_fwd_body, scale=scale, qb=qb, hd=hd), "attn_fwd", (n,),
        [cb(0), cb(n), cb(2 * n)], [cb(0), cb(0), cb(0)],
        [sds(S, D, dt=BF), sds(S, D), sds(S, D)], prefetch=1,
        flops=16 * S * S * D, nbytes=12 * MIB,
    )(ln, qkv, qkv, qkv)


def attn_bwd_body(ln, q_ref, k_ref, v_ref, o_ref, do_ref, nl_ref, g_ref, dqt_ref, kt_ref, ka_ref, va_ref, *, scale, kb, hd):
    S = q_ref.shape[0]
    n = ln[0]
    lane = lax.broadcasted_iota(jnp.int32, (1, LANES), 1)
    row = lax.broadcasted_iota(jnp.int32, (S, 1), 0)
    mask = jnp.where(row < n, 0.0, -1e30).astype(F32)
    kk = k_ref[...]
    kf = kk.astype(F32)
    vf = v_ref[...].astype(F32)
    dof = do_ref[...].astype(F32)
    qf = q_ref[...].astype(F32)
    hi, lo = split2(qf * (scale * LOG2E))
    hi = hi.astype(F32)
    lo = lo.astype(F32)
    n0, n1, n2 = split3(nl_ref[...])
    do_o = dof * o_ref[...]
    kt_ref[...] = kf.T.astype(BF)
    qa, qo, da, do_own = [], [], [], []
    for h in range(2):
        own = (lane // hd) == h
        base = (1 - h) * hd
        three = (lane > base) & (lane < base + 4)
        pick = lambda a, b, c: jnp.where(lane == base + 1, a, jnp.where(lane == base + 2, b, jnp.where(lane == base + 3, c, 0.0)))
        ka_ref[h, :, 0:LANES] = kk
        ka_ref[h, :, LANES:] = jnp.where(own, kf, jnp.where(lane == base, mask, jnp.where(three, 1.0, 0.0))).astype(BF)
        va_ref[h] = jnp.where(own, vf, jnp.where(three, 1.0, 0.0)).astype(BF)
        q1 = jnp.where(own, hi, 0.0).astype(BF)
        q2 = jnp.where(own, lo, jnp.where(lane == base, 1.0, pick(n0, n1, n2))).astype(BF)
        qa.append(jnp.concatenate([q1, q2], axis=1))
        qo.append(jnp.where(own, qf, 0.0).astype(BF))
        delta = -jnp.sum(jnp.where(own, do_o, 0.0), axis=1, keepdims=True)
        do_own.append(jnp.where(own, dof, 0.0).astype(BF))
        da.append(jnp.where(own, dof, pick(*split3(delta))).astype(BF))
    for b in range(S // kb):
        sl = slice(b * kb, (b + 1) * kb)

        @pl.when(b * kb < n)
        def _():
            dv = dk = None
            for h in range(2):
                p = jnp.exp2(nt(ka_ref[h, sl, :], qa[h]))
                ds = (p * nt(va_ref[h, sl, :], da[h])).astype(BF)
                dvh = nn(p.astype(BF), do_own[h])
                dkh = nn(ds, qo[h])
                dv = dvh if h == 0 else dv + dvh
                dk = dkh if h == 0 else dk + dkh
                dqt = nn(kt_ref[h * hd : (h + 1) * hd, sl], ds)
                if b == 0:
                    dqt_ref[h * hd : (h + 1) * hd, :] = dqt
                else:
                    dqt_ref[h * hd : (h + 1) * hd, :] += dqt
            g_ref[1, sl, :] = (dk * scale).astype(BF)
            g_ref[2, sl, :] = dv.astype(BF)

        @pl.when(b * kb >= n)
        def _():
            g_ref[1, sl, :] = jnp.zeros((kb, LANES), BF)
            g_ref[2, sl, :] = jnp.zeros((kb, LANES), BF)

    g_ref[0] = (dqt_ref[...].T * scale).astype(BF)


def attn_bwd(ln, qkv, o, do, nl, first, count, scale, hd, kb=512):
    S, D = qkv.shape[0], qkv.shape[1] // 3
    n = D // LANES
    kb = min(kb, S)
    cb = lambda off: pl.BlockSpec((S, LANES), lambda p, l: (0, off + first + p))
    return call(
        partial(attn_bwd_body, scale=scale, kb=kb, hd=hd), "attn_bwd", (count,),
        [cb(0), cb(n), cb(2 * n), cb(0), cb(0), cb(0)],
        pl.BlockSpec((3, S, LANES), lambda p, l: (0, 0, p)),
        sds(3, S, count * LANES, dt=BF),
        scratch=[pltpu.VMEM((LANES, S), F32), pltpu.VMEM((LANES, S), BF), pltpu.VMEM((2, S, 2 * LANES), BF), pltpu.VMEM((2, S, LANES), BF)],
        prefetch=1, flops=40 * S * S * LANES * count, nbytes=2 * MIB * count,
    )(ln, qkv, qkv, qkv, o, do, nl)


def mid_body(ln, tok, sp, att, wo, ob, g2, b2, wu, ub, cot, wd, mid_o, n2t, act_o, actt, gu_o, gf_o, attt, ubs, dbs, *, fb):
    i = pl.program_id(0)
    rb = tok.shape[0]
    FF = wu.shape[1]
    a = att[...]
    attt[...] = a.T
    mid = tok[...].astype(F32) + sp[...] + nn(a, wo[...]) + ob[...]
    mid_o[...] = mid
    n, _ = normed(mid)
    n2 = (n * g2[...] + b2[...]).astype(BF)
    n2t[...] = n2.T
    row = i * rb + lax.broadcasted_iota(jnp.int32, (rb, 1), 0)
    gf = jnp.where(row < ln[0], cot[...].astype(F32), 0.0)
    gfb = gf.astype(BF)
    gf_o[...] = gfb

    @pl.when(i == 0)
    def _():
        ubs[...] = jnp.zeros_like(ubs)
        dbs[...] = jnp.zeros_like(dbs)

    dbs[...] += colsum(gf)
    C = 0.7978845608
    C2 = C * 0.044715
    for j in range(FF // fb):
        sl = slice(j * fb, (j + 1) * fb)
        u = nn(n2, wu[:, sl]) + ub[:, sl]
        da = nt(gfb, wd[sl, :])
        cu = C2 * (u * u)
        h = 0.5 * jnp.tanh(u * (cu + C)) + 0.5
        act = u * h
        ab = act.astype(BF)
        act_o[:, sl] = ab
        actt[sl, :] = ab.T
        gu = (da * (h + act * (1.0 - h) * (6.0 * cu + 2.0 * C))).astype(BF)
        gu_o[:, sl] = gu
        ubs[:, sl] += colsum(gu.astype(F32))


def mid_ffn(ln, tok, sp, att, wo, ob, g2, b2, wu, ub, cot, wd, rb=256, fb=768):
    S, D = tok.shape
    FF = wu.shape[1]
    r = partial(rows_of, rb)
    t = lambda n: cols_of(n, rb)
    return call(
        partial(mid_body, fb=fb), "mid_ffn", (S // rb,),
        [r(D), const(1, D), r(D), const(D, D), const(1, D), const(1, D), const(1, D), const(D, FF), const(1, FF), r(D), const(FF, D)],
        [r(D), t(D), r(FF), t(FF), r(FF), r(D), t(D), const(1, FF), const(1, D)],
        [sds(S, D), sds(D, S, dt=BF), sds(S, FF, dt=BF), sds(FF, S, dt=BF), sds(S, FF, dt=BF), sds(S, D, dt=BF), sds(D, S, dt=BF), sds(1, FF), sds(1, D)],
        prefetch=1, mib=60, flops=4 * S * D * FF + 2 * S * D * D, nbytes=40 * MIB,
    )(ln, tok, sp, att, wo, ob, g2, b2, wu, ub, cot, wd)


def back2_body(ln, gu, wu, mid, g2, cot, wo, gm_o, gb_o, ga_o, gs, bs, obs):
    i = pl.program_id(0)
    rb = mid.shape[0]
    gn = nt(gu[...], wu[...])
    n, r = normed(mid[...])
    row = i * rb + lax.broadcasted_iota(jnp.int32, (rb, 1), 0)
    gf = jnp.where(row < ln[0], cot[...].astype(F32), 0.0)
    gm = gf + norm_back(gn, n, r, g2[...])
    gm_o[...] = gm
    gb = gm.astype(BF)
    gb_o[...] = gb
    ga_o[...] = nt(gb, wo[...]).astype(BF)

    @pl.when(i == 0)
    def _():
        for s in (gs, bs, obs):
            s[...] = jnp.zeros_like(s)

    gs[...] += colsum(gn * n)
    bs[...] += colsum(gn)
    obs[...] += colsum(gb.astype(F32))


def back2(ln, gu, wu, mid, g2, cot, wo, rb=256):
    S, D = mid.shape
    FF = wu.shape[1]
    r = partial(rows_of, rb)
    return call(
        back2_body, "back2", (S // rb,),
        [r(FF), const(D, FF), r(D), const(1, D), r(D), const(D, D)],
        [r(D), r(D), r(D), const(1, D), const(1, D), const(1, D)],
        [sds(S, D), sds(S, D, dt=BF), sds(S, D, dt=BF), sds(1, D), sds(1, D), sds(1, D)],
        prefetch=1, flops=2 * S * D * FF + 2 * S * D * D, nbytes=20 * MIB,
    )(ln, gu, wu, mid, g2, cot, wo)


def back1_body(gqa, gqb, w, tok, sp, g1, gm, gt_o, gs, bs, ss, qs, vs):
    i = pl.program_id(0)
    D = tok.shape[1]
    Da = gqa.shape[2]
    gn = None
    for t in range(3):
        for ref, lo, hi in ((gqa, 0, Da), (gqb, Da, D)):
            part = nt(ref[t], w[:, t * D + lo : t * D + hi])
            gn = part if gn is None else gn + part
    n, r = normed(tok[...].astype(F32) + sp[...])
    g = gm[...] + norm_back(gn, n, r, g1[...])
    gt_o[...] = g.astype(BF)

    @pl.when(i == 0)
    def _():
        for s in (gs, bs, ss, qs, vs):
            s[...] = jnp.zeros_like(s)

    gs[...] += colsum(gn * n)
    bs[...] += colsum(gn)
    ss[...] += colsum(g)
    for ref, lo, hi in ((gqa, 0, Da), (gqb, Da, D)):
        qs[:, lo:hi] += colsum(ref[0].astype(F32))
        vs[:, lo:hi] += colsum(ref[2].astype(F32))


def back1(gqa, gqb, w, tok, sp, g1, gm, rb=256):
    S, D = tok.shape
    r = partial(rows_of, rb)
    g = lambda x: pl.BlockSpec((3, rb, x.shape[2]), lambda i: (0, i, 0))
    return call(
        back1_body, "back1", (S // rb,),
        [g(gqa), g(gqb), const(D, 3 * D), r(D), const(1, D), const(1, D), r(D)],
        [r(D)] + [const(1, D)] * 5,
        [sds(S, D, dt=BF)] + [sds(1, D)] * 5,
        flops=6 * S * D * D, nbytes=16 * MIB,
    )(gqa, gqb, w, tok, sp, g1, gm)


def mixed_body(act, wd, mid, db, o):
    o[...] = (mid[...] + nn(act[...], wd[...]) + db[...]).astype(BF)


def mixed_out(act, wd, mid, db, rb=256):
    S, D = mid.shape
    FF = wd.shape[0]
    r = partial(rows_of, rb)
    return call(
        mixed_body, "mixed_out", (S // rb,),
        [r(FF), const(FF, D), r(D), const(1, D)], r(D), sds(S, D, dt=BF),
        flops=2 * S * D * FF, nbytes=16 * MIB,
    )(act, wd, mid, db)


def wgrad_body(w, a, b, o):
    o[...] = nn(a[...], b[...]) * w[0]


def wgrad(weight, at, b, nb=768):
    M, S = at.shape
    N = b.shape[1]
    mb = min(M, 768)
    return call(
        wgrad_body, "wgrad", (M // mb, N // nb),
        [pl.BlockSpec((mb, S), lambda i, j, w: (i, 0)), pl.BlockSpec((S, nb), lambda i, j, w: (0, j))],
        pl.BlockSpec((mb, nb), lambda i, j, w: (i, j)), sds(M, N),
        prefetch=1, flops=2 * M * N * S, nbytes=4 * M * N,
    )(weight, at, b)


def half_wd_body(pos, w, a, b, *rest, first):
    res = nn(a[...].reshape(-1, a.shape[-1]), b[...]) * w[0]
    if first:
        (o,) = rest
        o[...] = res.reshape(o.shape)
        return
    recv, a_send, a_keep, b_send, b_keep = rest
    s = pl.program_id(0)
    nz, R, nb = a.shape[0], a.shape[3], b.shape[1]
    res = res.reshape(nz, R, nb) + recv[...].reshape(nz, R, nb)
    top = res[:, : R // 2]
    low, high = res[:, R // 2 : 3 * R // 4], res[:, 3 * R // 4 :]

    @pl.when(s == 0)
    def _():
        a_send[...] = top

    @pl.when(s == 1)
    def _():
        a_keep[...] = top

    up = pos[2] == 1
    b_keep[...] = jnp.where(up, high, low).reshape(b_keep.shape)
    b_send[...] = jnp.where(up, low, high).reshape(b_send.shape)


def half_wd(pos, weight, actt, gf, recv=None, nb=256):
    FF, S = actt.shape
    D = gf.shape[1]
    nz, R = 4, FF // 16
    av = actt.reshape(nz, 2, 2, R, S)
    first = recv is None
    yof = lambda s, p: jnp.where(s == 0, 1 - p[1], p[1])
    ins = [
        pl.BlockSpec((nz, 1, 1, R, S), lambda s, j, p, w: (0, yof(s, p), p[0], 0, 0)),
        pl.BlockSpec((S, nb), lambda s, j, p, w: (0, j)),
    ]
    full = pl.BlockSpec((nz, 1, R, nb), lambda s, j, p, w: (0, yof(s, p), 0, j))
    nj = D // nb
    if first:
        outs, shapes, args = full, sds(nz, 2, R, D), (av, gf)
    else:
        ins = ins + [full]
        h = pl.BlockSpec((nz, 1, R // 4, nb), lambda s, j, p, w: (0, yof(s, p), 0, j))
        outs = [
            pl.BlockSpec((nz, R // 2, nb), lambda s, j, p, w: (0, 0, jnp.where(s == 0, j, nj - 1))),
            pl.BlockSpec((nz, R // 2, nb), lambda s, j, p, w: (0, 0, jnp.where(s == 0, 0, j))),
            h, h,
        ]
        shapes = [sds(nz, R // 2, D)] * 2 + [sds(nz, 2, R // 4, D)] * 2
        args = (av, gf, recv)
    return call(
        partial(half_wd_body, first=first), "half_wd", (2, nj), ins, outs, shapes,
        prefetch=2, flops=FF * D * S, nbytes=12 * MIB,
    )(pos, weight, *args)


def half_wu_body(pos, w, a, b, *rest, first):
    res = nn(a[...].reshape(-1, a.shape[-1]), b[...]) * w[0]
    nz, R, nb = a.shape[0], a.shape[3], b.shape[1]
    res = res.reshape(nz, 2, R, nb)
    j = pl.program_id(0)
    if first:
        (o,) = rest
        o[...] = res.reshape(o.shape)
        return
    recv, a_send, a_keep, b_send, b_keep = rest
    res = res + recv[...].reshape(res.shape)
    up = pos[1] == 1

    @pl.when(j < 2)
    def _():
        a_keep[...] = jnp.where(up, res[:, 1], res[:, 0]).reshape(a_keep.shape)
        a_send[...] = jnp.where(up, res[:, 0], res[:, 1]).reshape(a_send.shape)

    @pl.when(j == 2 + pos[2])
    def _():
        b_keep[...] = res

    @pl.when(j == 3 - pos[2])
    def _():
        b_send[...] = res


def half_wu(pos, weight, n2t, gu, recv=None):
    D, S = n2t.shape
    FF = gu.shape[1]
    nz, R, nj = 4, D // 16, 4
    nb = FF // nj
    av = n2t.reshape(nz, 2, 2, R, S)
    first = recv is None
    ins = [
        pl.BlockSpec((nz, 2, 1, R, S), lambda j, p, w: (0, 0, p[0], 0, 0)),
        pl.BlockSpec((S, nb), lambda j, p, w: (0, j)),
    ]
    full = pl.BlockSpec((nz, 2, 1, R, nb), lambda j, p, w: (0, 0, j, 0, 0))
    if first:
        outs, shapes, args = full, sds(nz, 2, nj, R, nb), (av, gu)
    else:
        ins = ins + [full]
        h = pl.BlockSpec((nz, 1, R, nb), lambda j, p, w: (0, jnp.minimum(j, 1), 0, 0))
        outs = [h, h, const(nz, 2, R, nb), const(nz, 2, R, nb)]
        shapes = [sds(nz, 2, R, nb)] * 4
        args = (av, gu, recv)
    return call(
        partial(half_wu_body, first=first), "half_wu", (nj,), ins, outs, shapes,
        prefetch=2, flops=FF * D * S, nbytes=12 * MIB,
    )(pos, weight, *args)


def half_wo_body(pos, w, a, b, *rest, first):
    nz, R = a.shape[0], a.shape[3]
    res = (nn(a[...].reshape(-1, a.shape[-1]), b[...]) * w[0]).reshape(nz, 2, R, -1)
    if first:
        rest[0][...] = res
        return
    recv, send, keep = rest
    res = res + recv[...]
    up = pos[1] == 1
    keep[...] = jnp.where(up, res[:, 1], res[:, 0])
    send[...] = jnp.where(up, res[:, 0], res[:, 1])


def half_wo(pos, weight, attt, gb, recv=None):
    D, S = attt.shape
    N = gb.shape[1]
    nz, R = 4, D // 16
    av = attt.reshape(nz, 2, 2, R, S)
    first = recv is None
    ins = [pl.BlockSpec((nz, 2, 1, R, S), lambda j, p, w: (0, 0, p[0], 0, 0)), const(S, N)]
    full = const(nz, 2, R, N)
    if first:
        outs, shapes, args = full, sds(nz, 2, R, N), (av, gb)
    else:
        ins = ins + [full]
        outs = [const(nz, R, N)] * 2
        shapes = [sds(nz, R, N)] * 2
        args = (av, gb, recv)
    return call(
        partial(half_wo_body, first=first), "half_wo", (1,), ins, outs, shapes,
        prefetch=2, flops=N * D * S, nbytes=4 * MIB,
    )(pos, weight, *args)


QA, QB = 80, 32


def half_wq_body(pos, w, a, b, *rest, first):
    nz, R = a.shape[0], a.shape[3]
    av = a[...].reshape(-1, a.shape[-1])
    res = [(nn(av, b[t]) * w[0]).reshape(nz, 2, R, -1) for t in range(3)]
    res = jnp.concatenate(res, axis=2)
    if first:
        rest[0][...] = res
        return
    recv, a_send, a_keep, b_send, b_keep = rest
    res = res + recv[...]
    up = pos[1] == 1
    top = res[:, :, :QA]
    a_keep[...] = jnp.where(up, top[:, 1], top[:, 0])
    a_send[...] = jnp.where(up, top[:, 0], top[:, 1])
    low, high = res[:, :, QA : QA + QB], res[:, :, QA + QB :]
    up = pos[2] == 1
    b_keep[...] = jnp.where(up, high, low)
    b_send[...] = jnp.where(up, low, high)


def half_wq(pos, weight, n1t, gq, recv=None):
    D, S = n1t.shape
    N = gq.shape[2]
    nz, R = 4, D // 16
    av = n1t.reshape(nz, 2, 2, R, S)
    first = recv is None
    ins = [pl.BlockSpec((nz, 2, 1, R, S), lambda j, p, w: (0, 0, p[0], 0, 0)), const(3, S, N)]
    full = const(nz, 2, 3 * R, N)
    if first:
        outs, shapes, args = full, sds(nz, 2, 3 * R, N), (av, gq)
    else:
        ins = ins + [full]
        outs = [const(nz, QA, N)] * 2 + [const(nz, 2, QB, N)] * 2
        shapes = [sds(nz, QA, N)] * 2 + [sds(nz, 2, QB, N)] * 2
        args = (av, gq, recv)
    return call(
        partial(half_wq_body, first=first), "half_wq", (1,), ins, outs, shapes,
        prefetch=2, flops=3 * N * D * S, nbytes=8 * MIB,
    )(pos, weight, *args)


def flip(bit):
    return [(i, i ^ bit) for i in range(16)]


def move(a, axis):
    if axis == "x":
        return lax.ppermute(a, "species", [(0, 1), (1, 0)])
    return lax.ppermute(a, "dp", flip({"core": 1, "y": 2, "z1": 4, "z2": 8}[axis]))


def pick(a, index, axis):
    return lax.dynamic_index_in_dim(a, index, axis, keepdims=False)


def z_steps(a, zl, zh):
    a = a.reshape((2, 2) + a.shape[1:])
    a = pick(a, zl, 1) + move(pick(a, 1 - zl, 1), "z1")
    return pick(a, zh, 0) + move(pick(a, 1 - zh, 0), "z2")


def sum_yzx(send, keep, zl, zh):
    a = keep + move(send, "y")
    a = z_steps(a, zl, zh)
    return a + move(a, "x")


def sum_xyz(send, keep, x, y, zl, zh):
    b = keep + move(send, "x")
    b = pick(b, y, 1) + move(pick(b, 1 - y, 1), "y")
    b = z_steps(b, zl, zh)
    other = move(b, "x")
    low = jnp.where(x == 0, b, other)
    high = jnp.where(x == 0, other, b)
    return low, high


def local(
    tokens, cotangent, lengths, species_ids, species_table, ln1_gain, ln1_bias, w_qkv, q_bias, v_bias,
    w_out, out_bias, ln2_gain, ln2_bias, w_up, up_bias, w_down, down_bias, *, dp_size,
):
    D = tokens.shape[2]
    hd = D // HEADS
    scale = hd ** (-0.5)
    FF = w_up.shape[1]
    tok = tokens[0]
    cot = cotangent[0]
    paired = dp_size == 16
    dp = lax.axis_index("dp")
    x = lax.axis_index("species")
    core, y, zl, zh = dp % 2, (dp // 2) % 2, (dp // 4) % 2, dp // 8
    length_float = lengths[0].astype(F32)
    if paired:
        count = jnp.full((8, LANES), length_float)
        for axis in ("core", "y", "z1", "z2"):
            count = count + move(count, axis)
        count = count[0, 0]
    else:
        count = lax.psum(length_float, "dp")
    weight = (length_float / (2.0 * count)).reshape(1)
    onehot = (jnp.arange(2) == species_ids[0]).astype(F32)
    sp = jnp.sum(onehot[:, None] * species_table.astype(F32), axis=0)[None]
    row = lambda v: v.astype(F32)[None]
    qkv_bias = jnp.concatenate([q_bias.astype(F32), jnp.zeros((D,), F32), v_bias.astype(F32)])[None]

    qkv, n1t = qkv_proj(tok, sp, row(ln1_gain), row(ln1_bias), w_qkv, qkv_bias)
    att, att_f32, nl = attn_fwd(lengths, qkv, scale, hd)
    mid, n2t, act, actt, gu, gf, attt, up_part, down_part = mid_ffn(
        lengths, tok, sp, att, w_out, row(out_bias), row(ln2_gain), row(ln2_bias), w_up, row(up_bias), cot, w_down
    )
    mine = jnp.stack([core, y, x]).astype(jnp.int32)
    theirs = jnp.stack([1 - core, y, x]).astype(jnp.int32)
    if paired:
        wd_other = move(half_wd(theirs, weight, actt, gf), "core")
        wu_other = move(half_wu(theirs, weight, n2t, gu), "core")
    gm, gb, ga, ln2g_part, ln2b_part, ob_part = back2(lengths, gu, w_up, mid, row(ln2_gain), cot, w_out)
    if paired:
        wd = half_wd(mine, weight, actt, gf, wd_other)
        wu = half_wu(mine, weight, n2t, gu, wu_other)
        wo_other = move(half_wo(theirs, weight, attt, gb), "core")
    pairs = D // LANES
    gqa = attn_bwd(lengths, qkv, att_f32, ga, nl, 0, pairs // 2, scale, hd)
    if paired:
        wqa_other = move(half_wq(theirs, weight, n1t, gqa), "core")
        wo = half_wo(mine, weight, attt, gb, wo_other)
    gqb = attn_bwd(lengths, qkv, att_f32, ga, nl, pairs // 2, pairs - pairs // 2, scale, hd)
    if paired:
        wqb_other = move(half_wq(theirs, weight, n1t, gqb), "core")
        wqa = half_wq(mine, weight, n1t, gqa, wqa_other)
    gt, ln1g_part, ln1b_part, sp_part, qb_part, vb_part = back1(gqa, gqb, w_qkv, tok, sp, row(ln1_gain), gm)
    if paired:
        wqb = half_wq(mine, weight, n1t, gqb, wqb_other)
    mixed = mixed_out(act, w_down, mid, row(down_bias))

    small = jnp.concatenate(
        [onehot[:, None] * sp_part, ln1g_part, ln1b_part, qb_part, vb_part, ob_part, ln2g_part, ln2b_part, down_part, up_part.reshape(-1, D)],
        axis=0,
    ) * weight[0]
    if paired:
        small = jnp.concatenate([small, jnp.zeros((-small.shape[0] % 8, D), F32)], axis=0)
        for axis in ("core", "y", "z1", "z2", "x"):
            small = small + move(small, axis)
    else:
        small = lax.psum(small, ("dp", "species"))
    n = D // dp_size
    share = lambda r: lax.dynamic_slice_in_dim(small[r], dp * n, n)
    species = lax.dynamic_slice_in_dim(small[:2], dp * n, n, axis=1)
    up_share = lax.dynamic_slice_in_dim(small[10 : 10 + FF // D].reshape(-1), dp * (FF // dp_size), FF // dp_size)

    if paired:
        args = (x, y, zl, zh)
        a = sum_yzx(wd[0], wd[1], zl, zh)
        b0, b1 = sum_xyz(wd[2], wd[3], *args)
        g_down = jnp.concatenate([a, b0, b1], axis=0)
        a = sum_yzx(wu[0], wu[1], zl, zh)
        b0, b1 = sum_xyz(wu[2], wu[3], *args)
        g_up = jnp.concatenate([a[0], a[1], b0, b1], axis=1)
        g_out = sum_yzx(wo[0], wo[1], zl, zh)
        qs = []
        for wq in (wqa, wqb):
            a = sum_yzx(wq[0], wq[1], zl, zh)
            b0, b1 = sum_xyz(wq[2], wq[3], *args)
            qs.append(jnp.concatenate([a, b0, b1], axis=0).reshape(3, n, -1))
        g_qkv = jnp.concatenate([qs[h][t] for t in range(3) for h in range(2)], axis=1)
    else:
        def total(part):
            return lax.psum(lax.psum_scatter(part, "dp", scatter_dimension=0, tiled=True), "species")

        g_down = total(wgrad(weight, actt, gf))
        g_up = total(wgrad(weight, n2t, gu))
        g_out = total(wgrad(weight, attt, gb))
        gq = jnp.concatenate([g for t in range(3) for g in (gqa[t], gqb[t])], axis=1)
        g_qkv = total(wgrad(weight, n1t, gq))
    return (
        mixed[None], gt[None], species, share(2), share(3), g_qkv, share(4), share(5), g_out, share(6),
        share(7), share(8), g_up, up_share, g_down, share(9),
    )


def solution(mesh):
    cells = P(("species", "dp"), None, None)
    scalars = P(("species", "dp"))
    in_specs = (cells, cells, scalars, scalars) + (P(),) * 14
    v, m = P("dp"), P("dp", None)
    out_specs = (cells, cells, P(None, "dp"), v, v, m, v, v, m, v, v, v, m, v, m, v)
    return jax.shard_map(
        partial(local, dp_size=mesh.shape["dp"]), mesh=mesh, in_specs=in_specs, out_specs=out_specs, check_vma=False
    )
```

```python
from functools import partial

import jax
import jax.numpy as jnp
from jax import lax
from jax.experimental import pallas as pl
from jax.experimental.pallas import tpu as pltpu
from jax.sharding import PartitionSpec as P

HEADS = 12
F32 = jnp.float32
BF = jnp.bfloat16
LOG2E = 1.4426950408889634
MIB = 1 << 20
LANES = 128


def nt(a, b):
    return lax.dot_general(a, b, (((1,), (1,)), ((), ())), preferred_element_type=F32)


def nn(a, b):
    return lax.dot_general(a, b, (((1,), (0,)), ((), ())), preferred_element_type=F32)


def call(body, name, grid, ins, outs, shapes, scratch=(), prefetch=0, mib=56, after=(), us=10):
    n = len(ins)
    extra = len(after)

    def run(*refs):
        return body(*refs[: prefetch + n], *refs[prefetch + n + extra :])

    f = pl.pallas_call(
        run,
        grid_spec=pltpu.PrefetchScalarGridSpec(
            num_scalar_prefetch=prefetch,
            grid=grid,
            in_specs=list(ins) + [pl.BlockSpec(memory_space=pl.ANY)] * extra,
            out_specs=outs,
            scratch_shapes=list(scratch),
        ),
        out_shape=shapes,
        compiler_params=pltpu.CompilerParams(vmem_limit_bytes=mib * MIB),
        cost_estimate=pl.CostEstimate(flops=1000, bytes_accessed=int(us * 2e4), transcendentals=0),
        name=name,
    )
    return lambda *args: f(*args, *after)


def const(*shape):
    return pl.BlockSpec(shape, lambda *a: (0,) * len(shape))


def sds(*shape, dt=F32):
    return jax.ShapeDtypeStruct(shape, dt)


def normed(x):
    c = x - jnp.mean(x, axis=-1, keepdims=True)
    r = lax.rsqrt(jnp.mean(c * c, axis=-1, keepdims=True) + 1e-5)
    return c * r, r


def norm_back(g, n, r, gain):
    e = g * gain
    return r * (e - jnp.mean(e, axis=-1, keepdims=True) - n * jnp.mean(e * n, axis=-1, keepdims=True))


def colsum(x):
    return jnp.sum(x, axis=0, keepdims=True)


def rows_of(rb, n):
    return pl.BlockSpec((rb, n), lambda i, *_: (i, 0))


def cols_of(n, rb):
    return pl.BlockSpec((n, rb), lambda i, *_: (0, i))


LEN, ID, CORE, Y, ZL, ZH, X = range(7)


def vec(ref):
    return ref[...].astype(F32)[None, :]


def species_row(info, table):
    rows = table[...].astype(F32)
    return jnp.where(info[ID] == 0, rows[0:1], rows[1:2])


def qkv_body(info, tok, tab, g, b, w, qb, vb, qkv, n1t):
    n, _ = normed(tok[...].astype(F32) + species_row(info, tab))
    nb = (n * vec(g) + vec(b)).astype(BF)
    n1t[...] = nb.T
    bias = jnp.concatenate([vec(qb), jnp.zeros((1, tok.shape[1]), F32), vec(vb)], axis=1)
    qkv[...] = (nn(nb, w[...]) + bias).astype(BF)


def qkv_proj(info, tok, tab, g, b, w, qb, vb, rb=256):
    S, D = tok.shape
    N = w.shape[1]
    return call(
        qkv_body, "qkv_proj", (S // rb,),
        [rows_of(rb, D), const(2, D), const(D), const(D), const(D, N), const(D), const(D)],
        [rows_of(rb, N), cols_of(D, rb)],
        [sds(S, N, dt=BF), sds(D, S, dt=BF)], prefetch=1, us=9,
    )(info, tok, tab, g, b, w, qb, vb)


def split2(x):
    hi = x.astype(BF)
    return hi, (x - hi.astype(F32)).astype(BF)


def split3(x):
    a = x.astype(BF).astype(F32)
    r = x - a
    b = r.astype(BF).astype(F32)
    return a, b, r - b


def attn_fwd_body(ln, q_ref, k_ref, v_ref, o_ref, of_ref, nl_ref, *, scale, qb, hd):
    S = q_ref.shape[0]
    lane = lax.broadcasted_iota(jnp.int32, (1, LANES), 1)
    row = lax.broadcasted_iota(jnp.int32, (S, 1), 0)
    mask = jnp.where(row < ln[0], 0.0, -1e30).astype(F32)
    kk = k_ref[...]
    kf = kk.astype(F32)
    vf = v_ref[...].astype(F32)
    hi, lo = split2(q_ref[...].astype(F32) * (scale * LOG2E))
    hi = hi.astype(F32)
    lo = lo.astype(F32)
    qa, ka, va = [], [], []
    for h in range(2):
        own = (lane // hd) == h
        aux = lane == (1 - h) * hd
        k2 = jnp.where(own, kf, jnp.where(aux, mask, 0.0)).astype(BF)
        ka.append(jnp.concatenate([kk, k2], axis=1))
        q1 = jnp.where(own, hi, 0.0).astype(BF)
        q2 = jnp.where(own, lo, jnp.where(aux, 1.0, 0.0)).astype(BF)
        qa.append(jnp.concatenate([q1, q2], axis=1))
        va.append(jnp.where(own, vf, 1.0).astype(BF))
    for b in range(S // qb):
        sl = slice(b * qb, (b + 1) * qb)
        outs, nls = [], []
        for h in range(2):
            s = nt(qa[h][sl], ka[h])
            m = jnp.max(s, axis=1, keepdims=True)
            p = jnp.exp2(s - m).astype(BF)
            o = nn(p, va[h])
            outs.append(o / pltpu.roll(o, hd, 1))
            nls.append(-(m + jnp.log2(o)))
        o = jnp.where(lane < hd, outs[0], outs[1])
        of_ref[sl, :] = o
        o_ref[sl, :] = o.astype(BF)
        nl_ref[sl, :] = jnp.where(lane < hd, nls[1], nls[0])


def attn_fwd(ln, qkv, scale, hd, qb=512):
    S, D = qkv.shape[0], qkv.shape[1] // 3
    n = D // LANES
    qb = min(qb, S)
    cb = lambda off: pl.BlockSpec((S, LANES), lambda p, l: (0, off + p))
    return call(
        partial(attn_fwd_body, scale=scale, qb=qb, hd=hd), "attn_fwd", (n,),
        [cb(0), cb(n), cb(2 * n)], [cb(0), cb(0), cb(0)],
        [sds(S, D, dt=BF), sds(S, D), sds(S, D)], prefetch=1, us=22,
    )(ln, qkv, qkv, qkv)


def attn_bwd_body(ln, q_ref, k_ref, v_ref, o_ref, do_ref, nl_ref, g_ref, dqt_ref, kt_ref, ka_ref, va_ref, *, scale, kb, hd):
    S = q_ref.shape[0]
    n = ln[0]
    lane = lax.broadcasted_iota(jnp.int32, (1, LANES), 1)
    row = lax.broadcasted_iota(jnp.int32, (S, 1), 0)
    mask = jnp.where(row < n, 0.0, -1e30).astype(F32)
    kk = k_ref[...]
    kf = kk.astype(F32)
    vf = v_ref[...].astype(F32)
    dof = do_ref[...].astype(F32)
    qf = q_ref[...].astype(F32)
    hi, lo = split2(qf * (scale * LOG2E))
    hi = hi.astype(F32)
    lo = lo.astype(F32)
    n0, n1, n2 = split3(nl_ref[...])
    do_o = dof * o_ref[...]
    kt_ref[...] = kf.T.astype(BF)
    qa, qo, da, do_own = [], [], [], []
    for h in range(2):
        own = (lane // hd) == h
        base = (1 - h) * hd
        three = (lane > base) & (lane < base + 4)
        pick = lambda a, b, c: jnp.where(lane == base + 1, a, jnp.where(lane == base + 2, b, jnp.where(lane == base + 3, c, 0.0)))
        ka_ref[h, :, 0:LANES] = kk
        ka_ref[h, :, LANES:] = jnp.where(own, kf, jnp.where(lane == base, mask, jnp.where(three, 1.0, 0.0))).astype(BF)
        va_ref[h] = jnp.where(own, vf, jnp.where(three, 1.0, 0.0)).astype(BF)
        q1 = jnp.where(own, hi, 0.0).astype(BF)
        q2 = jnp.where(own, lo, jnp.where(lane == base, 1.0, pick(n0, n1, n2))).astype(BF)
        qa.append(jnp.concatenate([q1, q2], axis=1))
        qo.append(jnp.where(own, qf, 0.0).astype(BF))
        delta = -jnp.sum(jnp.where(own, do_o, 0.0), axis=1, keepdims=True)
        do_own.append(jnp.where(own, dof, 0.0).astype(BF))
        da.append(jnp.where(own, dof, pick(*split3(delta))).astype(BF))
    for b in range(S // kb):
        sl = slice(b * kb, (b + 1) * kb)

        @pl.when(b * kb < n)
        def _():
            dv = dk = None
            for h in range(2):
                p = jnp.exp2(nt(ka_ref[h, sl, :], qa[h]))
                ds = (p * nt(va_ref[h, sl, :], da[h])).astype(BF)
                dvh = nn(p.astype(BF), do_own[h])
                dkh = nn(ds, qo[h])
                dv = dvh if h == 0 else dv + dvh
                dk = dkh if h == 0 else dk + dkh
                dqt = nn(kt_ref[h * hd : (h + 1) * hd, sl], ds)
                if b == 0:
                    dqt_ref[h * hd : (h + 1) * hd, :] = dqt
                else:
                    dqt_ref[h * hd : (h + 1) * hd, :] += dqt
            g_ref[1, sl, :] = (dk * scale).astype(BF)
            g_ref[2, sl, :] = dv.astype(BF)

        @pl.when(b * kb >= n)
        def _():
            g_ref[1, sl, :] = jnp.zeros((kb, LANES), BF)
            g_ref[2, sl, :] = jnp.zeros((kb, LANES), BF)

    g_ref[0] = (dqt_ref[...].T * scale).astype(BF)


def attn_bwd(ln, qkv, o, do, nl, first, count, scale, hd, kb=512, after=()):
    S, D = qkv.shape[0], qkv.shape[1] // 3
    n = D // LANES
    kb = min(kb, S)
    cb = lambda off: pl.BlockSpec((S, LANES), lambda p, l: (0, off + first + p))
    return call(
        partial(attn_bwd_body, scale=scale, kb=kb, hd=hd), "attn_bwd", (count,),
        [cb(0), cb(n), cb(2 * n), cb(0), cb(0), cb(0)],
        pl.BlockSpec((3, S, LANES), lambda p, l: (0, 0, p)),
        sds(3, S, count * LANES, dt=BF),
        scratch=[pltpu.VMEM((LANES, S), F32), pltpu.VMEM((LANES, S), BF), pltpu.VMEM((2, S, 2 * LANES), BF), pltpu.VMEM((2, S, LANES), BF)],
        prefetch=1, after=after, us=9 * count,
    )(ln, qkv, qkv, qkv, o, do, nl)


def mid1_body(info, tok, tab, att, wo, ob, g2, b2, wu, ub, cot, mid_o, n2t, act_o, actt, gp_o, gf_o, attt, dbs, *, fb):
    i = pl.program_id(0)
    rb = tok.shape[0]
    FF = wu.shape[1]
    a = att[...]
    attt[...] = a.T
    mid = tok[...].astype(F32) + species_row(info, tab) + nn(a, wo[...]) + vec(ob)
    mid_o[...] = mid
    n, _ = normed(mid)
    n2 = (n * vec(g2) + vec(b2)).astype(BF)
    n2t[...] = n2.T
    row = i * rb + lax.broadcasted_iota(jnp.int32, (rb, 1), 0)
    gf = jnp.where(row < info[LEN], cot[...].astype(F32), 0.0)
    gf_o[...] = gf.astype(BF)

    @pl.when(i == 0)
    def _():
        dbs[...] = jnp.zeros_like(dbs)

    dbs[...] += colsum(gf)
    C = 0.7978845608
    C2 = C * 0.044715
    bias = vec(ub)
    for j in range(FF // fb):
        sl = slice(j * fb, (j + 1) * fb)
        u = nn(n2, wu[:, sl]) + bias[:, sl]
        cu = C2 * (u * u)
        h = 0.5 * jnp.tanh(u * (cu + C)) + 0.5
        act = u * h
        ab = act.astype(BF)
        act_o[:, sl] = ab
        actt[sl, :] = ab.T
        gp_o[:, sl] = (h + act * (1.0 - h) * (6.0 * cu + 2.0 * C)).astype(BF)


def mid1(info, tok, tab, att, wo, ob, g2, b2, wu, ub, cot, rb=256, fb=768):
    S, D = tok.shape
    FF = wu.shape[1]
    r = partial(rows_of, rb)
    t = lambda n: cols_of(n, rb)
    return call(
        partial(mid1_body, fb=fb), "mid1", (S // rb,),
        [r(D), const(2, D), r(D), const(D, D), const(D), const(D), const(D), const(D, FF), const(FF), r(D)],
        [r(D), t(D), r(FF), t(FF), r(FF), r(D), t(D), const(1, D)],
        [sds(S, D), sds(D, S, dt=BF), sds(S, FF, dt=BF), sds(FF, S, dt=BF), sds(S, FF, dt=BF), sds(S, D, dt=BF), sds(D, S, dt=BF), sds(1, D)],
        prefetch=1, us=21,
    )(info, tok, tab, att, wo, ob, g2, b2, wu, ub, cot)


def mid2_body(gf, wd, gp, gu_o, ubs):
    gu = (nt(gf[...], wd[...]) * gp[...].astype(F32)).astype(BF)
    gu_o[...] = gu
    ubs[...] = colsum(gu.astype(F32))


def mid2(gf, wd, gp, nb=512, after=()):
    S, D = gf.shape
    FF = wd.shape[0]
    t = lambda n: pl.BlockSpec((n, nb), lambda j: (0, j))
    return call(
        mid2_body, "mid2", (FF // nb,),
        [const(S, D), pl.BlockSpec((nb, D), lambda j: (j, 0)), t(S)],
        [t(S), t(1)], [sds(S, FF, dt=BF), sds(1, FF)], after=after,
    )(gf, wd, gp)


def back2_body(ln, gu, wu, mid, g2, cot, wo, gm_o, gb_o, ga_o, gs, bs, obs):
    i = pl.program_id(0)
    rb = mid.shape[0]
    gn = nt(gu[...], wu[...])
    n, r = normed(mid[...])
    row = i * rb + lax.broadcasted_iota(jnp.int32, (rb, 1), 0)
    gf = jnp.where(row < ln[0], cot[...].astype(F32), 0.0)
    gm = gf + norm_back(gn, n, r, vec(g2))
    gm_o[...] = gm
    gb = gm.astype(BF)
    gb_o[...] = gb
    ga_o[...] = nt(gb, wo[...]).astype(BF)

    @pl.when(i == 0)
    def _():
        for s in (gs, bs, obs):
            s[...] = jnp.zeros_like(s)

    gs[...] += colsum(gn * n)
    bs[...] += colsum(gn)
    obs[...] += colsum(gb.astype(F32))


def back2(ln, gu, wu, mid, g2, cot, wo, rb=256, after=()):
    S, D = mid.shape
    FF = wu.shape[1]
    r = partial(rows_of, rb)
    return call(
        back2_body, "back2", (S // rb,),
        [r(FF), const(D, FF), r(D), const(D), r(D), const(D, D)],
        [r(D), r(D), r(D), const(1, D), const(1, D), const(1, D)],
        [sds(S, D), sds(S, D, dt=BF), sds(S, D, dt=BF), sds(1, D), sds(1, D), sds(1, D)],
        prefetch=1, after=after, us=16,
    )(ln, gu, wu, mid, g2, cot, wo)


def back1_body(info, *refs):
    *gq, w, tok, tab, g1, gm, gt_o, gs, bs, ss, qs, vs = refs
    i = pl.program_id(0)
    D = tok.shape[1]
    gn = None
    for t in range(3):
        whole = jnp.concatenate([g[t] for g in gq], axis=1)
        part = nt(whole, w[:, t * D : (t + 1) * D])
        gn = part if gn is None else gn + part
    n, r = normed(tok[...].astype(F32) + species_row(info, tab))
    g = gm[...] + norm_back(gn, n, r, vec(g1))
    gt_o[...] = g.astype(BF)

    @pl.when(i == 0)
    def _():
        for s in (gs, bs, ss, qs, vs):
            s[...] = jnp.zeros_like(s)

    gs[...] += colsum(gn * n)
    bs[...] += colsum(gn)
    ss[...] += colsum(g)
    qs[...] += colsum(jnp.concatenate([g[0] for g in gq], axis=1).astype(F32))
    vs[...] += colsum(jnp.concatenate([g[2] for g in gq], axis=1).astype(F32))


def back1(info, gq, w, tok, tab, g1, gm, rb=256, after=()):
    S, D = tok.shape
    r = partial(rows_of, rb)
    return call(
        back1_body, "back1", (S // rb,),
        [pl.BlockSpec((3, rb, g.shape[2]), lambda i, n: (0, i, 0)) for g in gq] + [const(D, 3 * D), r(D), const(2, D), const(D), r(D)],
        [r(D)] + [const(1, D)] * 5,
        [sds(S, D, dt=BF)] + [sds(1, D)] * 5, prefetch=1, after=after,
    )(info, *gq, w, tok, tab, g1, gm)


def mixed_body(act, wd, mid, db, o):
    o[...] = (mid[...] + nn(act[...], wd[...]) + vec(db)).astype(BF)


def mixed_out(act, wd, mid, db, first=0, count=4, rb=256, after=()):
    D = mid.shape[1]
    FF = wd.shape[0]
    r = lambda n: pl.BlockSpec((rb, n), lambda i: (first + i, 0))
    return call(
        mixed_body, "mixed_out", (count,),
        [r(FF), const(FF, D), r(D), const(D)], rows_of(rb, D), sds(count * rb, D, dt=BF), after=after,
    )(act, wd, mid, db)


def wgrad_body(w, a, b, o):
    o[...] = nn(a[...], b[...]) * w[0]


def wgrad(weight, at, b, nb=768, after=()):
    M, S = at.shape
    N = b.shape[1]
    mb = min(M, 768)
    return call(
        wgrad_body, "wgrad", (M // mb, N // nb),
        [pl.BlockSpec((mb, S), lambda i, j, w: (i, 0)), pl.BlockSpec((S, nb), lambda i, j, w: (0, j))],
        pl.BlockSpec((mb, nb), lambda i, j, w: (i, j)), sds(M, N),
        prefetch=1, after=after,
    )(weight, at, b)


NUMBER = {"y": Y, "zl": ZL, "zh": ZH, "x": X}
STEP = {"y": 2, "zl": 4, "zh": 8, "x": 16}
ORDERS = (("y", "zl", "zh", "x"), ("x", "y", "zl", "zh"))


def wide_body(info, w, lhs, *refs, counts, steps):
    n = sum(counts)
    rhs, (other, own, held) = refs[:n], refs[n:]
    j = pl.program_id(0)
    R = lhs.shape[2]
    nb = other.shape[-1]
    cores = (1 - info[CORE], info[CORE])

    @pl.when(j == 0)
    def _():
        rel = lambda a, k: 1 - info[a] if k else info[a]
        for i, core in enumerate(cores):
            for p in range(8):
                block = rel(ZH, p & 1) * 4 + rel(ZL, (p >> 1) & 1) * 2 + rel(Y, (p >> 2) & 1)
                held[(i * 8 + p) * R : (i * 8 + p + 1) * R, :] = lhs[block, core]

    at, lo = 0, 0
    for many, count in zip(counts, steps):
        parts = rhs[at : at + many]

        def run(parts=parts):
            for g in range(3):
                if len(parts[0].shape) == 3:
                    b = [r[g] for r in parts]
                    b = b[0] if many == 1 else jnp.concatenate(b, axis=1)
                else:
                    b = parts[0][:, g * nb : (g + 1) * nb]
                res = (nn(held[...], b) * w[0]).reshape(2, 8, 2, R // 2, nb)
                for i, (core, out) in enumerate(zip(cores, (other, own))):
                    for p in range(8):
                        for half in range(2):
                            far = 1 - info[X] if half else info[X]
                            place = jnp.where(core == 0, p * 2 + far, far * 8 + p)
                            out[place, g] = res[i, p, half]

        pl.when((j >= lo) & (j < lo + count))(run)
        at, lo = at + many, lo + count


def wide_grad(info, weight, lhs, rhs, nb, after=()):
    S = lhs.shape[1]
    R = lhs.shape[0] // 16
    ins, steps, lo = [const(8, 2, R, S)], [], 0
    for group in rhs:
        if group[0].ndim == 3:
            count = 1
            ins += [const(*b.shape) for b in group]
        else:
            count = group[0].shape[1] // (3 * nb)
            ins.append(pl.BlockSpec((S, 3 * nb), lambda j, *_, lo=lo, n=count: (0, jnp.clip(j - lo, 0, n - 1))))
        steps.append(count)
        lo += count
    return call(
        partial(wide_body, counts=[len(g) for g in rhs], steps=steps), "wide_grad", (lo,), ins,
        [pl.BlockSpec((16, 3, R // 2, nb), lambda j, *_: (0, j, 0, 0))] * 2,
        [sds(16, 3 * lo, R // 2, nb)] * 2,
        scratch=[pltpu.VMEM((16 * R, S), BF)], prefetch=2, after=after,
    )(info, weight, lhs.reshape(8, 2, R, S), *[b for g in rhs for b in g])


def to_core(a):
    return lax.ppermute(a, "dp", [(i, i ^ 1) for i in range(16)])


def to_stream(a):
    return lax.ppermute(a, "species", [(0, 1), (1, 0)])


def tie(a, *after):
    return lax.optimization_barrier((a, *after))[0] if after else a


class Sum:
    def __init__(self, parts):
        other, own = parts
        self.own, self.got = own, to_core(other)
        self.step = 0

    def start(self, *after):
        n = self.own.shape[0] // 2
        got = tie(self.got, *after)
        self.send = self.own[n:] + got[n:]
        self.keep = [self.own[:n], got[:n]]
        return self.send

    def advance(self, *after):
        bits = [STEP[order[self.step]] for order in ORDERS]
        got = lax.ppermute(self.send, ("species", "dp"), [(i, i ^ bits[i & 1]) for i in range(32)])
        got = tie(got, *after)
        self.step += 1
        n = got.shape[0] // 2
        terms = self.keep + [got]
        add = lambda lo, hi: sum((t[lo:hi] for t in terms[1:]), terms[0][lo:hi])
        if n:
            self.send, self.keep = add(n, 2 * n), [add(0, n)]
        else:
            self.send = add(0, 1)
            self.keep = [self.send]
        return self.send

    def finish(self):
        while self.step < 4:
            self.advance()
        unit = self.send[0]
        return unit, to_stream(unit)


def join_body(info, *refs, n, moves):
    pairs = [(refs[2 * i], refs[2 * i + 1]) for i in range(n)]
    outs = refs[2 * n :]
    up = info[X] == 1
    for i, g, o, c in moves:
        a, b = pairs[i][0][g], pairs[i][1][g]
        U, nb = a.shape
        outs[o][:U, c : c + nb] = jnp.where(up, b, a)
        outs[o][U:, c : c + nb] = jnp.where(up, a, b)


def join(info, pairs, moves, shapes, after=()):
    arrays = [a if a.ndim == 3 else a[None] for p in pairs for a in p]
    return call(
        partial(join_body, n=len(pairs), moves=moves), "join", (1,),
        [const(*a.shape) for a in arrays], [const(*s) for s in shapes], [sds(*s) for s in shapes], prefetch=1, after=after,
    )(info, *arrays)


def stack_body(info, w, *refs):
    *parts, o = refs
    D = o.shape[1]
    sp, rest, up = parts[0], parts[1:-1], parts[-1]
    o[...] = jnp.zeros_like(o)
    for k in range(2):
        o[k : k + 1, :] = jnp.where(info[ID] == k, sp[...], 0.0) * w[0]
    for k, r in enumerate(rest):
        o[2 + k : 3 + k, :] = r[...] * w[0]
    for k in range(up.shape[1] // D):
        o[2 + len(rest) + k : 3 + len(rest) + k, :] = up[:, k * D : (k + 1) * D] * w[0]


def stack(info, weight, parts):
    D = parts[0].shape[1]
    rows = 1 + sum(p.shape[1] // D for p in parts)
    rows += -rows % 8
    return call(
        stack_body, "stack", (1,), [const(*p.shape) for p in parts], const(rows, D), sds(rows, D), prefetch=2, us=1,
    )(info, weight, *parts)


def flat(chunks):
    return jnp.concatenate(list(chunks), axis=1)


def local(
    tokens, cotangent, lengths, species_ids, species_table, ln1_gain, ln1_bias, w_qkv, q_bias, v_bias,
    w_out, out_bias, ln2_gain, ln2_bias, w_up, up_bias, w_down, down_bias, *, dp_size,
):
    D = tokens.shape[2]
    hd = D // HEADS
    scale = hd ** (-0.5)
    FF = w_up.shape[1]
    tok = tokens[0]
    cot = cotangent[0]
    paired = dp_size == 16
    dp = lax.axis_index("dp")
    x = lax.axis_index("species")
    info = jnp.stack([lengths[0], species_ids[0], dp % 2, (dp // 2) % 2, (dp // 4) % 2, dp // 8, x]).astype(jnp.int32)
    length_float = lengths[0].astype(F32)

    qkv, n1t = qkv_proj(info, tok, species_table, ln1_gain, ln1_bias, w_qkv, q_bias, v_bias)
    att, att_f32, nl = attn_fwd(info, qkv, scale, hd)
    mid, n2t, act, actt, gp, gf, attt, down_part = mid1(
        info, tok, species_table, att, w_out, out_bias, ln2_gain, ln2_bias, w_up, up_bias, cot
    )
    back = lambda first, count, after: attn_bwd(info, qkv, att_f32, ga, nl, first, count, scale, hd, after=after)
    if paired:
        count = jnp.full((8, LANES), length_float)
        for bit, token in zip((1, 2, 4, 8), (None, n1t, nl, None)):
            count = count + lax.ppermute(count, "dp", [(i, i ^ bit) for i in range(16)])
            if token is not None:
                count = tie(count, token)
        weight = (length_float / (2.0 * count[0, 0])).reshape(1)
        nb = D // 3
        scatter = lambda a: lax.psum_scatter(a, "dp", scatter_dimension=0, tiled=True)
        part = wgrad(weight, actt, gf)
        down = scatter(part)
        gu, up_part = mid2(gf, w_down, gp, after=[part])
        up = Sum(wide_grad(info, weight, n2t, [[gu]], nb))
        gm, gb, ga, ln2g_part, ln2b_part, ob_part = back2(info, gu, w_up, mid, ln2_gain, cot, w_out, after=[up.own])
        up.start(ob_part)
        gq0 = back(0, 2, [up.send])
        part = wgrad(weight, attt, gb, after=[gq0])
        out_part = part
        gq1 = back(2, 2, [part])
        up.advance(gq1)
        gq2 = back(4, 1, [gq1, up.send])
        first = Sum(wide_grad(info, weight, n1t, [[gq0], [gq1]], nb, after=[gq2]))
        gq3 = back(5, 1, [first.own])
        first.start(gq3)
        up.advance(gq3)
        last = Sum(wide_grad(info, weight, n1t, [[gq2, gq3]], nb, after=[first.send, up.send]))
        out = scatter(tie(out_part, down, last.own))
        gt, ln1g_part, ln1b_part, sp_part, qb_part, vb_part = back1(
            info, [gq0, gq1, gq2, gq3], w_qkv, tok, species_table, ln1_gain, gm, after=[last.own]
        )
        last.start(sp_part)
        first.advance(sp_part)
        up.advance(sp_part)
        small = stack(info, weight, [sp_part, ln1g_part, ln1b_part, qb_part, vb_part, ob_part, ln2g_part, ln2b_part, down_part, up_part])
        hop = lambda a, bit, *after: a + tie(lax.ppermute(a, "dp", [(i, i ^ bit) for i in range(16)]), *after)
        mixed_a = mixed_out(act, w_down, mid, down_bias, 0, 2, after=[last.send, first.send, up.send, small])
        last.advance(mixed_a)
        first.advance(mixed_a)
        up.advance(mixed_a)
        small = hop(small, 1, mixed_a)
        mixed_b = mixed_out(act, w_down, mid, down_bias, 2, 2, after=[last.send, first.send, up.send, small])
        last.advance(mixed_b)
        first.advance(mixed_b)
        small = hop(small, 2, mixed_b)
        (g_up,) = join(info, [up.finish()], [(0, g, 0, g * nb) for g in range(FF // nb)], [(D // dp_size, FF)], after=[last.send, first.send, small])
        last.advance(g_up)
        first.advance(g_up)
        small = hop(small, 4, g_up)
        last.advance()
        small = hop(small, 8, last.send)
        small = small + to_stream(small)
        mixed = jnp.concatenate([mixed_a, mixed_b], axis=0)
    else:
        weight = (length_float / (2.0 * lax.psum(length_float, "dp"))).reshape(1)
        gu, up_part = mid2(gf, w_down, gp)
        gm, gb, ga, ln2g_part, ln2b_part, ob_part = back2(info, gu, w_up, mid, ln2_gain, cot, w_out)
        gqs = [back(0, D // LANES, ())]
        gt, ln1g_part, ln1b_part, sp_part, qb_part, vb_part = back1(info, gqs, w_qkv, tok, species_table, ln1_gain, gm)
        mixed = mixed_out(act, w_down, mid, down_bias)
        small = stack(info, weight, [sp_part, ln1g_part, ln1b_part, qb_part, vb_part, ob_part, ln2g_part, ln2b_part, down_part, up_part])
        small = lax.psum(lax.psum(small, "dp"), "species")
    n = D // dp_size
    share = lambda r: lax.dynamic_slice_in_dim(small[r], dp * n, n)
    species = lax.dynamic_slice_in_dim(small[:2], dp * n, n, axis=1)
    up_share = lax.dynamic_slice_in_dim(small[10 : 10 + FF // D].reshape(-1), dp * (FF // dp_size), FF // dp_size)

    if paired:
        g_down = down + to_stream(down)
        g_out = out + to_stream(out)
        moves = [(0, 3 * h + t, 0, t * D + h * nb) for t in range(3) for h in range(2)]
        moves += [(1, t, 0, t * D + 2 * nb) for t in range(3)]
        (g_qkv,) = join(info, [first.finish(), last.finish()], moves, [(n, 3 * D)])
    else:
        def total(part):
            return lax.psum(lax.psum_scatter(part, "dp", scatter_dimension=0, tiled=True), "species")

        g_down = total(wgrad(weight, actt, gf))
        g_up = total(wgrad(weight, n2t, gu))
        g_out = total(wgrad(weight, attt, gb))
        g_qkv = total(wgrad(weight, n1t, flat(gqs[0])))
    return (
        mixed[None], gt[None], species, share(2), share(3), g_qkv, share(4), share(5), g_out, share(6),
        share(7), share(8), g_up, up_share, g_down, share(9),
    )


def solution(mesh):
    cells = P(("species", "dp"), None, None)
    scalars = P(("species", "dp"))
    in_specs = (cells, cells, scalars, scalars) + (P(),) * 14
    v, m = P("dp"), P("dp", None)
    out_specs = (cells, cells, P(None, "dp"), v, v, m, v, v, m, v, v, v, m, v, m, v)
    return jax.shard_map(
        partial(local, dp_size=mesh.shape["dp"]), mesh=mesh, in_specs=in_specs, out_specs=out_specs, check_vma=False
    )
```

```python
from functools import partial

import jax
import jax.numpy as jnp
from jax import lax
from jax.experimental import pallas as pl
from jax.experimental.pallas import tpu as pltpu
from jax.sharding import PartitionSpec as P

HEADS = 12
F32 = jnp.float32
BF = jnp.bfloat16
LOG2E = 1.4426950408889634
MIB = 1 << 20
LANES = 128


def nt(a, b):
    return lax.dot_general(a, b, (((1,), (1,)), ((), ())), preferred_element_type=F32)


def nn(a, b):
    return lax.dot_general(a, b, (((1,), (0,)), ((), ())), preferred_element_type=F32)


def tie(a, *after):
    return lax.optimization_barrier((a, *after))[0] if after else a


def call(body, name, grid, ins, outs, shapes, scratch=(), prefetch=0, mib=56, after=(), us=0.05):
    f = pl.pallas_call(
        body,
        grid_spec=pltpu.PrefetchScalarGridSpec(
            num_scalar_prefetch=prefetch, grid=grid, in_specs=ins, out_specs=outs, scratch_shapes=list(scratch)
        ),
        out_shape=shapes,
        compiler_params=pltpu.CompilerParams(vmem_limit_bytes=mib * MIB),
        cost_estimate=pl.CostEstimate(flops=1000, bytes_accessed=int(us * 3.2e6), transcendentals=0),
        name=name,
    )
    return lambda first, *rest: f(tie(first, *after), *rest)


def const(*shape):
    return pl.BlockSpec(shape, lambda *a: (0,) * len(shape))


def sds(*shape, dt=F32):
    return jax.ShapeDtypeStruct(shape, dt)


def normed(x):
    c = x - jnp.mean(x, axis=-1, keepdims=True)
    r = lax.rsqrt(jnp.mean(c * c, axis=-1, keepdims=True) + 1e-5)
    return c * r, r


def norm_back(g, n, r, gain):
    e = g * gain
    return r * (e - jnp.mean(e, axis=-1, keepdims=True) - n * jnp.mean(e * n, axis=-1, keepdims=True))


def colsum(x):
    return jnp.sum(x, axis=0, keepdims=True)


def rows_of(rb, n):
    return pl.BlockSpec((rb, n), lambda i, *_: (i, 0))


def cols_of(n, rb):
    return pl.BlockSpec((n, rb), lambda i, *_: (0, i))


LEN, ID, CORE, Y, ZL, ZH, X = range(7)


def vec(ref):
    return ref[...].astype(F32)[None, :]


def species_row(info, table):
    rows = table[...].astype(F32)
    return jnp.where(info[ID] == 0, rows[0:1], rows[1:2])


def qkv_body(info, tok, tab, g, b, w, qb, vb, qkv, n1t):
    n, _ = normed(tok[...].astype(F32) + species_row(info, tab))
    nb = (n * vec(g) + vec(b)).astype(BF)
    n1t[...] = nb.T
    bias = jnp.concatenate([vec(qb), jnp.zeros((1, tok.shape[1]), F32), vec(vb)], axis=1)
    qkv[...] = (nn(nb, w[...]) + bias).astype(BF)


def qkv_proj(info, tok, tab, g, b, w, qb, vb, rb=256):
    S, D = tok.shape
    N = w.shape[1]
    return call(
        qkv_body, "qkv_proj", (S // rb,),
        [rows_of(rb, D), const(2, D), const(D), const(D), const(D, N), const(D), const(D)],
        [rows_of(rb, N), cols_of(D, rb)],
        [sds(S, N, dt=BF), sds(D, S, dt=BF)], prefetch=1,
    )(info, tok, tab, g, b, w, qb, vb)


def split2(x):
    hi = x.astype(BF)
    return hi, (x - hi.astype(F32)).astype(BF)


def split3(x):
    a = x.astype(BF).astype(F32)
    r = x - a
    b = r.astype(BF).astype(F32)
    return a, b, r - b


def attn_fwd_body(ln, q_ref, k_ref, v_ref, o_ref, of_ref, nl_ref, *, scale, qb, hd):
    S = q_ref.shape[0]
    lane = lax.broadcasted_iota(jnp.int32, (1, LANES), 1)
    row = lax.broadcasted_iota(jnp.int32, (S, 1), 0)
    mask = jnp.where(row < ln[0], 0.0, -1e30).astype(F32)
    kk = k_ref[...]
    kf = kk.astype(F32)
    vf = v_ref[...].astype(F32)
    hi, lo = split2(q_ref[...].astype(F32) * (scale * LOG2E))
    hi = hi.astype(F32)
    lo = lo.astype(F32)
    qa, ka, va = [], [], []
    for h in range(2):
        own = (lane // hd) == h
        aux = lane == (1 - h) * hd
        k2 = jnp.where(own, kf, jnp.where(aux, mask, 0.0)).astype(BF)
        ka.append(jnp.concatenate([kk, k2], axis=1))
        q1 = jnp.where(own, hi, 0.0).astype(BF)
        q2 = jnp.where(own, lo, jnp.where(aux, 1.0, 0.0)).astype(BF)
        qa.append(jnp.concatenate([q1, q2], axis=1))
        va.append(jnp.where(own, vf, 1.0).astype(BF))
    for b in range(S // qb):
        sl = slice(b * qb, (b + 1) * qb)
        outs, nls = [], []
        for h in range(2):
            s = nt(qa[h][sl], ka[h])
            m = jnp.max(s, axis=1, keepdims=True)
            p = jnp.exp2(s - m).astype(BF)
            o = nn(p, va[h])
            outs.append(o / pltpu.roll(o, hd, 1))
            nls.append(-(m + jnp.log2(o)))
        o = jnp.where(lane < hd, outs[0], outs[1])
        of_ref[sl, :] = o
        o_ref[sl, :] = o.astype(BF)
        nl_ref[sl, :] = jnp.where(lane < hd, nls[1], nls[0])


def attn_fwd(ln, qkv, scale, hd, qb=512, after=()):
    S, D = qkv.shape[0], qkv.shape[1] // 3
    n = D // LANES
    qb = min(qb, S)
    cb = lambda off: pl.BlockSpec((S, LANES), lambda p, l: (0, off + p))
    return call(
        partial(attn_fwd_body, scale=scale, qb=qb, hd=hd), "attn_fwd", (n,),
        [cb(0), cb(n), cb(2 * n)], [cb(0), cb(0), cb(0)],
        [sds(S, D, dt=BF), sds(S, D), sds(S, D)], prefetch=1, after=after,
    )(ln, qkv, qkv, qkv)


def attn_bwd_body(ln, q_ref, k_ref, v_ref, o_ref, do_ref, nl_ref, g_ref, dqt_ref, kt_ref, ka_ref, va_ref, *, scale, kb, hd):
    S = q_ref.shape[0]
    n = ln[0]
    lane = lax.broadcasted_iota(jnp.int32, (1, LANES), 1)
    row = lax.broadcasted_iota(jnp.int32, (S, 1), 0)
    mask = jnp.where(row < n, 0.0, -1e30).astype(F32)
    kk = k_ref[...]
    kf = kk.astype(F32)
    vf = v_ref[...].astype(F32)
    dof = do_ref[...].astype(F32)
    qf = q_ref[...].astype(F32)
    hi, lo = split2(qf * (scale * LOG2E))
    hi = hi.astype(F32)
    lo = lo.astype(F32)
    n0, n1, n2 = split3(nl_ref[...])
    do_o = dof * o_ref[...]
    kt_ref[...] = kf.T.astype(BF)
    qa, qo, da, do_own = [], [], [], []
    for h in range(2):
        own = (lane // hd) == h
        base = (1 - h) * hd
        three = (lane > base) & (lane < base + 4)
        pick = lambda a, b, c: jnp.where(lane == base + 1, a, jnp.where(lane == base + 2, b, jnp.where(lane == base + 3, c, 0.0)))
        ka_ref[h, :, 0:LANES] = kk
        ka_ref[h, :, LANES:] = jnp.where(own, kf, jnp.where(lane == base, mask, jnp.where(three, 1.0, 0.0))).astype(BF)
        va_ref[h] = jnp.where(own, vf, jnp.where(three, 1.0, 0.0)).astype(BF)
        q1 = jnp.where(own, hi, 0.0).astype(BF)
        q2 = jnp.where(own, lo, jnp.where(lane == base, 1.0, pick(n0, n1, n2))).astype(BF)
        qa.append(jnp.concatenate([q1, q2], axis=1))
        qo.append(jnp.where(own, qf, 0.0).astype(BF))
        delta = -jnp.sum(jnp.where(own, do_o, 0.0), axis=1, keepdims=True)
        do_own.append(jnp.where(own, dof, 0.0).astype(BF))
        da.append(jnp.where(own, dof, pick(*split3(delta))).astype(BF))
    for b in range(S // kb):
        sl = slice(b * kb, (b + 1) * kb)

        @pl.when(b * kb < n)
        def _():
            dv = dk = None
            for h in range(2):
                p = jnp.exp2(nt(ka_ref[h, sl, :], qa[h]))
                ds = (p * nt(va_ref[h, sl, :], da[h])).astype(BF)
                dvh = nn(p.astype(BF), do_own[h])
                dkh = nn(ds, qo[h])
                dv = dvh if h == 0 else dv + dvh
                dk = dkh if h == 0 else dk + dkh
                dqt = nn(kt_ref[h * hd : (h + 1) * hd, sl], ds)
                if b == 0:
                    dqt_ref[h * hd : (h + 1) * hd, :] = dqt
                else:
                    dqt_ref[h * hd : (h + 1) * hd, :] += dqt
            g_ref[1, sl, :] = (dk * scale).astype(BF)
            g_ref[2, sl, :] = dv.astype(BF)

        @pl.when(b * kb >= n)
        def _():
            g_ref[1, sl, :] = jnp.zeros((kb, LANES), BF)
            g_ref[2, sl, :] = jnp.zeros((kb, LANES), BF)

    g_ref[0] = (dqt_ref[...].T * scale).astype(BF)


def attn_bwd(ln, qkv, o, do, nl, first, count, scale, hd, kb=512, after=()):
    S, D = qkv.shape[0], qkv.shape[1] // 3
    n = D // LANES
    kb = min(kb, S)
    cb = lambda off: pl.BlockSpec((S, LANES), lambda p, l: (0, off + first + p))
    return call(
        partial(attn_bwd_body, scale=scale, kb=kb, hd=hd), "attn_bwd", (count,),
        [cb(0), cb(n), cb(2 * n), cb(0), cb(0), cb(0)],
        pl.BlockSpec((3, S, LANES), lambda p, l: (0, 0, p)),
        sds(3, S, count * LANES, dt=BF),
        scratch=[pltpu.VMEM((LANES, S), F32), pltpu.VMEM((LANES, S), BF), pltpu.VMEM((2, S, 2 * LANES), BF), pltpu.VMEM((2, S, LANES), BF)],
        prefetch=1, after=after, us=9 * count if count == 1 else 0.05,
    )(ln, qkv, qkv, qkv, o, do, nl)


def mid1_body(info, tok, tab, att, wo, ob, g2, b2, wu, ub, cot, mid_o, n2t, act_o, actt, gp_o, gf_o, attt, dbs, *, fb):
    i = pl.program_id(0)
    rb = tok.shape[0]
    FF = wu.shape[1]
    a = att[...]
    attt[...] = a.T
    mid = tok[...].astype(F32) + species_row(info, tab) + nn(a, wo[...]) + vec(ob)
    mid_o[...] = mid
    n, _ = normed(mid)
    n2 = (n * vec(g2) + vec(b2)).astype(BF)
    n2t[...] = n2.T
    row = i * rb + lax.broadcasted_iota(jnp.int32, (rb, 1), 0)
    gf = jnp.where(row < info[LEN], cot[...].astype(F32), 0.0)
    gf_o[...] = gf.astype(BF)

    @pl.when(i == 0)
    def _():
        dbs[...] = jnp.zeros_like(dbs)

    dbs[...] += colsum(gf)
    C = 0.7978845608
    C2 = C * 0.044715
    bias = vec(ub)
    for j in range(FF // fb):
        sl = slice(j * fb, (j + 1) * fb)
        u = nn(n2, wu[:, sl]) + bias[:, sl]
        cu = C2 * (u * u)
        h = 0.5 * jnp.tanh(u * (cu + C)) + 0.5
        act = u * h
        ab = act.astype(BF)
        act_o[:, sl] = ab
        actt[sl, :] = ab.T
        gp_o[:, sl] = (h + act * (1.0 - h) * (6.0 * cu + 2.0 * C)).astype(BF)


def mid1(info, tok, tab, att, wo, ob, g2, b2, wu, ub, cot, rb=256, fb=768):
    S, D = tok.shape
    FF = wu.shape[1]
    r = partial(rows_of, rb)
    t = lambda n: cols_of(n, rb)
    return call(
        partial(mid1_body, fb=fb), "mid1", (S // rb,),
        [r(D), const(2, D), r(D), const(D, D), const(D), const(D), const(D), const(D, FF), const(FF), r(D)],
        [r(D), t(D), r(FF), t(FF), r(FF), r(D), t(D), const(1, D)],
        [sds(S, D), sds(D, S, dt=BF), sds(S, FF, dt=BF), sds(FF, S, dt=BF), sds(S, FF, dt=BF), sds(S, D, dt=BF), sds(D, S, dt=BF), sds(1, D)],
        prefetch=1,
    )(info, tok, tab, att, wo, ob, g2, b2, wu, ub, cot)


def mid2_body(gf, wd, gp, gu_o, ubs):
    gu = (nt(gf[...], wd[...]) * gp[...].astype(F32)).astype(BF)
    gu_o[...] = gu
    ubs[...] = colsum(gu.astype(F32))


def mid2(gf, wd, gp, nb=512, after=()):
    S, D = gf.shape
    FF = wd.shape[0]
    t = lambda n: pl.BlockSpec((n, nb), lambda j: (0, j))
    return call(
        mid2_body, "mid2", (FF // nb,),
        [const(S, D), pl.BlockSpec((nb, D), lambda j: (j, 0)), t(S)],
        [t(S), t(1)], [sds(S, FF, dt=BF), sds(1, FF)], after=after,
    )(gf, wd, gp)


def back2_body(ln, gu, wu, mid, g2, cot, wo, gm_o, gb_o, ga_o, gs, bs, obs):
    i = pl.program_id(0)
    rb = mid.shape[0]
    gn = nt(gu[...], wu[...])
    n, r = normed(mid[...])
    row = i * rb + lax.broadcasted_iota(jnp.int32, (rb, 1), 0)
    gf = jnp.where(row < ln[0], cot[...].astype(F32), 0.0)
    gm = gf + norm_back(gn, n, r, vec(g2))
    gm_o[...] = gm
    gb = gm.astype(BF)
    gb_o[...] = gb
    ga_o[...] = nt(gb, wo[...]).astype(BF)

    @pl.when(i == 0)
    def _():
        for s in (gs, bs, obs):
            s[...] = jnp.zeros_like(s)

    gs[...] += colsum(gn * n)
    bs[...] += colsum(gn)
    obs[...] += colsum(gb.astype(F32))


def back2(ln, gu, wu, mid, g2, cot, wo, rb=256, after=()):
    S, D = mid.shape
    FF = wu.shape[1]
    r = partial(rows_of, rb)
    return call(
        back2_body, "back2", (S // rb,),
        [r(FF), const(D, FF), r(D), const(D), r(D), const(D, D)],
        [r(D), r(D), r(D), const(1, D), const(1, D), const(1, D)],
        [sds(S, D), sds(S, D, dt=BF), sds(S, D, dt=BF), sds(1, D), sds(1, D), sds(1, D)],
        prefetch=1, after=after,
    )(ln, gu, wu, mid, g2, cot, wo)


def back1_body(info, *refs):
    *gq, w, tok, tab, g1, gm, gt_o, gs, bs, ss, qs, vs = refs
    i = pl.program_id(0)
    D = tok.shape[1]
    gn = None
    for t in range(3):
        whole = jnp.concatenate([g[t] for g in gq], axis=1)
        part = nt(whole, w[:, t * D : (t + 1) * D])
        gn = part if gn is None else gn + part
    n, r = normed(tok[...].astype(F32) + species_row(info, tab))
    g = gm[...] + norm_back(gn, n, r, vec(g1))
    gt_o[...] = g.astype(BF)

    @pl.when(i == 0)
    def _():
        for s in (gs, bs, ss, qs, vs):
            s[...] = jnp.zeros_like(s)

    gs[...] += colsum(gn * n)
    bs[...] += colsum(gn)
    ss[...] += colsum(g)
    qs[...] += colsum(jnp.concatenate([g[0] for g in gq], axis=1).astype(F32))
    vs[...] += colsum(jnp.concatenate([g[2] for g in gq], axis=1).astype(F32))


def back1(info, gq, w, tok, tab, g1, gm, rb=256, after=()):
    S, D = tok.shape
    r = partial(rows_of, rb)
    return call(
        back1_body, "back1", (S // rb,),
        [pl.BlockSpec((3, rb, g.shape[2]), lambda i, n: (0, i, 0)) for g in gq] + [const(D, 3 * D), r(D), const(2, D), const(D), r(D)],
        [r(D)] + [const(1, D)] * 5,
        [sds(S, D, dt=BF)] + [sds(1, D)] * 5, prefetch=1, after=after, us=11,
    )(info, *gq, w, tok, tab, g1, gm)


def mixed_body(act, wd, mid, db, o):
    o[...] = (mid[...] + nn(act[...], wd[...]) + vec(db)).astype(BF)


def mixed_out(act, wd, mid, db, first=0, count=4, rb=256, after=()):
    D = mid.shape[1]
    FF = wd.shape[0]
    r = lambda n: pl.BlockSpec((rb, n), lambda i: (first + i, 0))
    return call(
        mixed_body, "mixed_out", (count,),
        [r(FF), const(FF, D), r(D), const(D)], rows_of(rb, D), sds(count * rb, D, dt=BF), after=after,
    )(act, wd, mid, db)


def wgrad_body(w, a, b, o):
    o[...] = nn(a[...], b[...]) * w[0]


def wgrad(weight, at, b, nb=768, after=()):
    M, S = at.shape
    N = b.shape[1]
    mb = min(M, 768)
    return call(
        wgrad_body, "wgrad", (M // mb, N // nb),
        [pl.BlockSpec((mb, S), lambda i, j, w: (i, 0)), pl.BlockSpec((S, nb), lambda i, j, w: (0, j))],
        pl.BlockSpec((mb, nb), lambda i, j, w: (i, j)), sds(M, N),
        prefetch=1, after=after,
    )(weight, at, b)


NUMBER = {"y": Y, "zl": ZL, "zh": ZH, "x": X}
STEP = {"y": 2, "zl": 4, "zh": 8, "x": 16}
YX = (("y", "zl", "zh", "x"), ("x", "y", "zl", "zh"))
ZX = (("zl", "x", "y", "zh"), ("x", "zl", "y", "zh"))
YXZ = (("y", "x", "zl", "zh"), ("x", "y", "zh", "zl"))
XYZ = (("y", "x", "zl", "zh"),) * 2
ORDERS = {"up": YXZ, "first": YX, "last": XYZ}


def places(info, core, p, half, orders):
    far = 1 - info[X] if half else info[X]
    bit = {"y": (p >> 2) & 1, "zl": (p >> 1) & 1, "zh": p & 1, "x": far}
    at = [sum(bit[a] * (8 >> k) for k, a in enumerate(order)) for order in orders]
    return jnp.where(core == 0, at[0], at[1])


def wide_body(info, w, *refs, counts, steps, orders):
    n = sum(counts)
    many_lhs = len(counts)
    lefts, rhs, (other, own, held) = refs[:many_lhs], refs[many_lhs : many_lhs + n], refs[many_lhs + n :]
    j = pl.program_id(0)
    R = lefts[0].shape[2]
    nb = other.shape[-1]
    cores = (1 - info[CORE], info[CORE])

    def bring(lhs):
        rel = lambda a, k: 1 - info[a] if k else info[a]
        for i, core in enumerate(cores):
            for p in range(8):
                block = rel(ZH, p & 1) * 4 + rel(ZL, (p >> 1) & 1) * 2 + rel(Y, (p >> 2) & 1)
                held[(i * 8 + p) * R : (i * 8 + p + 1) * R, :] = lhs[block, core]

    at, lo = 0, 0
    for left, many, count in zip(lefts, counts, steps):
        parts = rhs[at : at + many]

        def run(parts=parts, left=left, many=many):
            bring(left)
            for t in range(3):
                if len(parts[0].shape) == 3:
                    b = [r[t] for r in parts]
                    b = b[0] if many == 1 else jnp.concatenate(b, axis=1)
                else:
                    b = parts[0][:, t * (parts[0].shape[1] // 3) : (t + 1) * (parts[0].shape[1] // 3)]
                G = b.shape[1] // nb
                res = nn(held[...], b) * w[0]
                for h in range(G):
                    part = res[:, h * nb : (h + 1) * nb].reshape(2, 8, 2, R // 2, nb)
                    for i, (core, out) in enumerate(zip(cores, (other, own))):
                        for p in range(8):
                            for half in range(2):
                                out[places(info, core, p, half, orders), t * G + h] = part[i, p, half]

        pl.when((j >= lo) & (j < lo + count))(run)
        at, lo = at + many, lo + count


def wide_grad(info, weight, lhs, rhs, nb, orders, after=()):
    S = lhs[0].shape[1]
    R = lhs[0].shape[0] // 16
    specs, arrays = [], []
    for b in (b for group in rhs for b in group):
        b, k = b if isinstance(b, tuple) else (b, None)
        arrays.append(b)
        specs.append(const(*b.shape) if k is None else pl.BlockSpec((3, S, nb), lambda *_, k=k: (0, 0, k)))
    return call(
        partial(wide_body, counts=[len(g) for g in rhs], steps=[1] * len(rhs), orders=orders), "wide_grad", (len(rhs),),
        [const(8, 2, R, S) for _ in lhs] + specs,
        [pl.BlockSpec((16, 3, R // 2, nb), lambda j, *_: (0, j, 0, 0))] * 2,
        [sds(16, 3 * len(rhs), R // 2, nb)] * 2,
        scratch=[pltpu.VMEM((16 * R, S), BF)], prefetch=2, after=after, us=10,
    )(info, weight, *[a.reshape(8, 2, R, S) for a in lhs], *arrays)


def last_body(info, w, lhs, *refs, n, orders):
    rhs, parts = refs[:n], refs[n:-5]
    other, own, held, rows, turned = refs[-5:]
    R = lhs.shape[2]
    nb = other.shape[-1]
    cores = (1 - info[CORE], info[CORE])
    rel = lambda a, k: 1 - info[a] if k else info[a]
    for i, core in enumerate(cores):
        for p in range(8):
            block = rel(ZH, p & 1) * 4 + rel(ZL, (p >> 1) & 1) * 2 + rel(Y, (p >> 2) & 1)
            held[(i * 8 + p) * R : (i * 8 + p + 1) * R, :] = lhs[block, core]
    for t in range(3):
        res = nn(held[...], jnp.concatenate([r[t] for r in rhs], axis=1)) * w[0]
        part = res.reshape(2, 8, 2, R // 2, nb)
        for i, (core, out) in enumerate(zip(cores, (other, own))):
            for p in range(8):
                for half in range(2):
                    out[places(info, core, p, half, orders), t] = part[i, p, half]
    sp, *rest, up = parts
    rows[...] = jnp.zeros_like(rows)
    for k in range(2):
        rows[k : k + 1, :] = jnp.where(info[ID] == k, sp[...], 0.0) * w[0]
    at = 2
    for r in rest:
        rows[at : at + 1, :] = r[...] * w[0]
        at += 1
    D = rows.shape[1]
    many = up.shape[0]
    for k in range(many):
        rows[at + k : at + k + 1, :] = up[k] * w[0]
    turned[...] = rows[...].T
    blank = jnp.zeros((R // 2, nb - LANES), F32)
    lane = lax.broadcasted_iota(jnp.int32, (1, LANES), 1)
    span = many * R
    for core, out in zip(cores, (other, own)):
        for p in range(8):
            block = rel(ZH, p & 1) * 8 + rel(ZL, (p >> 1) & 1) * 4 + rel(Y, (p >> 2) & 1) * 2 + core
            row, start = block * span // D, block * span % D
            for half in range(2):
                place = places(info, core, p, half, orders)
                here = pl.ds(pl.multiple_of(block * R + half * (R // 2), 8), R // 2)
                value = jnp.where(lane < at, turned[here, :], 0.0)
                for k in range(many):
                    there = pl.ds(pl.multiple_of(start + k * R + half * (R // 2), 8), R // 2)
                    column = jnp.sum(jnp.where(lane == at + row, turned[there, :], 0.0), axis=1, keepdims=True)
                    value = jnp.where(lane == at + k, column, value)
                out[place, 3, :, :LANES] = value
                out[place, 3, :, LANES:] = blank


def last_grad(info, weight, lhs, rhs, parts, nb, orders, after=()):
    D, S = lhs.shape
    R = D // 16
    units = const(16, 4, R // 2, nb)
    lanes = [pl.BlockSpec((3, S, LANES), lambda *_, k=k: (0, 0, k)) for _, k in rhs]
    return call(
        partial(last_body, n=len(rhs), orders=orders), "last_grad", (1,),
        [const(8, 2, R, S)] + lanes + [const(*b.shape) for b in parts], [units, units], [sds(16, 4, R // 2, nb)] * 2,
        scratch=[pltpu.VMEM((D, S), BF), pltpu.VMEM((LANES, D), F32), pltpu.VMEM((D, LANES), F32)],
        prefetch=2, after=after,
    )(info, weight, lhs.reshape(8, 2, R, S), *[b for b, _ in rhs], *parts)


def scatter_units(info, res, other, own, orders):
    nb = other.shape[-1]
    R = res.shape[0] // 16
    cores = (1 - info[CORE], info[CORE])
    for g in range(res.shape[1] // nb):
        part = res[:, g * nb : (g + 1) * nb].reshape(2, 8, 2, R // 2, nb)
        for i, (core, out) in enumerate(zip(cores, (other, own))):
            for p in range(8):
                for half in range(2):
                    out[places(info, core, p, half, orders), g] = part[i, p, half]


def gather_blocks(info, natural, held):
    R = natural.shape[1]
    rel = lambda a, k: 1 - info[a] if k else info[a]
    for i, core in enumerate((1 - info[CORE], info[CORE])):
        for p in range(8):
            block = rel(ZH, p & 1) * 8 + rel(ZL, (p >> 1) & 1) * 4 + rel(Y, (p >> 2) & 1) * 2 + core
            held[(i * 8 + p) * R : (i * 8 + p + 1) * R, :] = natural[block]


def ffn_a_body(
    info, w, tok, tab, att, wo, ob, g2, b2, wu, ub, cot,
    mid_o, n2g, gf_o, act_o, gp_o, wd_o, dbs,
    n2_s, nat_s, actt_s, ub_s, *, rb,
):
    j = pl.program_id(0)
    S, D = tok.shape
    fb = wu.shape[1]
    R = nat_s.shape[1]
    blocks = [slice(i, i + rb) for i in range(0, S, rb)]

    @pl.when(j == 0)
    def _():
        sp = species_row(info, tab)
        total = None
        for r in blocks:
            mid = tok[r, :].astype(F32) + sp + nn(att[r, :], wo[...]) + vec(ob)
            mid_o[r, :] = mid
            n, _ = normed(mid)
            n2 = (n * vec(g2) + vec(b2)).astype(BF)
            n2_s[r, :] = n2
            nat_s[:, :, r] = n2.T.reshape(16, R, rb)
            row = r.start + lax.broadcasted_iota(jnp.int32, (rb, 1), 0)
            gf = jnp.where(row < info[LEN], cot[r, :].astype(F32), 0.0)
            gf_o[r, :] = gf.astype(BF)
            total = colsum(gf) if total is None else total + colsum(gf)
        dbs[...] = total
        gather_blocks(info, nat_s, n2g)
        bias = vec(ub)
        for c in range(ub_s.shape[0]):
            ub_s[c] = bias[:, c * fb : (c + 1) * fb]

    C = 0.7978845608
    C2 = C * 0.044715
    bias = ub_s[j]
    for r in blocks:
        u = nn(n2_s[r, :], wu[...]) + bias
        cu = C2 * (u * u)
        h = 0.5 * jnp.tanh(u * (cu + C)) + 0.5
        act = u * h
        ab = act.astype(BF)
        act_o[r, :] = ab
        actt_s[:, r] = ab.T
        gp_o[r, :] = (h + act * (1.0 - h) * (6.0 * cu + 2.0 * C)).astype(BF)
    wd_o[...] = nn(actt_s[...], gf_o[...]) * w[0]


def single(*shape):
    return pl.BlockSpec(shape, lambda *a: (0,) * len(shape), pipeline_mode=pl.Buffered(1))


def ffn_a(info, weight, tok, tab, att, wo, ob, g2, b2, wu, ub, cot, rb=256, after=()):
    S, D = tok.shape
    FF = wu.shape[1]
    n = FF // D
    cols = lambda m: pl.BlockSpec((m, D), lambda j, *_: (0, j))
    return call(
        partial(ffn_a_body, rb=rb), "ffn_a", (n,),
        [
            single(S, D), const(2, D), single(S, D), single(D, D), const(D), const(D), const(D),
            cols(D), const(FF), single(S, D),
        ],
        [single(S, D), single(D, S), single(S, D), cols(S), cols(S), pl.BlockSpec((D, D), lambda j, *_: (j, 0)), const(1, D)],
        [sds(S, D), sds(D, S, dt=BF), sds(S, D, dt=BF), sds(S, FF, dt=BF), sds(S, FF, dt=BF), sds(FF, D), sds(1, D)],
        scratch=[pltpu.VMEM((S, D), BF), pltpu.VMEM((16, D // 16, S), BF), pltpu.VMEM((D, S), BF), pltpu.VMEM((n, 1, D), F32)],
        prefetch=2, after=after,
    )(info, weight, tok, tab, att, wo, ob, g2, b2, wu, ub, cot)


def ffn_b_body(info, w, gf, wd, gp, n2g, gu, other, own, ubs, *, rb):
    S = gf.shape[0]
    total = None
    for i in range(0, S, rb):
        r = slice(i, i + rb)
        g = (nt(gf[r, :], wd[...]) * gp[r, :].astype(F32)).astype(BF)
        gu[r, :] = g
        here = colsum(g.astype(F32))
        total = here if total is None else total + here
    ubs[0] = total
    scatter_units(info, nn(n2g[...], gu[...]) * w[0], other, own, ORDERS["up"])


def ffn_b(info, weight, gf, wd, gp, n2g, rb=256, after=()):
    S, D = gf.shape
    FF = wd.shape[0]
    n = FF // D
    R, nb = D // 16, D // 3
    units = pl.BlockSpec((16, 3, R // 2, nb), lambda j, *_: (0, j, 0, 0))
    cols = pl.BlockSpec((S, D), lambda j, *_: (0, j))
    return call(
        partial(ffn_b_body, rb=rb), "ffn_b", (n,),
        [single(S, D), pl.BlockSpec((D, D), lambda j, *_: (j, 0)), cols, single(D, S)],
        [cols, units, units, pl.BlockSpec((1, 1, D), lambda j, *_: (j, 0, 0))],
        [sds(S, FF, dt=BF), sds(16, 3 * n, R // 2, nb), sds(16, 3 * n, R // 2, nb), sds(n, 1, D)],
        prefetch=2, after=after,
    )(info, weight, gf, wd, gp, n2g)


def ffn_c_body(gu, act, wu, wd, gf, mid_i, att, g2, wo, db, ga_o, gm_o, mixed_o, gb_o, attt, gs, bs, obs, gn_s, fe_s, *, rb):
    j = pl.program_id(0)
    last = pl.num_programs(0) - 1
    S = gf.shape[0]
    blocks = [slice(i, i + rb) for i in range(0, S, rb)]

    @pl.when(j == 0)
    def _():
        for r in blocks:
            fe_s[r, :] = nn(act[r, :], wd[...])
            gn_s[r, :] = nt(gu[r, :], wu[...])
        attt[...] = att[...].T

    @pl.when((j > 0) & (j < last))
    def _():
        for r in blocks:
            fe_s[r, :] += nn(act[r, :], wd[...])
            gn_s[r, :] += nt(gu[r, :], wu[...])

    @pl.when(j == last)
    def _():
        sums = None
        for r in blocks:
            mid = mid_i[r, :]
            gn = gn_s[r, :] + nt(gu[r, :], wu[...])
            n, rs = normed(mid)
            gm = gf[r, :].astype(F32) + norm_back(gn, n, rs, vec(g2))
            gm_o[r, :] = gm
            gb = gm.astype(BF)
            gb_o[r, :] = gb
            ga_o[r, :] = nt(gb, wo[...]).astype(BF)
            mixed_o[r, :] = (mid + (fe_s[r, :] + nn(act[r, :], wd[...])) + vec(db)).astype(BF)
            here = [colsum(gn * n), colsum(gn), colsum(gb.astype(F32))]
            sums = here if sums is None else [a + b for a, b in zip(sums, here)]
        gs[...], bs[...], obs[...] = sums


def ffn_c(gu, act, wu, wd, gf, mid, att, g2, wo, db, rb=256, after=()):
    S, D = gf.shape
    FF = wd.shape[0]
    cols = lambda m: pl.BlockSpec((m, D), lambda j: (0, j))
    return call(
        partial(ffn_c_body, rb=rb), "ffn_c", (FF // D,),
        [cols(S), cols(S), cols(D), pl.BlockSpec((D, D), lambda j: (j, 0)), single(S, D), single(S, D), single(S, D), const(D), single(D, D), const(D)],
        [single(S, D), single(S, D), single(S, D), single(S, D), single(D, S), const(1, D), const(1, D), const(1, D)],
        [sds(S, D, dt=BF), sds(S, D), sds(S, D, dt=BF), sds(S, D, dt=BF), sds(D, S, dt=BF), sds(1, D), sds(1, D), sds(1, D)],
        scratch=[pltpu.VMEM((S, D), F32), pltpu.VMEM((S, D), F32)], after=after,
    )(gu, act, wu, wd, gf, mid, att, g2, wo, db)


def to_core(a):
    return lax.ppermute(a, "dp", [(i, i ^ 1) for i in range(16)])


def to_stream(a):
    return lax.ppermute(a, "species", [(0, 1), (1, 0)])


class Sum:
    def __init__(self, name, parts):
        other, own = parts
        self.orders = ORDERS[name]
        self.own, self.got = own, to_core(other)
        self.step = 0

    def start(self, *after):
        n = self.own.shape[0] // 2
        got = tie(self.got, *after)
        self.send = self.own[n:] + got[n:]
        self.keep = [self.own[:n], got[:n]]
        return self.send

    def advance(self, *after):
        bits = [STEP[order[self.step]] for order in self.orders]
        got = lax.ppermute(self.send, ("species", "dp"), [(i, i ^ bits[i & 1]) for i in range(32)])
        got = tie(got, *after)
        self.step += 1
        n = got.shape[0] // 2
        terms = self.keep + [got]
        add = lambda lo, hi: sum((t[lo:hi] for t in terms[1:]), terms[0][lo:hi])
        if n:
            self.send, self.keep = add(n, 2 * n), [add(0, n)]
        else:
            self.send = add(0, 1)
            self.keep = [self.send]
        return self.send

    def finish(self):
        while self.step < 4:
            self.advance()
        unit = self.send[0]
        return unit, to_stream(unit)


def join_body(info, *refs, n, moves):
    pairs = [(refs[2 * i], refs[2 * i + 1]) for i in range(n)]
    outs = refs[2 * n :]
    up = info[X] == 1
    for i, g, o, c in moves:
        a, b = pairs[i][0][g], pairs[i][1][g]
        U, nb = a.shape
        if c is None:
            both = [a[:, :LANES], b[:, :LANES]]
            low, high = jnp.where(up, both[1], both[0]), jnp.where(up, both[0], both[1])
            outs[o][...] = jnp.concatenate([low, high], axis=0).T[: outs[o].shape[0]]
            continue
        outs[o][:U, c : c + nb] = jnp.where(up, b, a)
        outs[o][U:, c : c + nb] = jnp.where(up, a, b)


def join(info, pairs, moves, shapes, after=()):
    arrays = [a if a.ndim == 3 else a[None] for p in pairs for a in p]
    return call(
        partial(join_body, n=len(pairs), moves=moves), "join", (1,),
        [const(*a.shape) for a in arrays], [const(*s) for s in shapes], [sds(*s) for s in shapes], prefetch=1, after=after,
    )(info, *arrays)


def stack_body(info, w, *refs):
    *parts, o = refs
    D = o.shape[1]
    sp, rest, up = parts[0], parts[1:-1], parts[-1]
    o[...] = jnp.zeros_like(o)
    for k in range(2):
        o[k : k + 1, :] = jnp.where(info[ID] == k, sp[...], 0.0) * w[0]
    for k, r in enumerate(rest):
        o[2 + k : 3 + k, :] = r[...] * w[0]
    for k in range(up.shape[1] // D):
        o[2 + len(rest) + k : 3 + len(rest) + k, :] = up[:, k * D : (k + 1) * D] * w[0]


def stack(info, weight, parts, after=()):
    D = parts[0].shape[1]
    rows = 1 + sum(p.shape[1] // D for p in parts)
    rows += -rows % 8
    return call(
        stack_body, "stack", (1,), [const(*p.shape) for p in parts], const(rows, D), sds(rows, D), prefetch=2, after=after,
    )(info, weight, *parts)


def flat(chunks):
    return jnp.concatenate(list(chunks), axis=1)


def local(
    tokens, cotangent, lengths, species_ids, species_table, ln1_gain, ln1_bias, w_qkv, q_bias, v_bias,
    w_out, out_bias, ln2_gain, ln2_bias, w_up, up_bias, w_down, down_bias, *, dp_size,
):
    D = tokens.shape[2]
    hd = D // HEADS
    scale = hd ** (-0.5)
    FF = w_up.shape[1]
    tok = tokens[0]
    cot = cotangent[0]
    paired = dp_size == 16
    dp = lax.axis_index("dp")
    x = lax.axis_index("species")
    info = jnp.stack([lengths[0], species_ids[0], dp % 2, (dp // 2) % 2, (dp // 4) % 2, dp // 8, x]).astype(jnp.int32)
    length_float = lengths[0].astype(F32)

    exchange = lambda a, bit: lax.ppermute(a, "dp", [(i, i ^ bit) for i in range(16)])
    gather = lambda a, *bits: [exchange(a, bit) for bit in bits]
    qkv, n1t = qkv_proj(info, tok, species_table, ln1_gain, ln1_bias, w_qkv, q_bias, v_bias)
    hops = []
    if paired:
        count = jnp.full((8, LANES), length_float)
        count = count + sum(tie(c, n1t) for c in gather(count, 1, 2, 3))
        hops = [count]
    att, att_f32, nl = attn_fwd(info, qkv, scale, hd, after=hops)
    if paired:
        count = count + sum(tie(c, nl) for c in gather(count, 4, 8, 12))
        hops = [count]
    back = lambda first, count, after: attn_bwd(info, qkv, att_f32, ga, nl, first, count, scale, hd, after=after)
    if paired:
        nb = D // 3
        scatter = lambda a: lax.psum_scatter(a, "dp", scatter_dimension=0, tiled=True)
        mid, n2g, gf, act, gp, part, down_part = ffn_a(
            info, length_float.reshape(1), tok, species_table, att, w_out, out_bias, ln2_gain, ln2_bias, w_up, up_bias, cot, after=hops
        )
        down = scatter(part)
        share_weight = 1.0 / (2.0 * count[0, 0])
        weight = (length_float * share_weight).reshape(1)
        gu, up_other, up_own, up_part = ffn_b(info, weight, gf, w_down, gp, n2g, after=[part])
        up = Sum("up", (up_other, up_own))
        ga, gm, mixed, gb, attt, ln2g_part, ln2b_part, ob_part = ffn_c(
            gu, act, w_up, w_down, gf, mid, att, ln2_gain, w_out, down_bias, after=[up_part]
        )
        up.start(ob_part)
        gq0 = back(0, 5, [up.send])
        first = Sum("first", wide_grad(info, weight, [n1t, n1t, attt], [[(gq0, 0)], [(gq0, 1)], [gb]], nb, ORDERS["first"], after=[gq0]))
        up.advance(first.own)
        gq1 = back(5, 1, [first.own, up.send])
        first.start(gq1)
        up.advance(first.send)
        gt, ln1g_part, ln1b_part, sp_part, qb_part, vb_part = back1(
            info, [gq0, gq1], w_qkv, tok, species_table, ln1_gain, gm, after=[first.send, up.send]
        )
        up.advance(sp_part)
        down = tie(down, up.send) * share_weight
        down_other = to_stream(down)
        n = D // dp_size
        last = Sum("last", last_grad(
            info, weight, n1t, [(gq0, 4), (gq1, 0)],
            [sp_part, ln1g_part, ln1b_part, qb_part, vb_part, ob_part, ln2g_part, ln2b_part, down_part, up_part],
            nb, ORDERS["last"], after=[up.send, down],
        ))
        first.advance(last.own)
        last.start(first.send)
        up.advance(last.send)
        first.advance(up.send)
        g_down = down + tie(down_other, first.send)
        last.advance(g_down)
        up_pair = up.finish()
        up_pair = (up_pair[0], tie(up_pair[1], last.send))
        (g_up,) = join(info, [up_pair], [(0, g, 0, g * nb) for g in range(FF // nb)], [(n, FF)])
        first.advance(g_up)
        last.advance(first.send)
        first.advance(last.send)
        last.advance(first.send)
        last.advance(last.send)
    else:
        weight = (length_float / (2.0 * lax.psum(length_float, "dp"))).reshape(1)
        mid, n2t, act, actt, gp, gf, attt, down_part = mid1(
            info, tok, species_table, att, w_out, out_bias, ln2_gain, ln2_bias, w_up, up_bias, cot
        )
        gu, up_part = mid2(gf, w_down, gp)
        gm, gb, ga, ln2g_part, ln2b_part, ob_part = back2(info, gu, w_up, mid, ln2_gain, cot, w_out)
        gqs = [back(0, D // LANES, ())]
        gt, ln1g_part, ln1b_part, sp_part, qb_part, vb_part = back1(info, gqs, w_qkv, tok, species_table, ln1_gain, gm)
        mixed = mixed_out(act, w_down, mid, down_bias)
        small = stack(info, weight, [sp_part, ln1g_part, ln1b_part, qb_part, vb_part, ob_part, ln2g_part, ln2b_part, down_part, up_part])
        small = lax.psum(lax.psum(small, "dp"), "species")
    n = D // dp_size
    if not paired:
        share = lambda r: lax.dynamic_slice_in_dim(small[r], dp * n, n)
        species = lax.dynamic_slice_in_dim(small[:2], dp * n, n, axis=1)
        up_share = lax.dynamic_slice_in_dim(small[10 : 10 + FF // D].reshape(-1), dp * (FF // dp_size), FF // dp_size)
    if paired:
        moves = [(0, 3 * h + t, 0, t * D + h * nb) for t in range(3) for h in range(2)]
        moves += [(1, t, 0, t * D + 2 * nb) for t in range(3)] + [(1, 3, 1, None)] + [(0, 6 + t, 2, t * nb) for t in range(3)]
        g_qkv, small, g_out = join(info, [first.finish(), last.finish()], moves, [(n, 3 * D), (16, n), (n, D)])
        share = lambda r: small[r]
        species, up_share = small[:2], small[10 : 10 + FF // D].reshape(-1)
    else:
        def total(part):
            return lax.psum(lax.psum_scatter(part, "dp", scatter_dimension=0, tiled=True), "species")

        g_down = total(wgrad(weight, actt, gf))
        g_up = total(wgrad(weight, n2t, gu))
        g_out = total(wgrad(weight, attt, gb))
        g_qkv = total(wgrad(weight, n1t, flat(gqs[0])))
    return (
        mixed[None], gt[None], species, share(2), share(3), g_qkv, share(4), share(5), g_out, share(6),
        share(7), share(8), g_up, up_share, g_down, share(9),
    )


def solution(mesh):
    cells = P(("species", "dp"), None, None)
    scalars = P(("species", "dp"))
    in_specs = (cells, cells, scalars, scalars) + (P(),) * 14
    v, m = P("dp"), P("dp", None)
    out_specs = (cells, cells, P(None, "dp"), v, v, m, v, v, m, v, v, v, m, v, m, v)
    return jax.shard_map(
        partial(local, dp_size=mesh.shape["dp"]), mesh=mesh, in_specs=in_specs, out_specs=out_specs, check_vma=False
    )
```

```python
from functools import partial

import jax
import jax.numpy as jnp
from jax import lax
from jax.experimental import pallas as pl
from jax.experimental.pallas import tpu as pltpu
from jax.sharding import PartitionSpec as P

HEADS = 12
F32 = jnp.float32
BF = jnp.bfloat16
LOG2E = 1.4426950408889634
MIB = 1 << 20
LANES = 128


def nt(a, b):
    return lax.dot_general(a, b, (((1,), (1,)), ((), ())), preferred_element_type=F32)


def nn(a, b):
    return lax.dot_general(a, b, (((1,), (0,)), ((), ())), preferred_element_type=F32)


def tie(a, *after):
    return lax.optimization_barrier((a, *after))[0] if after else a


def call(body, name, grid, ins, outs, shapes, scratch=(), prefetch=0, mib=56, after=(), us=0.05):
    f = pl.pallas_call(
        body,
        grid_spec=pltpu.PrefetchScalarGridSpec(
            num_scalar_prefetch=prefetch, grid=grid, in_specs=ins, out_specs=outs, scratch_shapes=list(scratch)
        ),
        out_shape=shapes,
        compiler_params=pltpu.CompilerParams(vmem_limit_bytes=mib * MIB),
        cost_estimate=pl.CostEstimate(flops=1000, bytes_accessed=int(us * 3.2e6), transcendentals=0),
        name=name,
    )
    return lambda first, *rest: f(tie(first, *after), *rest)


def const(*shape):
    return pl.BlockSpec(shape, lambda *a: (0,) * len(shape))


def sds(*shape, dt=F32):
    return jax.ShapeDtypeStruct(shape, dt)


def normed(x):
    c = x - jnp.mean(x, axis=-1, keepdims=True)
    r = lax.rsqrt(jnp.mean(c * c, axis=-1, keepdims=True) + 1e-5)
    return c * r, r


def norm_back(g, n, r, gain):
    e = g * gain
    return r * (e - jnp.mean(e, axis=-1, keepdims=True) - n * jnp.mean(e * n, axis=-1, keepdims=True))


def colsum(x):
    return jnp.sum(x, axis=0, keepdims=True)


def rows_of(rb, n):
    return pl.BlockSpec((rb, n), lambda i, *_: (i, 0))


def cols_of(n, rb):
    return pl.BlockSpec((n, rb), lambda i, *_: (0, i))


LEN, ID, CORE, Y, ZL, ZH, X = range(7)


def vec(ref):
    return ref[...].astype(F32)[None, :]


def species_row(info, table):
    rows = table[...].astype(F32)
    return jnp.where(info[ID] == 0, rows[0:1], rows[1:2])


def qkv_body(info, tok, tab, g, b, w, qb, vb, qkv, n1t):
    n, _ = normed(tok[...].astype(F32) + species_row(info, tab))
    nb = (n * vec(g) + vec(b)).astype(BF)
    n1t[...] = nb.T
    bias = jnp.concatenate([vec(qb), jnp.zeros((1, tok.shape[1]), F32), vec(vb)], axis=1)
    qkv[...] = (nn(nb, w[...]) + bias).astype(BF)


def qkv_proj(info, tok, tab, g, b, w, qb, vb, rb=256):
    S, D = tok.shape
    N = w.shape[1]
    return call(
        qkv_body, "qkv_proj", (S // rb,),
        [rows_of(rb, D), const(2, D), const(D), const(D), const(D, N), const(D), const(D)],
        [rows_of(rb, N), cols_of(D, rb)],
        [sds(S, N, dt=BF), sds(D, S, dt=BF)], prefetch=1,
    )(info, tok, tab, g, b, w, qb, vb)


def split2(x):
    hi = x.astype(BF)
    return hi, (x - hi.astype(F32)).astype(BF)


def split3(x):
    a = x.astype(BF).astype(F32)
    r = x - a
    b = r.astype(BF).astype(F32)
    return a, b, r - b


def attn_fwd_body(ln, q_ref, k_ref, v_ref, o_ref, of_ref, nl_ref, *, scale, qb, hd):
    S = q_ref.shape[0]
    lane = lax.broadcasted_iota(jnp.int32, (1, LANES), 1)
    row = lax.broadcasted_iota(jnp.int32, (S, 1), 0)
    mask = jnp.where(row < ln[0], 0.0, -1e30).astype(F32)
    kk = k_ref[...]
    kf = kk.astype(F32)
    vf = v_ref[...].astype(F32)
    hi, lo = split2(q_ref[...].astype(F32) * (scale * LOG2E))
    hi = hi.astype(F32)
    lo = lo.astype(F32)
    qa, ka, va = [], [], []
    for h in range(2):
        own = (lane // hd) == h
        aux = lane == (1 - h) * hd
        k2 = jnp.where(own, kf, jnp.where(aux, mask, 0.0)).astype(BF)
        ka.append(jnp.concatenate([kk, k2], axis=1))
        q1 = jnp.where(own, hi, 0.0).astype(BF)
        q2 = jnp.where(own, lo, jnp.where(aux, 1.0, 0.0)).astype(BF)
        qa.append(jnp.concatenate([q1, q2], axis=1))
        va.append(jnp.where(own, vf, 1.0).astype(BF))
    for b in range(S // qb):
        sl = slice(b * qb, (b + 1) * qb)
        outs, nls = [], []
        for h in range(2):
            s = nt(qa[h][sl], ka[h])
            m = jnp.max(s, axis=1, keepdims=True)
            p = jnp.exp2(s - m).astype(BF)
            o = nn(p, va[h])
            outs.append(o / pltpu.roll(o, hd, 1))
            nls.append(-(m + jnp.log2(o)))
        o = jnp.where(lane < hd, outs[0], outs[1])
        of_ref[sl, :] = o
        o_ref[sl, :] = o.astype(BF)
        nl_ref[sl, :] = jnp.where(lane < hd, nls[1], nls[0])


def attn_fwd(ln, qkv, scale, hd, qb=512, after=()):
    S, D = qkv.shape[0], qkv.shape[1] // 3
    n = D // LANES
    qb = min(qb, S)
    cb = lambda off: pl.BlockSpec((S, LANES), lambda p, l: (0, off + p))
    return call(
        partial(attn_fwd_body, scale=scale, qb=qb, hd=hd), "attn_fwd", (n,),
        [cb(0), cb(n), cb(2 * n)], [cb(0), cb(0), cb(0)],
        [sds(S, D, dt=BF), sds(S, D), sds(S, D)], prefetch=1, after=after,
    )(ln, qkv, qkv, qkv)


def attn_bwd_body(ln, q_ref, k_ref, v_ref, o_ref, do_ref, nl_ref, g_ref, dqt_ref, kt_ref, ka_ref, va_ref, *, scale, kb, hd):
    S = q_ref.shape[0]
    n = ln[0]
    lane = lax.broadcasted_iota(jnp.int32, (1, LANES), 1)
    row = lax.broadcasted_iota(jnp.int32, (S, 1), 0)
    mask = jnp.where(row < n, 0.0, -1e30).astype(F32)
    kk = k_ref[...]
    kf = kk.astype(F32)
    vf = v_ref[...].astype(F32)
    dof = do_ref[...].astype(F32)
    qf = q_ref[...].astype(F32)
    hi, lo = split2(qf * (scale * LOG2E))
    hi = hi.astype(F32)
    lo = lo.astype(F32)
    n0, n1, n2 = split3(nl_ref[...])
    do_o = dof * o_ref[...]
    kt_ref[...] = kf.T.astype(BF)
    qa, qo, da, do_own = [], [], [], []
    for h in range(2):
        own = (lane // hd) == h
        base = (1 - h) * hd
        three = (lane > base) & (lane < base + 4)
        pick = lambda a, b, c: jnp.where(lane == base + 1, a, jnp.where(lane == base + 2, b, jnp.where(lane == base + 3, c, 0.0)))
        ka_ref[h, :, 0:LANES] = kk
        ka_ref[h, :, LANES:] = jnp.where(own, kf, jnp.where(lane == base, mask, jnp.where(three, 1.0, 0.0))).astype(BF)
        va_ref[h] = jnp.where(own, vf, jnp.where(three, 1.0, 0.0)).astype(BF)
        q1 = jnp.where(own, hi, 0.0).astype(BF)
        q2 = jnp.where(own, lo, jnp.where(lane == base, 1.0, pick(n0, n1, n2))).astype(BF)
        qa.append(jnp.concatenate([q1, q2], axis=1))
        qo.append(jnp.where(own, qf, 0.0).astype(BF))
        delta = -jnp.sum(jnp.where(own, do_o, 0.0), axis=1, keepdims=True)
        do_own.append(jnp.where(own, dof, 0.0).astype(BF))
        da.append(jnp.where(own, dof, pick(*split3(delta))).astype(BF))
    for b in range(S // kb):
        sl = slice(b * kb, (b + 1) * kb)

        @pl.when(b * kb < n)
        def _():
            dv = dk = None
            for h in range(2):
                p = jnp.exp2(nt(ka_ref[h, sl, :], qa[h]))
                ds = (p * nt(va_ref[h, sl, :], da[h])).astype(BF)
                dvh = nn(p.astype(BF), do_own[h])
                dkh = nn(ds, qo[h])
                dv = dvh if h == 0 else dv + dvh
                dk = dkh if h == 0 else dk + dkh
                dqt = nn(kt_ref[h * hd : (h + 1) * hd, sl], ds)
                if b == 0:
                    dqt_ref[h * hd : (h + 1) * hd, :] = dqt
                else:
                    dqt_ref[h * hd : (h + 1) * hd, :] += dqt
            g_ref[1, sl, :] = (dk * scale).astype(BF)
            g_ref[2, sl, :] = dv.astype(BF)

        @pl.when(b * kb >= n)
        def _():
            g_ref[1, sl, :] = jnp.zeros((kb, LANES), BF)
            g_ref[2, sl, :] = jnp.zeros((kb, LANES), BF)

    g_ref[0] = (dqt_ref[...].T * scale).astype(BF)


def attn_bwd(ln, qkv, o, do, nl, first, count, scale, hd, kb=1024, after=()):
    S, D = qkv.shape[0], qkv.shape[1] // 3
    n = D // LANES
    kb = min(kb, S)
    cb = lambda off: pl.BlockSpec((S, LANES), lambda p, l: (0, off + first + p))
    return call(
        partial(attn_bwd_body, scale=scale, kb=kb, hd=hd), "attn_bwd", (count,),
        [cb(0), cb(n), cb(2 * n), cb(0), cb(0), cb(0)],
        pl.BlockSpec((3, S, LANES), lambda p, l: (0, 0, p)),
        sds(3, S, count * LANES, dt=BF),
        scratch=[pltpu.VMEM((LANES, S), F32), pltpu.VMEM((LANES, S), BF), pltpu.VMEM((2, S, 2 * LANES), BF), pltpu.VMEM((2, S, LANES), BF)],
        prefetch=1, after=after, us=9 if count == 1 else 0.05,
    )(ln, qkv, qkv, qkv, o, do, nl)


def mid1_body(info, tok, tab, att, wo, ob, g2, b2, wu, ub, cot, mid_o, n2t, act_o, actt, gp_o, gf_o, attt, dbs, *, fb):
    i = pl.program_id(0)
    rb = tok.shape[0]
    FF = wu.shape[1]
    a = att[...]
    attt[...] = a.T
    mid = tok[...].astype(F32) + species_row(info, tab) + nn(a, wo[...]) + vec(ob)
    mid_o[...] = mid
    n, _ = normed(mid)
    n2 = (n * vec(g2) + vec(b2)).astype(BF)
    n2t[...] = n2.T
    row = i * rb + lax.broadcasted_iota(jnp.int32, (rb, 1), 0)
    gf = jnp.where(row < info[LEN], cot[...].astype(F32), 0.0)
    gf_o[...] = gf.astype(BF)

    @pl.when(i == 0)
    def _():
        dbs[...] = jnp.zeros_like(dbs)

    dbs[...] += colsum(gf)
    C = 0.7978845608
    C2 = C * 0.044715
    bias = vec(ub)
    for j in range(FF // fb):
        sl = slice(j * fb, (j + 1) * fb)
        u = nn(n2, wu[:, sl]) + bias[:, sl]
        cu = C2 * (u * u)
        h = 0.5 * jnp.tanh(u * (cu + C)) + 0.5
        act = u * h
        ab = act.astype(BF)
        act_o[:, sl] = ab
        actt[sl, :] = ab.T
        gp_o[:, sl] = (h + act * (1.0 - h) * (6.0 * cu + 2.0 * C)).astype(BF)


def mid1(info, tok, tab, att, wo, ob, g2, b2, wu, ub, cot, rb=256, fb=768):
    S, D = tok.shape
    FF = wu.shape[1]
    r = partial(rows_of, rb)
    t = lambda n: cols_of(n, rb)
    return call(
        partial(mid1_body, fb=fb), "mid1", (S // rb,),
        [r(D), const(2, D), r(D), const(D, D), const(D), const(D), const(D), const(D, FF), const(FF), r(D)],
        [r(D), t(D), r(FF), t(FF), r(FF), r(D), t(D), const(1, D)],
        [sds(S, D), sds(D, S, dt=BF), sds(S, FF, dt=BF), sds(FF, S, dt=BF), sds(S, FF, dt=BF), sds(S, D, dt=BF), sds(D, S, dt=BF), sds(1, D)],
        prefetch=1,
    )(info, tok, tab, att, wo, ob, g2, b2, wu, ub, cot)


def mid2_body(gf, wd, gp, gu_o, ubs):
    gu = (nt(gf[...], wd[...]) * gp[...].astype(F32)).astype(BF)
    gu_o[...] = gu
    ubs[...] = colsum(gu.astype(F32))


def mid2(gf, wd, gp, nb=512, after=()):
    S, D = gf.shape
    FF = wd.shape[0]
    t = lambda n: pl.BlockSpec((n, nb), lambda j: (0, j))
    return call(
        mid2_body, "mid2", (FF // nb,),
        [const(S, D), pl.BlockSpec((nb, D), lambda j: (j, 0)), t(S)],
        [t(S), t(1)], [sds(S, FF, dt=BF), sds(1, FF)], after=after,
    )(gf, wd, gp)


def back2_body(ln, gu, wu, mid, g2, cot, wo, gm_o, gb_o, ga_o, gs, bs, obs):
    i = pl.program_id(0)
    rb = mid.shape[0]
    gn = nt(gu[...], wu[...])
    n, r = normed(mid[...])
    row = i * rb + lax.broadcasted_iota(jnp.int32, (rb, 1), 0)
    gf = jnp.where(row < ln[0], cot[...].astype(F32), 0.0)
    gm = gf + norm_back(gn, n, r, vec(g2))
    gm_o[...] = gm
    gb = gm.astype(BF)
    gb_o[...] = gb
    ga_o[...] = nt(gb, wo[...]).astype(BF)

    @pl.when(i == 0)
    def _():
        for s in (gs, bs, obs):
            s[...] = jnp.zeros_like(s)

    gs[...] += colsum(gn * n)
    bs[...] += colsum(gn)
    obs[...] += colsum(gb.astype(F32))


def back2(ln, gu, wu, mid, g2, cot, wo, rb=256, after=()):
    S, D = mid.shape
    FF = wu.shape[1]
    r = partial(rows_of, rb)
    return call(
        back2_body, "back2", (S // rb,),
        [r(FF), const(D, FF), r(D), const(D), r(D), const(D, D)],
        [r(D), r(D), r(D), const(1, D), const(1, D), const(1, D)],
        [sds(S, D), sds(S, D, dt=BF), sds(S, D, dt=BF), sds(1, D), sds(1, D), sds(1, D)],
        prefetch=1, after=after,
    )(ln, gu, wu, mid, g2, cot, wo)


def back1_body(info, *refs):
    *gq, w, tok, tab, g1, gm, gt_o, gs, bs, ss, qs, vs = refs
    i = pl.program_id(0)
    D = tok.shape[1]
    gn = None
    for t in range(3):
        whole = jnp.concatenate([g[t] for g in gq], axis=1)
        part = nt(whole, w[:, t * D : (t + 1) * D])
        gn = part if gn is None else gn + part
    n, r = normed(tok[...].astype(F32) + species_row(info, tab))
    g = gm[...] + norm_back(gn, n, r, vec(g1))
    gt_o[...] = g.astype(BF)

    @pl.when(i == 0)
    def _():
        for s in (gs, bs, ss, qs, vs):
            s[...] = jnp.zeros_like(s)

    gs[...] += colsum(gn * n)
    bs[...] += colsum(gn)
    ss[...] += colsum(g)
    qs[...] += colsum(jnp.concatenate([g[0] for g in gq], axis=1).astype(F32))
    vs[...] += colsum(jnp.concatenate([g[2] for g in gq], axis=1).astype(F32))


def back1(info, gq, w, tok, tab, g1, gm, rb=256, after=()):
    S, D = tok.shape
    r = partial(rows_of, rb)
    return call(
        back1_body, "back1", (S // rb,),
        [pl.BlockSpec((3, rb, g.shape[2]), lambda i, n: (0, i, 0)) for g in gq] + [const(D, 3 * D), r(D), const(2, D), const(D), r(D)],
        [r(D)] + [const(1, D)] * 5,
        [sds(S, D, dt=BF)] + [sds(1, D)] * 5, prefetch=1, after=after, us=11,
    )(info, *gq, w, tok, tab, g1, gm)


def mixed_body(act, wd, mid, db, o):
    o[...] = (mid[...] + nn(act[...], wd[...]) + vec(db)).astype(BF)


def mixed_out(act, wd, mid, db, first=0, count=4, rb=256, after=()):
    D = mid.shape[1]
    FF = wd.shape[0]
    r = lambda n: pl.BlockSpec((rb, n), lambda i: (first + i, 0))
    return call(
        mixed_body, "mixed_out", (count,),
        [r(FF), const(FF, D), r(D), const(D)], rows_of(rb, D), sds(count * rb, D, dt=BF), after=after,
    )(act, wd, mid, db)


def wgrad_body(w, a, b, o):
    o[...] = nn(a[...], b[...]) * w[0]


def wgrad(weight, at, b, nb=768, after=()):
    M, S = at.shape
    N = b.shape[1]
    mb = min(M, 768)
    return call(
        wgrad_body, "wgrad", (M // mb, N // nb),
        [pl.BlockSpec((mb, S), lambda i, j, w: (i, 0)), pl.BlockSpec((S, nb), lambda i, j, w: (0, j))],
        pl.BlockSpec((mb, nb), lambda i, j, w: (i, j)), sds(M, N),
        prefetch=1, after=after,
    )(weight, at, b)


NUMBER = {"y": Y, "zl": ZL, "zh": ZH, "x": X}
STEP = {"y": 2, "zl": 4, "zh": 8, "x": 16}
YX = (("y", "zl", "zh", "x"), ("x", "y", "zl", "zh"))
ZX = (("zl", "x", "y", "zh"), ("x", "zl", "y", "zh"))
YXZ = (("y", "x", "zl", "zh"), ("x", "y", "zh", "zl"))
XYZ = (("y", "x", "zl", "zh"), ("x", "y", "zl", "zh"))
ORDERS = {"up": YXZ, "first": YX, "last": XYZ}


def places(info, core, p, half, orders):
    far = 1 - info[X] if half else info[X]
    bit = {"y": (p >> 2) & 1, "zl": (p >> 1) & 1, "zh": p & 1, "x": far}
    at = [sum(bit[a] * (8 >> k) for k, a in enumerate(order)) for order in orders]
    return jnp.where(core == 0, at[0], at[1])


def wide_body(info, w, *refs, counts, steps, orders):
    n = sum(counts)
    many_lhs = len(counts)
    lefts, rhs, (other, own, held) = refs[:many_lhs], refs[many_lhs : many_lhs + n], refs[many_lhs + n :]
    j = pl.program_id(0)
    R = lefts[0].shape[2]
    nb = other.shape[-1]
    cores = (1 - info[CORE], info[CORE])

    def bring(lhs):
        rel = lambda a, k: 1 - info[a] if k else info[a]
        for i, core in enumerate(cores):
            for p in range(8):
                block = rel(ZH, p & 1) * 4 + rel(ZL, (p >> 1) & 1) * 2 + rel(Y, (p >> 2) & 1)
                held[(i * 8 + p) * R : (i * 8 + p + 1) * R, :] = lhs[block, core]

    at, lo = 0, 0
    for left, many, count in zip(lefts, counts, steps):
        parts = rhs[at : at + many]

        def run(parts=parts, left=left, many=many):
            bring(left)
            for t in range(3):
                if len(parts[0].shape) == 3:
                    b = [r[t] for r in parts]
                    b = b[0] if many == 1 else jnp.concatenate(b, axis=1)
                else:
                    b = parts[0][:, t * (parts[0].shape[1] // 3) : (t + 1) * (parts[0].shape[1] // 3)]
                G = b.shape[1] // nb
                res = nn(held[...], b) * w[0]
                for h in range(G):
                    part = res[:, h * nb : (h + 1) * nb].reshape(2, 8, 2, R // 2, nb)
                    for i, (core, out) in enumerate(zip(cores, (other, own))):
                        for p in range(8):
                            for half in range(2):
                                out[places(info, core, p, half, orders), t * G + h] = part[i, p, half]

        pl.when((j >= lo) & (j < lo + count))(run)
        at, lo = at + many, lo + count


def wide_grad(info, weight, lhs, rhs, nb, orders, after=()):
    S = lhs[0].shape[1]
    R = lhs[0].shape[0] // 16
    specs, arrays = [], []
    for b in (b for group in rhs for b in group):
        b, k = b if isinstance(b, tuple) else (b, None)
        arrays.append(b)
        specs.append(const(*b.shape) if k is None else pl.BlockSpec((3, S, nb), lambda *_, k=k: (0, 0, k)))
    return call(
        partial(wide_body, counts=[len(g) for g in rhs], steps=[1] * len(rhs), orders=orders), "wide_grad", (len(rhs),),
        [const(8, 2, R, S) for _ in lhs] + specs,
        [pl.BlockSpec((16, 3, R // 2, nb), lambda j, *_: (0, j, 0, 0))] * 2,
        [sds(16, 3 * len(rhs), R // 2, nb)] * 2,
        scratch=[pltpu.VMEM((16 * R, S), BF)], prefetch=2, after=after, us=10,
    )(info, weight, *[a.reshape(8, 2, R, S) for a in lhs], *arrays)


def last_body(info, w, lhs, *refs, n, orders):
    rhs, parts = refs[:n], refs[n:-5]
    other, own, held, rows, turned = refs[-5:]
    R = lhs.shape[2]
    nb = other.shape[-1]
    cores = (1 - info[CORE], info[CORE])
    rel = lambda a, k: 1 - info[a] if k else info[a]
    for i, core in enumerate(cores):
        for p in range(8):
            block = rel(ZH, p & 1) * 4 + rel(ZL, (p >> 1) & 1) * 2 + rel(Y, (p >> 2) & 1)
            held[(i * 8 + p) * R : (i * 8 + p + 1) * R, :] = lhs[block, core]
    for t in range(3):
        res = nn(held[...], jnp.concatenate([r[t] for r in rhs], axis=1)) * w[0]
        part = res.reshape(2, 8, 2, R // 2, nb)
        for i, (core, out) in enumerate(zip(cores, (other, own))):
            for p in range(8):
                for half in range(2):
                    out[places(info, core, p, half, orders), t] = part[i, p, half]
    sp, *rest, up = parts
    rows[...] = jnp.zeros_like(rows)
    for k in range(2):
        rows[k : k + 1, :] = jnp.where(info[ID] == k, sp[...], 0.0) * w[0]
    at = 2
    for r in rest:
        rows[at : at + 1, :] = r[...] * w[0]
        at += 1
    D = rows.shape[1]
    many = up.shape[0]
    for k in range(many):
        rows[at + k : at + k + 1, :] = up[k] * w[0]
    turned[...] = rows[...].T
    blank = jnp.zeros((R // 2, nb - LANES), F32)
    lane = lax.broadcasted_iota(jnp.int32, (1, LANES), 1)
    span = many * R
    for core, out in zip(cores, (other, own)):
        for p in range(8):
            block = rel(ZH, p & 1) * 8 + rel(ZL, (p >> 1) & 1) * 4 + rel(Y, (p >> 2) & 1) * 2 + core
            row, start = block * span // D, block * span % D
            for half in range(2):
                place = places(info, core, p, half, orders)
                here = pl.ds(pl.multiple_of(block * R + half * (R // 2), 8), R // 2)
                value = jnp.where(lane < at, turned[here, :], 0.0)
                for k in range(many):
                    there = pl.ds(pl.multiple_of(start + k * R + half * (R // 2), 8), R // 2)
                    column = jnp.sum(jnp.where(lane == at + row, turned[there, :], 0.0), axis=1, keepdims=True)
                    value = jnp.where(lane == at + k, column, value)
                out[place, 3, :, :LANES] = value
                out[place, 3, :, LANES:] = blank


def last_grad(info, weight, lhs, rhs, parts, nb, orders, after=()):
    D, S = lhs.shape
    R = D // 16
    units = const(16, 4, R // 2, nb)
    lanes = [pl.BlockSpec((3, S, LANES), lambda *_, k=k: (0, 0, k)) for _, k in rhs]
    return call(
        partial(last_body, n=len(rhs), orders=orders), "last_grad", (1,),
        [const(8, 2, R, S)] + lanes + [const(*b.shape) for b in parts], [units, units], [sds(16, 4, R // 2, nb)] * 2,
        scratch=[pltpu.VMEM((D, S), BF), pltpu.VMEM((LANES, D), F32), pltpu.VMEM((D, LANES), F32)],
        prefetch=2, after=after,
    )(info, weight, lhs.reshape(8, 2, R, S), *[b for b, _ in rhs], *parts)


def scatter_units(info, res, other, own, orders):
    nb = other.shape[-1]
    R = res.shape[0] // 16
    cores = (1 - info[CORE], info[CORE])
    for g in range(res.shape[1] // nb):
        part = res[:, g * nb : (g + 1) * nb].reshape(2, 8, 2, R // 2, nb)
        for i, (core, out) in enumerate(zip(cores, (other, own))):
            for p in range(8):
                for half in range(2):
                    out[places(info, core, p, half, orders), g] = part[i, p, half]


def gather_blocks(info, natural, held):
    R = natural.shape[1]
    rel = lambda a, k: 1 - info[a] if k else info[a]
    for i, core in enumerate((1 - info[CORE], info[CORE])):
        for p in range(8):
            block = rel(ZH, p & 1) * 8 + rel(ZL, (p >> 1) & 1) * 4 + rel(Y, (p >> 2) & 1) * 2 + core
            held[(i * 8 + p) * R : (i * 8 + p + 1) * R, :] = natural[block]


def ffn_a_body(
    info, w, tok, tab, att, wo, ob, g2, b2, wu, ub, cot,
    mid_o, n2g, gf_o, act_o, gp_o, wd_o, dbs,
    n2_s, nat_s, actt_s, ub_s, *, rb,
):
    j = pl.program_id(0)
    S, D = tok.shape
    fb = wu.shape[1]
    R = nat_s.shape[1]
    blocks = [slice(i, i + rb) for i in range(0, S, rb)]

    @pl.when(j == 0)
    def _():
        sp = species_row(info, tab)
        total = None
        for r in blocks:
            mid = tok[r, :].astype(F32) + sp + nn(att[r, :], wo[...]) + vec(ob)
            mid_o[r, :] = mid
            n, _ = normed(mid)
            n2 = (n * vec(g2) + vec(b2)).astype(BF)
            n2_s[r, :] = n2
            nat_s[:, :, r] = n2.T.reshape(16, R, rb)
            row = r.start + lax.broadcasted_iota(jnp.int32, (rb, 1), 0)
            gf = jnp.where(row < info[LEN], cot[r, :].astype(F32), 0.0)
            gf_o[r, :] = gf.astype(BF)
            total = colsum(gf) if total is None else total + colsum(gf)
        dbs[...] = total
        gather_blocks(info, nat_s, n2g)
        bias = vec(ub)
        for c in range(ub_s.shape[0]):
            ub_s[c] = bias[:, c * fb : (c + 1) * fb]

    C = 0.7978845608
    C2 = C * 0.044715
    bias = ub_s[j]
    for r in blocks:
        u = nn(n2_s[r, :], wu[...]) + bias
        cu = C2 * (u * u)
        h = 0.5 * jnp.tanh(u * (cu + C)) + 0.5
        act = u * h
        ab = act.astype(BF)
        act_o[r, :] = ab
        actt_s[:, r] = ab.T
        gp_o[r, :] = (h + act * (1.0 - h) * (6.0 * cu + 2.0 * C)).astype(BF)
    wd_o[...] = nn(actt_s[...], gf_o[...]) * w[0]


def single(*shape):
    return pl.BlockSpec(shape, lambda *a: (0,) * len(shape), pipeline_mode=pl.Buffered(1))


def ffn_a(info, weight, tok, tab, att, wo, ob, g2, b2, wu, ub, cot, rb=256, after=()):
    S, D = tok.shape
    FF = wu.shape[1]
    n = FF // D
    cols = lambda m: pl.BlockSpec((m, D), lambda j, *_: (0, j))
    return call(
        partial(ffn_a_body, rb=rb), "ffn_a", (n,),
        [
            single(S, D), const(2, D), single(S, D), single(D, D), const(D), const(D), const(D),
            cols(D), const(FF), single(S, D),
        ],
        [single(S, D), single(D, S), single(S, D), cols(S), cols(S), pl.BlockSpec((D, D), lambda j, *_: (j, 0)), const(1, D)],
        [sds(S, D), sds(D, S, dt=BF), sds(S, D, dt=BF), sds(S, FF, dt=BF), sds(S, FF, dt=BF), sds(FF, D), sds(1, D)],
        scratch=[pltpu.VMEM((S, D), BF), pltpu.VMEM((16, D // 16, S), BF), pltpu.VMEM((D, S), BF), pltpu.VMEM((n, 1, D), F32)],
        prefetch=2, after=after,
    )(info, weight, tok, tab, att, wo, ob, g2, b2, wu, ub, cot)


def ffn_b_body(info, w, gf, wd, gp, n2g, gu, other, own, ubs, *, rb):
    S = gf.shape[0]
    total = None
    for i in range(0, S, rb):
        r = slice(i, i + rb)
        g = (nt(gf[r, :], wd[...]) * gp[r, :].astype(F32)).astype(BF)
        gu[r, :] = g
        here = colsum(g.astype(F32))
        total = here if total is None else total + here
    ubs[0] = total
    scatter_units(info, nn(n2g[...], gu[...]) * w[0], other, own, ORDERS["up"])


def ffn_b(info, weight, gf, wd, gp, n2g, rb=256, after=()):
    S, D = gf.shape
    FF = wd.shape[0]
    n = FF // D
    R, nb = D // 16, D // 3
    units = pl.BlockSpec((16, 3, R // 2, nb), lambda j, *_: (0, j, 0, 0))
    cols = pl.BlockSpec((S, D), lambda j, *_: (0, j))
    return call(
        partial(ffn_b_body, rb=rb), "ffn_b", (n,),
        [single(S, D), pl.BlockSpec((D, D), lambda j, *_: (j, 0)), cols, single(D, S)],
        [cols, units, units, pl.BlockSpec((1, 1, D), lambda j, *_: (j, 0, 0))],
        [sds(S, FF, dt=BF), sds(16, 3 * n, R // 2, nb), sds(16, 3 * n, R // 2, nb), sds(n, 1, D)],
        prefetch=2, after=after,
    )(info, weight, gf, wd, gp, n2g)


def ffn_c_body(gu, act, wu, wd, gf, mid_i, att, g2, wo, db, ga_o, gm_o, mixed_o, gb_o, attt, gs, bs, obs, gn_s, fe_s, *, rb):
    j = pl.program_id(0)
    last = pl.num_programs(0) - 1
    S = gf.shape[0]
    blocks = [slice(i, i + rb) for i in range(0, S, rb)]

    @pl.when(j == 0)
    def _():
        for r in blocks:
            fe_s[r, :] = nn(act[r, :], wd[...])
            gn_s[r, :] = nt(gu[r, :], wu[...])
        attt[...] = att[...].T

    @pl.when((j > 0) & (j < last))
    def _():
        for r in blocks:
            fe_s[r, :] += nn(act[r, :], wd[...])
            gn_s[r, :] += nt(gu[r, :], wu[...])

    @pl.when(j == last)
    def _():
        sums = None
        for r in blocks:
            mid = mid_i[r, :]
            gn = gn_s[r, :] + nt(gu[r, :], wu[...])
            n, rs = normed(mid)
            gm = gf[r, :].astype(F32) + norm_back(gn, n, rs, vec(g2))
            gm_o[r, :] = gm
            gb = gm.astype(BF)
            gb_o[r, :] = gb
            ga_o[r, :] = nt(gb, wo[...]).astype(BF)
            mixed_o[r, :] = (mid + (fe_s[r, :] + nn(act[r, :], wd[...])) + vec(db)).astype(BF)
            here = [colsum(gn * n), colsum(gn), colsum(gb.astype(F32))]
            sums = here if sums is None else [a + b for a, b in zip(sums, here)]
        gs[...], bs[...], obs[...] = sums


def ffn_c(gu, act, wu, wd, gf, mid, att, g2, wo, db, rb=256, after=()):
    S, D = gf.shape
    FF = wd.shape[0]
    cols = lambda m: pl.BlockSpec((m, D), lambda j: (0, j))
    return call(
        partial(ffn_c_body, rb=rb), "ffn_c", (FF // D,),
        [cols(S), cols(S), cols(D), pl.BlockSpec((D, D), lambda j: (j, 0)), single(S, D), single(S, D), single(S, D), const(D), single(D, D), const(D)],
        [single(S, D), single(S, D), single(S, D), single(S, D), single(D, S), const(1, D), const(1, D), const(1, D)],
        [sds(S, D, dt=BF), sds(S, D), sds(S, D, dt=BF), sds(S, D, dt=BF), sds(D, S, dt=BF), sds(1, D), sds(1, D), sds(1, D)],
        scratch=[pltpu.VMEM((S, D), F32), pltpu.VMEM((S, D), F32)], after=after,
    )(gu, act, wu, wd, gf, mid, att, g2, wo, db)


def to_core(a):
    return lax.ppermute(a, "dp", [(i, i ^ 1) for i in range(16)])


def to_stream(a):
    return lax.ppermute(a, "species", [(0, 1), (1, 0)])


class Sum:
    def __init__(self, name, parts):
        other, own = parts
        self.orders = ORDERS[name]
        self.own, self.got = own, to_core(other)
        self.step = 0

    def start(self, *after):
        n = self.own.shape[0] // 2
        got = tie(self.got, *after)
        self.send = self.own[n:] + got[n:]
        self.keep = [self.own[:n], got[:n]]
        return self.send

    def advance(self, *after):
        bits = [STEP[order[self.step]] for order in self.orders]
        got = lax.ppermute(self.send, ("species", "dp"), [(i, i ^ bits[i & 1]) for i in range(32)])
        got = tie(got, *after)
        self.step += 1
        n = got.shape[0] // 2
        terms = self.keep + [got]
        add = lambda lo, hi: sum((t[lo:hi] for t in terms[1:]), terms[0][lo:hi])
        if n:
            self.send, self.keep = add(n, 2 * n), [add(0, n)]
        else:
            self.send = add(0, 1)
            self.keep = [self.send]
        return self.send

    def finish(self):
        while self.step < 4:
            self.advance()
        unit = self.send[0]
        return unit, to_stream(unit)


def join_body(info, *refs, n, moves):
    pairs = [(refs[2 * i], refs[2 * i + 1]) for i in range(n)]
    outs = refs[2 * n :]
    up = info[X] == 1
    for i, g, o, c in moves:
        a, b = pairs[i][0][g], pairs[i][1][g]
        U, nb = a.shape
        if c is None:
            both = [a[:, :LANES], b[:, :LANES]]
            low, high = jnp.where(up, both[1], both[0]), jnp.where(up, both[0], both[1])
            rows = jnp.concatenate([low, high], axis=0).T
            outs[o][...] = rows[:2]
            for k in range(8):
                outs[o + 1 + k][...] = rows[2 + k]
            outs[o + 9][...] = rows[10 : 10 + outs[o + 9].shape[0]]
            continue
        outs[o][:U, c : c + nb] = jnp.where(up, b, a)
        outs[o][U:, c : c + nb] = jnp.where(up, a, b)


def join(info, pairs, moves, shapes, after=()):
    arrays = [a if a.ndim == 3 else a[None] for p in pairs for a in p]
    return call(
        partial(join_body, n=len(pairs), moves=moves), "join", (1,),
        [const(*a.shape) for a in arrays], [const(*s) for s in shapes], [sds(*s) for s in shapes], prefetch=1, after=after,
    )(info, *arrays)


def stack_body(info, w, *refs):
    *parts, o = refs
    D = o.shape[1]
    sp, rest, up = parts[0], parts[1:-1], parts[-1]
    o[...] = jnp.zeros_like(o)
    for k in range(2):
        o[k : k + 1, :] = jnp.where(info[ID] == k, sp[...], 0.0) * w[0]
    for k, r in enumerate(rest):
        o[2 + k : 3 + k, :] = r[...] * w[0]
    for k in range(up.shape[1] // D):
        o[2 + len(rest) + k : 3 + len(rest) + k, :] = up[:, k * D : (k + 1) * D] * w[0]


def stack(info, weight, parts, after=()):
    D = parts[0].shape[1]
    rows = 1 + sum(p.shape[1] // D for p in parts)
    rows += -rows % 8
    return call(
        stack_body, "stack", (1,), [const(*p.shape) for p in parts], const(rows, D), sds(rows, D), prefetch=2, after=after,
    )(info, weight, *parts)


def flat(chunks):
    return jnp.concatenate(list(chunks), axis=1)


def local(
    tokens, cotangent, lengths, species_ids, species_table, ln1_gain, ln1_bias, w_qkv, q_bias, v_bias,
    w_out, out_bias, ln2_gain, ln2_bias, w_up, up_bias, w_down, down_bias, *, dp_size,
):
    D = tokens.shape[2]
    hd = D // HEADS
    scale = hd ** (-0.5)
    FF = w_up.shape[1]
    tok = tokens[0]
    cot = cotangent[0]
    paired = dp_size == 16
    dp = lax.axis_index("dp")
    x = lax.axis_index("species")
    info = jnp.stack([lengths[0], species_ids[0], dp % 2, (dp // 2) % 2, (dp // 4) % 2, dp // 8, x]).astype(jnp.int32)
    length_float = lengths[0].astype(F32)

    exchange = lambda a, bit: lax.ppermute(a, "dp", [(i, i ^ bit) for i in range(16)])
    gather = lambda a, *bits: [exchange(a, bit) for bit in bits]
    qkv, n1t = qkv_proj(info, tok, species_table, ln1_gain, ln1_bias, w_qkv, q_bias, v_bias)
    hops = []
    if paired:
        count = jnp.full((8, LANES), length_float)
        count = count + sum(tie(c, n1t) for c in gather(count, 1, 2, 3))
        hops = [count]
    att, att_f32, nl = attn_fwd(info, qkv, scale, hd, after=hops)
    if paired:
        count = count + sum(tie(c, nl) for c in gather(count, 4, 8, 12))
        hops = [count]
    back = lambda first, count, after: attn_bwd(info, qkv, att_f32, ga, nl, first, count, scale, hd, after=after)
    if paired:
        nb = D // 3
        scatter = lambda a: lax.psum_scatter(a, "dp", scatter_dimension=0, tiled=True)
        mid, n2g, gf, act, gp, part, down_part = ffn_a(
            info, length_float.reshape(1), tok, species_table, att, w_out, out_bias, ln2_gain, ln2_bias, w_up, up_bias, cot, after=hops
        )
        down = scatter(part)
        share_weight = 1.0 / (2.0 * count[0, 0])
        weight = (length_float * share_weight).reshape(1)
        gu, up_other, up_own, up_part = ffn_b(info, weight, gf, w_down, gp, n2g, after=[part])
        up = Sum("up", (up_other, up_own))
        ga, gm, mixed, gb, attt, ln2g_part, ln2b_part, ob_part = ffn_c(
            gu, act, w_up, w_down, gf, mid, att, ln2_gain, w_out, down_bias, after=[up_part]
        )
        up.start(ob_part)
        gq0 = back(0, 5, [up.send])
        first = Sum("first", wide_grad(info, weight, [n1t, n1t, attt], [[(gq0, 0)], [(gq0, 1)], [gb]], nb, ORDERS["first"], after=[gq0]))
        up.advance(first.own)
        gq1 = back(5, 1, [first.own, up.send])
        first.start(gq1)
        up.advance(first.send)
        gt, ln1g_part, ln1b_part, sp_part, qb_part, vb_part = back1(
            info, [gq0, gq1], w_qkv, tok, species_table, ln1_gain, gm, after=[first.send, up.send]
        )
        up.advance(sp_part)
        down = tie(down, up.send) * share_weight
        n = D // dp_size
        last = Sum("last", last_grad(
            info, weight, n1t, [(gq0, 4), (gq1, 0)],
            [sp_part, ln1g_part, ln1b_part, qb_part, vb_part, ob_part, ln2g_part, ln2b_part, down_part, up_part],
            nb, ORDERS["last"], after=[up.send, down],
        ))
        first.advance(last.own)
        last.start(first.send)
        up.advance(last.send)
        first.advance(up.send)
        last.advance(first.send)
        down_other = to_stream(tie(down, last.send))
        up_pair = up.finish()
        up_pair = (up_pair[0], tie(up_pair[1], last.send))
        (g_up,) = join(info, [up_pair], [(0, g, 0, g * nb) for g in range(FF // nb)], [(n, FF)])
        last.advance(g_up)
        first.advance(last.send)
        last.advance(first.send)
        first.advance(last.send)
        last.advance(first.send)
        g_down = down + tie(down_other, last.send)
    else:
        weight = (length_float / (2.0 * lax.psum(length_float, "dp"))).reshape(1)
        mid, n2t, act, actt, gp, gf, attt, down_part = mid1(
            info, tok, species_table, att, w_out, out_bias, ln2_gain, ln2_bias, w_up, up_bias, cot
        )
        gu, up_part = mid2(gf, w_down, gp)
        gm, gb, ga, ln2g_part, ln2b_part, ob_part = back2(info, gu, w_up, mid, ln2_gain, cot, w_out)
        gqs = [back(0, D // LANES, ())]
        gt, ln1g_part, ln1b_part, sp_part, qb_part, vb_part = back1(info, gqs, w_qkv, tok, species_table, ln1_gain, gm)
        mixed = mixed_out(act, w_down, mid, down_bias)
        small = stack(info, weight, [sp_part, ln1g_part, ln1b_part, qb_part, vb_part, ob_part, ln2g_part, ln2b_part, down_part, up_part])
        small = lax.psum(lax.psum(small, "dp"), "species")
    n = D // dp_size
    if not paired:
        share = lambda r: lax.dynamic_slice_in_dim(small[r], dp * n, n)
        species = lax.dynamic_slice_in_dim(small[:2], dp * n, n, axis=1)
        up_share = lax.dynamic_slice_in_dim(small[10 : 10 + FF // D].reshape(-1), dp * (FF // dp_size), FF // dp_size)
    if paired:
        moves = [(0, 3 * h + t, 0, t * D + h * nb) for t in range(3) for h in range(2)]
        moves += [(1, t, 0, t * D + 2 * nb) for t in range(3)] + [(1, 3, 2, None)] + [(0, 6 + t, 1, t * nb) for t in range(3)]
        g_qkv, g_out, species, *vectors, up_share = join(
            info, [first.finish(), last.finish()], moves, [(n, 3 * D), (n, D), (2, n)] + [(n,)] * 8 + [(FF // D, n)]
        )
        share = lambda r: vectors[r - 2]
        up_share = up_share.reshape(-1)
    else:
        def total(part):
            return lax.psum(lax.psum_scatter(part, "dp", scatter_dimension=0, tiled=True), "species")

        g_down = total(wgrad(weight, actt, gf))
        g_up = total(wgrad(weight, n2t, gu))
        g_out = total(wgrad(weight, attt, gb))
        g_qkv = total(wgrad(weight, n1t, flat(gqs[0])))
    return (
        mixed[None], gt[None], species, share(2), share(3), g_qkv, share(4), share(5), g_out, share(6),
        share(7), share(8), g_up, up_share, g_down, share(9),
    )


def solution(mesh):
    cells = P(("species", "dp"), None, None)
    scalars = P(("species", "dp"))
    in_specs = (cells, cells, scalars, scalars) + (P(),) * 14
    v, m = P("dp"), P("dp", None)
    out_specs = (cells, cells, P(None, "dp"), v, v, m, v, v, m, v, v, v, m, v, m, v)
    return jax.shard_map(
        partial(local, dp_size=mesh.shape["dp"]), mesh=mesh, in_specs=in_specs, out_specs=out_specs, check_vma=False
    )
```

```python
from functools import partial

import jax
import jax.numpy as jnp
from jax import lax
from jax.experimental import pallas as pl
from jax.experimental.pallas import tpu as pltpu
from jax.sharding import PartitionSpec as P

HEADS = 12
F32 = jnp.float32
BF = jnp.bfloat16
LOG2E = 1.4426950408889634
MIB = 1 << 20
LANES = 128


def nt(a, b):
    return lax.dot_general(a, b, (((1,), (1,)), ((), ())), preferred_element_type=F32)


def nn(a, b):
    return lax.dot_general(a, b, (((1,), (0,)), ((), ())), preferred_element_type=F32)


def tie(a, *after):
    return lax.optimization_barrier((a, *after))[0] if after else a


def call(body, name, grid, ins, outs, shapes, scratch=(), prefetch=0, mib=56, after=(), us=0.05):
    f = pl.pallas_call(
        body,
        grid_spec=pltpu.PrefetchScalarGridSpec(
            num_scalar_prefetch=prefetch, grid=grid, in_specs=ins, out_specs=outs, scratch_shapes=list(scratch)
        ),
        out_shape=shapes,
        compiler_params=pltpu.CompilerParams(vmem_limit_bytes=mib * MIB),
        cost_estimate=pl.CostEstimate(flops=1000, bytes_accessed=int(us * 3.2e6), transcendentals=0),
        name=name,
    )
    return lambda first, *rest: f(tie(first, *after), *rest)


def const(*shape):
    return pl.BlockSpec(shape, lambda *a: (0,) * len(shape))


def sds(*shape, dt=F32):
    return jax.ShapeDtypeStruct(shape, dt)


def normed(x):
    c = x - jnp.mean(x, axis=-1, keepdims=True)
    r = lax.rsqrt(jnp.mean(c * c, axis=-1, keepdims=True) + 1e-5)
    return c * r, r


def norm_back(g, n, r, gain):
    e = g * gain
    return r * (e - jnp.mean(e, axis=-1, keepdims=True) - n * jnp.mean(e * n, axis=-1, keepdims=True))


def colsum(x):
    return jnp.sum(x, axis=0, keepdims=True)


def rows_of(rb, n):
    return pl.BlockSpec((rb, n), lambda i, *_: (i, 0))


def cols_of(n, rb):
    return pl.BlockSpec((n, rb), lambda i, *_: (0, i))


LEN, ID, CORE, Y, ZL, ZH, X = range(7)


def vec(ref):
    return ref[...].astype(F32)[None, :]


def species_row(info, table):
    rows = table[...].astype(F32)
    return jnp.where(info[ID] == 0, rows[0:1], rows[1:2])


def qkv_body(info, tok, tab, g, b, w, qb, vb, qkv, n1t):
    n, _ = normed(tok[...].astype(F32) + species_row(info, tab))
    nb = (n * vec(g) + vec(b)).astype(BF)
    n1t[...] = nb.T
    bias = jnp.concatenate([vec(qb), jnp.zeros((1, tok.shape[1]), F32), vec(vb)], axis=1)
    qkv[...] = (nn(nb, w[...]) + bias).astype(BF)


def qkv_proj(info, tok, tab, g, b, w, qb, vb, rb=256):
    S, D = tok.shape
    N = w.shape[1]
    return call(
        qkv_body, "qkv_proj", (S // rb,),
        [rows_of(rb, D), const(2, D), const(D), const(D), const(D, N), const(D), const(D)],
        [rows_of(rb, N), cols_of(D, rb)],
        [sds(S, N, dt=BF), sds(D, S, dt=BF)], prefetch=1,
    )(info, tok, tab, g, b, w, qb, vb)


def split2(x):
    hi = x.astype(BF)
    return hi, (x - hi.astype(F32)).astype(BF)


def split3(x):
    a = x.astype(BF).astype(F32)
    r = x - a
    b = r.astype(BF).astype(F32)
    return a, b, r - b


def attn_fwd_body(ln, q_ref, k_ref, v_ref, o_ref, of_ref, nl_ref, *, scale, qb, hd):
    S = q_ref.shape[0]
    lane = lax.broadcasted_iota(jnp.int32, (1, LANES), 1)
    row = lax.broadcasted_iota(jnp.int32, (S, 1), 0)
    mask = jnp.where(row < ln[0], 0.0, -1e30).astype(F32)
    kk = k_ref[...]
    kf = kk.astype(F32)
    vf = v_ref[...].astype(F32)
    hi, lo = split2(q_ref[...].astype(F32) * (scale * LOG2E))
    hi = hi.astype(F32)
    lo = lo.astype(F32)
    qa, ka, va = [], [], []
    for h in range(2):
        own = (lane // hd) == h
        aux = lane == (1 - h) * hd
        k2 = jnp.where(own, kf, jnp.where(aux, mask, 0.0)).astype(BF)
        ka.append(jnp.concatenate([kk, k2], axis=1))
        q1 = jnp.where(own, hi, 0.0).astype(BF)
        q2 = jnp.where(own, lo, jnp.where(aux, 1.0, 0.0)).astype(BF)
        qa.append(jnp.concatenate([q1, q2], axis=1))
        va.append(jnp.where(own, vf, 1.0).astype(BF))
    for b in range(S // qb):
        sl = slice(b * qb, (b + 1) * qb)
        outs, nls = [], []
        for h in range(2):
            s = nt(qa[h][sl], ka[h])
            m = jnp.max(s, axis=1, keepdims=True)
            p = jnp.exp2(s - m).astype(BF)
            o = nn(p, va[h])
            outs.append(o / pltpu.roll(o, hd, 1))
            nls.append(-(m + jnp.log2(o)))
        o = jnp.where(lane < hd, outs[0], outs[1])
        of_ref[sl, :] = o
        o_ref[sl, :] = o.astype(BF)
        nl_ref[sl, :] = jnp.where(lane < hd, nls[1], nls[0])


def attn_fwd(ln, qkv, scale, hd, qb=512, after=()):
    S, D = qkv.shape[0], qkv.shape[1] // 3
    n = D // LANES
    qb = min(qb, S)
    cb = lambda off: pl.BlockSpec((S, LANES), lambda p, l: (0, off + p))
    return call(
        partial(attn_fwd_body, scale=scale, qb=qb, hd=hd), "attn_fwd", (n,),
        [cb(0), cb(n), cb(2 * n)], [cb(0), cb(0), cb(0)],
        [sds(S, D, dt=BF), sds(S, D), sds(S, D)], prefetch=1, after=after,
    )(ln, qkv, qkv, qkv)


def attn_bwd_body(ln, q_ref, k_ref, v_ref, o_ref, do_ref, nl_ref, g_ref, dqt_ref, kt_ref, ka_ref, va_ref, *, scale, kb, hd):
    S = q_ref.shape[0]
    n = ln[0]
    lane = lax.broadcasted_iota(jnp.int32, (1, LANES), 1)
    row = lax.broadcasted_iota(jnp.int32, (S, 1), 0)
    mask = jnp.where(row < n, 0.0, -1e30).astype(F32)
    kk = k_ref[...]
    kf = kk.astype(F32)
    vf = v_ref[...].astype(F32)
    dof = do_ref[...].astype(F32)
    qf = q_ref[...].astype(F32)
    hi, lo = split2(qf * (scale * LOG2E))
    hi = hi.astype(F32)
    lo = lo.astype(F32)
    n0, n1, n2 = split3(nl_ref[...])
    do_o = dof * o_ref[...]
    kt_ref[...] = kf.T.astype(BF)
    qa, qo, da, do_own = [], [], [], []
    for h in range(2):
        own = (lane // hd) == h
        base = (1 - h) * hd
        three = (lane > base) & (lane < base + 4)
        pick = lambda a, b, c: jnp.where(lane == base + 1, a, jnp.where(lane == base + 2, b, jnp.where(lane == base + 3, c, 0.0)))
        ka_ref[h, :, 0:LANES] = kk
        ka_ref[h, :, LANES:] = jnp.where(own, kf, jnp.where(lane == base, mask, jnp.where(three, 1.0, 0.0))).astype(BF)
        va_ref[h] = jnp.where(own, vf, jnp.where(three, 1.0, 0.0)).astype(BF)
        q1 = jnp.where(own, hi, 0.0).astype(BF)
        q2 = jnp.where(own, lo, jnp.where(lane == base, 1.0, pick(n0, n1, n2))).astype(BF)
        qa.append(jnp.concatenate([q1, q2], axis=1))
        qo.append(jnp.where(own, qf, 0.0).astype(BF))
        delta = -jnp.sum(jnp.where(own, do_o, 0.0), axis=1, keepdims=True)
        do_own.append(jnp.where(own, dof, 0.0).astype(BF))
        da.append(jnp.where(own, dof, pick(*split3(delta))).astype(BF))
    for b in range(S // kb):
        sl = slice(b * kb, (b + 1) * kb)

        @pl.when(b * kb < n)
        def _():
            dv = dk = None
            for h in range(2):
                p = jnp.exp2(nt(ka_ref[h, sl, :], qa[h]))
                ds = (p * nt(va_ref[h, sl, :], da[h])).astype(BF)
                dvh = nn(p.astype(BF), do_own[h])
                dkh = nn(ds, qo[h])
                dv = dvh if h == 0 else dv + dvh
                dk = dkh if h == 0 else dk + dkh
                dqt = nn(kt_ref[h * hd : (h + 1) * hd, sl], ds)
                if b == 0:
                    dqt_ref[h * hd : (h + 1) * hd, :] = dqt
                else:
                    dqt_ref[h * hd : (h + 1) * hd, :] += dqt
            g_ref[1, sl, :] = (dk * scale).astype(BF)
            g_ref[2, sl, :] = dv.astype(BF)

        @pl.when(b * kb >= n)
        def _():
            g_ref[1, sl, :] = jnp.zeros((kb, LANES), BF)
            g_ref[2, sl, :] = jnp.zeros((kb, LANES), BF)

    g_ref[0] = (dqt_ref[...].T * scale).astype(BF)


def attn_bwd(ln, qkv, o, do, nl, first, count, scale, hd, kb=1024, after=()):
    S, D = qkv.shape[0], qkv.shape[1] // 3
    n = D // LANES
    kb = min(kb, S)
    cb = lambda off: pl.BlockSpec((S, LANES), lambda p, l: (0, off + first + p))
    return call(
        partial(attn_bwd_body, scale=scale, kb=kb, hd=hd), "attn_bwd", (count,),
        [cb(0), cb(n), cb(2 * n), cb(0), cb(0), cb(0)],
        pl.BlockSpec((3, S, LANES), lambda p, l: (0, 0, p)),
        sds(3, S, count * LANES, dt=BF),
        scratch=[pltpu.VMEM((LANES, S), F32), pltpu.VMEM((LANES, S), BF), pltpu.VMEM((2, S, 2 * LANES), BF), pltpu.VMEM((2, S, LANES), BF)],
        prefetch=1, after=after, us=9 if count == 1 else 0.05,
    )(ln, qkv, qkv, qkv, o, do, nl)


def mid1_body(info, tok, tab, att, wo, ob, g2, b2, wu, ub, cot, mid_o, n2t, act_o, actt, gp_o, gf_o, attt, dbs, *, fb):
    i = pl.program_id(0)
    rb = tok.shape[0]
    FF = wu.shape[1]
    a = att[...]
    attt[...] = a.T
    mid = tok[...].astype(F32) + species_row(info, tab) + nn(a, wo[...]) + vec(ob)
    mid_o[...] = mid
    n, _ = normed(mid)
    n2 = (n * vec(g2) + vec(b2)).astype(BF)
    n2t[...] = n2.T
    row = i * rb + lax.broadcasted_iota(jnp.int32, (rb, 1), 0)
    gf = jnp.where(row < info[LEN], cot[...].astype(F32), 0.0)
    gf_o[...] = gf.astype(BF)

    @pl.when(i == 0)
    def _():
        dbs[...] = jnp.zeros_like(dbs)

    dbs[...] += colsum(gf)
    C = 0.7978845608
    C2 = C * 0.044715
    bias = vec(ub)
    for j in range(FF // fb):
        sl = slice(j * fb, (j + 1) * fb)
        u = nn(n2, wu[:, sl]) + bias[:, sl]
        cu = C2 * (u * u)
        h = 0.5 * jnp.tanh(u * (cu + C)) + 0.5
        act = u * h
        ab = act.astype(BF)
        act_o[:, sl] = ab
        actt[sl, :] = ab.T
        gp_o[:, sl] = (h + act * (1.0 - h) * (6.0 * cu + 2.0 * C)).astype(BF)


def mid1(info, tok, tab, att, wo, ob, g2, b2, wu, ub, cot, rb=256, fb=768):
    S, D = tok.shape
    FF = wu.shape[1]
    r = partial(rows_of, rb)
    t = lambda n: cols_of(n, rb)
    return call(
        partial(mid1_body, fb=fb), "mid1", (S // rb,),
        [r(D), const(2, D), r(D), const(D, D), const(D), const(D), const(D), const(D, FF), const(FF), r(D)],
        [r(D), t(D), r(FF), t(FF), r(FF), r(D), t(D), const(1, D)],
        [sds(S, D), sds(D, S, dt=BF), sds(S, FF, dt=BF), sds(FF, S, dt=BF), sds(S, FF, dt=BF), sds(S, D, dt=BF), sds(D, S, dt=BF), sds(1, D)],
        prefetch=1,
    )(info, tok, tab, att, wo, ob, g2, b2, wu, ub, cot)


def mid2_body(gf, wd, gp, gu_o, ubs):
    gu = (nt(gf[...], wd[...]) * gp[...].astype(F32)).astype(BF)
    gu_o[...] = gu
    ubs[...] = colsum(gu.astype(F32))


def mid2(gf, wd, gp, nb=512, after=()):
    S, D = gf.shape
    FF = wd.shape[0]
    t = lambda n: pl.BlockSpec((n, nb), lambda j: (0, j))
    return call(
        mid2_body, "mid2", (FF // nb,),
        [const(S, D), pl.BlockSpec((nb, D), lambda j: (j, 0)), t(S)],
        [t(S), t(1)], [sds(S, FF, dt=BF), sds(1, FF)], after=after,
    )(gf, wd, gp)


def back2_body(ln, gu, wu, mid, g2, cot, wo, gm_o, gb_o, ga_o, gs, bs, obs):
    i = pl.program_id(0)
    rb = mid.shape[0]
    gn = nt(gu[...], wu[...])
    n, r = normed(mid[...])
    row = i * rb + lax.broadcasted_iota(jnp.int32, (rb, 1), 0)
    gf = jnp.where(row < ln[0], cot[...].astype(F32), 0.0)
    gm = gf + norm_back(gn, n, r, vec(g2))
    gm_o[...] = gm
    gb = gm.astype(BF)
    gb_o[...] = gb
    ga_o[...] = nt(gb, wo[...]).astype(BF)

    @pl.when(i == 0)
    def _():
        for s in (gs, bs, obs):
            s[...] = jnp.zeros_like(s)

    gs[...] += colsum(gn * n)
    bs[...] += colsum(gn)
    obs[...] += colsum(gb.astype(F32))


def back2(ln, gu, wu, mid, g2, cot, wo, rb=256, after=()):
    S, D = mid.shape
    FF = wu.shape[1]
    r = partial(rows_of, rb)
    return call(
        back2_body, "back2", (S // rb,),
        [r(FF), const(D, FF), r(D), const(D), r(D), const(D, D)],
        [r(D), r(D), r(D), const(1, D), const(1, D), const(1, D)],
        [sds(S, D), sds(S, D, dt=BF), sds(S, D, dt=BF), sds(1, D), sds(1, D), sds(1, D)],
        prefetch=1, after=after,
    )(ln, gu, wu, mid, g2, cot, wo)


def back1_body(info, *refs):
    *gq, w, tok, tab, g1, gm, gt_o, gs, bs, ss, qs, vs = refs
    i = pl.program_id(0)
    D = tok.shape[1]
    gn = None
    for t in range(3):
        whole = jnp.concatenate([g[t] for g in gq], axis=1)
        part = nt(whole, w[:, t * D : (t + 1) * D])
        gn = part if gn is None else gn + part
    n, r = normed(tok[...].astype(F32) + species_row(info, tab))
    g = gm[...] + norm_back(gn, n, r, vec(g1))
    gt_o[...] = g.astype(BF)

    @pl.when(i == 0)
    def _():
        for s in (gs, bs, ss, qs, vs):
            s[...] = jnp.zeros_like(s)

    gs[...] += colsum(gn * n)
    bs[...] += colsum(gn)
    ss[...] += colsum(g)
    qs[...] += colsum(jnp.concatenate([g[0] for g in gq], axis=1).astype(F32))
    vs[...] += colsum(jnp.concatenate([g[2] for g in gq], axis=1).astype(F32))


def back1(info, gq, w, tok, tab, g1, gm, rb=256, after=()):
    S, D = tok.shape
    r = partial(rows_of, rb)
    return call(
        back1_body, "back1", (S // rb,),
        [pl.BlockSpec((3, rb, g.shape[2]), lambda i, n: (0, i, 0)) for g in gq] + [const(D, 3 * D), r(D), const(2, D), const(D), r(D)],
        [r(D)] + [const(1, D)] * 5,
        [sds(S, D, dt=BF)] + [sds(1, D)] * 5, prefetch=1, after=after, us=11,
    )(info, *gq, w, tok, tab, g1, gm)


def mixed_body(act, wd, mid, db, o):
    o[...] = (mid[...] + nn(act[...], wd[...]) + vec(db)).astype(BF)


def mixed_out(act, wd, mid, db, first=0, count=4, rb=256, after=()):
    D = mid.shape[1]
    FF = wd.shape[0]
    r = lambda n: pl.BlockSpec((rb, n), lambda i: (first + i, 0))
    return call(
        mixed_body, "mixed_out", (count,),
        [r(FF), const(FF, D), r(D), const(D)], rows_of(rb, D), sds(count * rb, D, dt=BF), after=after,
    )(act, wd, mid, db)


def wgrad_body(w, a, b, o):
    o[...] = nn(a[...], b[...]) * w[0]


def wgrad(weight, at, b, nb=768, after=()):
    M, S = at.shape
    N = b.shape[1]
    mb = min(M, 768)
    return call(
        wgrad_body, "wgrad", (M // mb, N // nb),
        [pl.BlockSpec((mb, S), lambda i, j, w: (i, 0)), pl.BlockSpec((S, nb), lambda i, j, w: (0, j))],
        pl.BlockSpec((mb, nb), lambda i, j, w: (i, j)), sds(M, N),
        prefetch=1, after=after,
    )(weight, at, b)


NUMBER = {"y": Y, "zl": ZL, "zh": ZH, "x": X}
STEP = {"y": 2, "zl": 4, "zh": 8, "x": 16}
YX = (("y", "zl", "zh", "x"), ("x", "y", "zl", "zh"))
ZX = (("zl", "x", "y", "zh"), ("x", "zl", "y", "zh"))
YXZ = (("y", "x", "zl", "zh"), ("x", "y", "zh", "zl"))
XYZ = (("y", "x", "zl", "zh"), ("x", "y", "zl", "zh"))
ORDERS = {"up": YXZ, "first": YX, "last": XYZ}


def places(info, core, p, half, orders):
    far = 1 - info[X] if half else info[X]
    bit = {"y": (p >> 2) & 1, "zl": (p >> 1) & 1, "zh": p & 1, "x": far}
    at = [sum(bit[a] * (8 >> k) for k, a in enumerate(order)) for order in orders]
    return jnp.where(core == 0, at[0], at[1])


def wide_body(info, w, *refs, counts, steps, orders):
    n = sum(counts)
    many_lhs = len(counts)
    lefts, rhs, (other, own, held) = refs[:many_lhs], refs[many_lhs : many_lhs + n], refs[many_lhs + n :]
    j = pl.program_id(0)
    R = lefts[0].shape[2]
    nb = other.shape[-1]
    cores = (1 - info[CORE], info[CORE])

    def bring(lhs):
        rel = lambda a, k: 1 - info[a] if k else info[a]
        for i, core in enumerate(cores):
            for p in range(8):
                block = rel(ZH, p & 1) * 4 + rel(ZL, (p >> 1) & 1) * 2 + rel(Y, (p >> 2) & 1)
                held[(i * 8 + p) * R : (i * 8 + p + 1) * R, :] = lhs[block, core]

    at, lo = 0, 0
    for left, many, count in zip(lefts, counts, steps):
        parts = rhs[at : at + many]

        def run(parts=parts, left=left, many=many):
            bring(left)
            for t in range(3):
                if len(parts[0].shape) == 3:
                    b = [r[t] for r in parts]
                    b = b[0] if many == 1 else jnp.concatenate(b, axis=1)
                else:
                    b = parts[0][:, t * (parts[0].shape[1] // 3) : (t + 1) * (parts[0].shape[1] // 3)]
                G = b.shape[1] // nb
                res = nn(held[...], b) * w[0]
                for h in range(G):
                    part = res[:, h * nb : (h + 1) * nb].reshape(2, 8, 2, R // 2, nb)
                    for i, (core, out) in enumerate(zip(cores, (other, own))):
                        for p in range(8):
                            for half in range(2):
                                out[places(info, core, p, half, orders), t * G + h] = part[i, p, half]

        pl.when((j >= lo) & (j < lo + count))(run)
        at, lo = at + many, lo + count


def wide_grad(info, weight, lhs, rhs, nb, orders, after=()):
    S = lhs[0].shape[1]
    R = lhs[0].shape[0] // 16
    specs, arrays = [], []
    for b in (b for group in rhs for b in group):
        b, k = b if isinstance(b, tuple) else (b, None)
        arrays.append(b)
        specs.append(const(*b.shape) if k is None else pl.BlockSpec((3, S, nb), lambda *_, k=k: (0, 0, k)))
    return call(
        partial(wide_body, counts=[len(g) for g in rhs], steps=[1] * len(rhs), orders=orders), "wide_grad", (len(rhs),),
        [const(8, 2, R, S) for _ in lhs] + specs,
        [pl.BlockSpec((16, 3, R // 2, nb), lambda j, *_: (0, j, 0, 0))] * 2,
        [sds(16, 3 * len(rhs), R // 2, nb)] * 2,
        scratch=[pltpu.VMEM((16 * R, S), BF)], prefetch=2, after=after, us=10,
    )(info, weight, *[a.reshape(8, 2, R, S) for a in lhs], *arrays)


def last_body(info, w, lhs, *refs, n, orders):
    rhs, parts = refs[:n], refs[n:-5]
    other, own, held, rows, turned = refs[-5:]
    R = lhs.shape[2]
    nb = other.shape[-1]
    cores = (1 - info[CORE], info[CORE])
    rel = lambda a, k: 1 - info[a] if k else info[a]
    for i, core in enumerate(cores):
        for p in range(8):
            block = rel(ZH, p & 1) * 4 + rel(ZL, (p >> 1) & 1) * 2 + rel(Y, (p >> 2) & 1)
            held[(i * 8 + p) * R : (i * 8 + p + 1) * R, :] = lhs[block, core]
    for t in range(3):
        res = nn(held[...], jnp.concatenate([r[t] for r in rhs], axis=1)) * w[0]
        part = res.reshape(2, 8, 2, R // 2, nb)
        for i, (core, out) in enumerate(zip(cores, (other, own))):
            for p in range(8):
                for half in range(2):
                    out[places(info, core, p, half, orders), t] = part[i, p, half]
    sp, *rest, up = parts
    rows[...] = jnp.zeros_like(rows)
    for k in range(2):
        rows[k : k + 1, :] = jnp.where(info[ID] == k, sp[...], 0.0) * w[0]
    at = 2
    for r in rest:
        rows[at : at + 1, :] = r[...] * w[0]
        at += 1
    D = rows.shape[1]
    many = up.shape[0]
    for k in range(many):
        rows[at + k : at + k + 1, :] = up[k] * w[0]
    turned[...] = rows[...].T
    blank = jnp.zeros((R // 2, nb - LANES), F32)
    lane = lax.broadcasted_iota(jnp.int32, (1, LANES), 1)
    span = many * R
    for core, out in zip(cores, (other, own)):
        for p in range(8):
            block = rel(ZH, p & 1) * 8 + rel(ZL, (p >> 1) & 1) * 4 + rel(Y, (p >> 2) & 1) * 2 + core
            row, start = block * span // D, block * span % D
            for half in range(2):
                place = places(info, core, p, half, orders)
                here = pl.ds(pl.multiple_of(block * R + half * (R // 2), 8), R // 2)
                value = jnp.where(lane < at, turned[here, :], 0.0)
                for k in range(many):
                    there = pl.ds(pl.multiple_of(start + k * R + half * (R // 2), 8), R // 2)
                    column = jnp.sum(jnp.where(lane == at + row, turned[there, :], 0.0), axis=1, keepdims=True)
                    value = jnp.where(lane == at + k, column, value)
                out[place, 3, :, :LANES] = value
                out[place, 3, :, LANES:] = blank


def last_grad(info, weight, lhs, rhs, parts, nb, orders, after=()):
    D, S = lhs.shape
    R = D // 16
    units = const(16, 4, R // 2, nb)
    lanes = [pl.BlockSpec((3, S, LANES), lambda *_, k=k: (0, 0, k)) for _, k in rhs]
    return call(
        partial(last_body, n=len(rhs), orders=orders), "last_grad", (1,),
        [const(8, 2, R, S)] + lanes + [const(*b.shape) for b in parts], [units, units], [sds(16, 4, R // 2, nb)] * 2,
        scratch=[pltpu.VMEM((D, S), BF), pltpu.VMEM((LANES, D), F32), pltpu.VMEM((D, LANES), F32)],
        prefetch=2, after=after,
    )(info, weight, lhs.reshape(8, 2, R, S), *[b for b, _ in rhs], *parts)


def scatter_units(info, res, other, own, orders):
    nb = other.shape[-1]
    R = res.shape[0] // 16
    cores = (1 - info[CORE], info[CORE])
    for g in range(res.shape[1] // nb):
        part = res[:, g * nb : (g + 1) * nb].reshape(2, 8, 2, R // 2, nb)
        for i, (core, out) in enumerate(zip(cores, (other, own))):
            for p in range(8):
                for half in range(2):
                    out[places(info, core, p, half, orders), g] = part[i, p, half]


def gather_blocks(info, natural, held):
    R = natural.shape[1]
    rel = lambda a, k: 1 - info[a] if k else info[a]
    for i, core in enumerate((1 - info[CORE], info[CORE])):
        for p in range(8):
            block = rel(ZH, p & 1) * 8 + rel(ZL, (p >> 1) & 1) * 4 + rel(Y, (p >> 2) & 1) * 2 + core
            held[(i * 8 + p) * R : (i * 8 + p + 1) * R, :] = natural[block]


def ffn_a_body(
    info, w, tok, tab, att, wo, ob, g2, b2, wu, ub, cot,
    mid_o, n2g, gf_o, act_o, gp_o, wd_o, dbs,
    n2_s, nat_s, actt_s, ub_s, *, rb,
):
    j = pl.program_id(0)
    S, D = tok.shape
    fb = wu.shape[1]
    R = nat_s.shape[1]
    blocks = [slice(i, i + rb) for i in range(0, S, rb)]

    @pl.when(j == 0)
    def _():
        sp = species_row(info, tab)
        total = None
        for r in blocks:
            mid = tok[r, :].astype(F32) + sp + nn(att[r, :], wo[...]) + vec(ob)
            mid_o[r, :] = mid
            n, _ = normed(mid)
            n2 = (n * vec(g2) + vec(b2)).astype(BF)
            n2_s[r, :] = n2
            nat_s[:, :, r] = n2.T.reshape(16, R, rb)
            row = r.start + lax.broadcasted_iota(jnp.int32, (rb, 1), 0)
            gf = jnp.where(row < info[LEN], cot[r, :].astype(F32), 0.0)
            gf_o[r, :] = gf.astype(BF)
            total = colsum(gf) if total is None else total + colsum(gf)
        dbs[...] = total
        gather_blocks(info, nat_s, n2g)
        bias = vec(ub)
        for c in range(ub_s.shape[0]):
            ub_s[c] = bias[:, c * fb : (c + 1) * fb]

    C = 0.7978845608
    C2 = C * 0.044715
    bias = ub_s[j]
    for r in blocks:
        u = nn(n2_s[r, :], wu[...]) + bias
        cu = C2 * (u * u)
        h = 0.5 * jnp.tanh(u * (cu + C)) + 0.5
        act = u * h
        ab = act.astype(BF)
        act_o[r, :] = ab
        actt_s[:, r] = ab.T
        gp_o[r, :] = (h + act * (1.0 - h) * (6.0 * cu + 2.0 * C)).astype(BF)
    wd_o[...] = nn(actt_s[...], gf_o[...]) * w[0]


def single(*shape):
    return pl.BlockSpec(shape, lambda *a: (0,) * len(shape), pipeline_mode=pl.Buffered(1))


def ffn_a(info, weight, tok, tab, att, wo, ob, g2, b2, wu, ub, cot, rb=256, after=()):
    S, D = tok.shape
    FF = wu.shape[1]
    n = FF // D
    cols = lambda m: pl.BlockSpec((m, D), lambda j, *_: (0, j))
    return call(
        partial(ffn_a_body, rb=rb), "ffn_a", (n,),
        [
            single(S, D), const(2, D), single(S, D), single(D, D), const(D), const(D), const(D),
            cols(D), const(FF), single(S, D),
        ],
        [single(S, D), single(D, S), single(S, D), cols(S), cols(S), pl.BlockSpec((D, D), lambda j, *_: (j, 0)), const(1, D)],
        [sds(S, D), sds(D, S, dt=BF), sds(S, D, dt=BF), sds(S, FF, dt=BF), sds(S, FF, dt=BF), sds(FF, D), sds(1, D)],
        scratch=[pltpu.VMEM((S, D), BF), pltpu.VMEM((16, D // 16, S), BF), pltpu.VMEM((D, S), BF), pltpu.VMEM((n, 1, D), F32)],
        prefetch=2, after=after,
    )(info, weight, tok, tab, att, wo, ob, g2, b2, wu, ub, cot)


def ffn_b_body(info, w, gf, wd, gp, n2g, gu, other, own, ubs, *, rb):
    S = gf.shape[0]
    total = None
    for i in range(0, S, rb):
        r = slice(i, i + rb)
        g = (nt(gf[r, :], wd[...]) * gp[r, :].astype(F32)).astype(BF)
        gu[r, :] = g
        here = colsum(g.astype(F32))
        total = here if total is None else total + here
    ubs[0] = total
    scatter_units(info, nn(n2g[...], gu[...]) * w[0], other, own, ORDERS["up"])


def ffn_b(info, weight, gf, wd, gp, n2g, rb=256, after=()):
    S, D = gf.shape
    FF = wd.shape[0]
    n = FF // D
    R, nb = D // 16, D // 3
    units = pl.BlockSpec((16, 3, R // 2, nb), lambda j, *_: (0, j, 0, 0))
    cols = pl.BlockSpec((S, D), lambda j, *_: (0, j))
    return call(
        partial(ffn_b_body, rb=rb), "ffn_b", (n,),
        [single(S, D), pl.BlockSpec((D, D), lambda j, *_: (j, 0)), cols, single(D, S)],
        [cols, units, units, pl.BlockSpec((1, 1, D), lambda j, *_: (j, 0, 0))],
        [sds(S, FF, dt=BF), sds(16, 3 * n, R // 2, nb), sds(16, 3 * n, R // 2, nb), sds(n, 1, D)],
        prefetch=2, after=after,
    )(info, weight, gf, wd, gp, n2g)


def ffn_c_body(gu, act, wu, wd, gf, mid_i, att, g2, wo, db, ga_o, gm_o, mixed_o, gb_o, attt, gs, bs, obs, gn_s, fe_s, *, rb):
    j = pl.program_id(0)
    last = pl.num_programs(0) - 1
    S = gf.shape[0]
    blocks = [slice(i, i + rb) for i in range(0, S, rb)]

    @pl.when(j == 0)
    def _():
        for r in blocks:
            fe_s[r, :] = nn(act[r, :], wd[...])
            gn_s[r, :] = nt(gu[r, :], wu[...])
        attt[...] = att[...].T

    @pl.when((j > 0) & (j < last))
    def _():
        for r in blocks:
            fe_s[r, :] += nn(act[r, :], wd[...])
            gn_s[r, :] += nt(gu[r, :], wu[...])

    @pl.when(j == last)
    def _():
        sums = None
        for r in blocks:
            mid = mid_i[r, :]
            gn = gn_s[r, :] + nt(gu[r, :], wu[...])
            n, rs = normed(mid)
            gm = gf[r, :].astype(F32) + norm_back(gn, n, rs, vec(g2))
            gm_o[r, :] = gm
            gb = gm.astype(BF)
            gb_o[r, :] = gb
            ga_o[r, :] = nt(gb, wo[...]).astype(BF)
            mixed_o[r, :] = (mid + (fe_s[r, :] + nn(act[r, :], wd[...])) + vec(db)).astype(BF)
            here = [colsum(gn * n), colsum(gn), colsum(gb.astype(F32))]
            sums = here if sums is None else [a + b for a, b in zip(sums, here)]
        gs[...], bs[...], obs[...] = sums


def ffn_c(gu, act, wu, wd, gf, mid, att, g2, wo, db, rb=256, after=()):
    S, D = gf.shape
    FF = wd.shape[0]
    cols = lambda m: pl.BlockSpec((m, D), lambda j: (0, j))
    return call(
        partial(ffn_c_body, rb=rb), "ffn_c", (FF // D,),
        [cols(S), cols(S), cols(D), pl.BlockSpec((D, D), lambda j: (j, 0)), single(S, D), single(S, D), single(S, D), const(D), single(D, D), const(D)],
        [single(S, D), single(S, D), single(S, D), single(S, D), single(D, S), const(1, D), const(1, D), const(1, D)],
        [sds(S, D, dt=BF), sds(S, D), sds(S, D, dt=BF), sds(S, D, dt=BF), sds(D, S, dt=BF), sds(1, D), sds(1, D), sds(1, D)],
        scratch=[pltpu.VMEM((S, D), F32), pltpu.VMEM((S, D), F32)], after=after,
    )(gu, act, wu, wd, gf, mid, att, g2, wo, db)


def to_core(a):
    return lax.ppermute(a, "dp", [(i, i ^ 1) for i in range(16)])


def to_stream(a):
    return lax.ppermute(a, "species", [(0, 1), (1, 0)])


class Sum:
    def __init__(self, name, parts):
        other, own = parts
        self.orders = ORDERS[name]
        self.own, self.got = own, to_core(other)
        self.step = 0

    def start(self, *after):
        n = self.own.shape[0] // 2
        got = tie(self.got, *after)
        self.send = self.own[n:] + got[n:]
        self.keep = [self.own[:n], got[:n]]
        return self.send

    def advance(self, *after):
        bits = [STEP[order[self.step]] for order in self.orders]
        got = lax.ppermute(self.send, ("species", "dp"), [(i, i ^ bits[i & 1]) for i in range(32)])
        got = tie(got, *after)
        self.step += 1
        n = got.shape[0] // 2
        terms = self.keep + [got]
        add = lambda lo, hi: sum((t[lo:hi] for t in terms[1:]), terms[0][lo:hi])
        if n:
            self.send, self.keep = add(n, 2 * n), [add(0, n)]
        else:
            self.send = add(0, 1)
            self.keep = [self.send]
        return self.send

    def finish(self):
        while self.step < 4:
            self.advance()
        unit = self.send[0]
        return unit, to_stream(unit)


def join_body(info, *refs, n, moves):
    pairs = [(refs[2 * i], refs[2 * i + 1]) for i in range(n)]
    outs = refs[2 * n :]
    up = info[X] == 1
    for i, g, o, c in moves:
        a, b = pairs[i][0][g], pairs[i][1][g]
        U, nb = a.shape
        if c is None:
            both = [a[:, :LANES], b[:, :LANES]]
            low, high = jnp.where(up, both[1], both[0]), jnp.where(up, both[0], both[1])
            rows = jnp.concatenate([low, high], axis=0).T
            outs[o][...] = rows[:2]
            for k in range(8):
                outs[o + 1 + k][...] = rows[2 + k]
            outs[o + 9][...] = rows[10 : 10 + outs[o + 9].shape[0]]
            continue
        outs[o][:U, c : c + nb] = jnp.where(up, b, a)
        outs[o][U:, c : c + nb] = jnp.where(up, a, b)


def join(info, pairs, moves, shapes, after=()):
    arrays = [a if a.ndim == 3 else a[None] for p in pairs for a in p]
    return call(
        partial(join_body, n=len(pairs), moves=moves), "join", (1,),
        [const(*a.shape) for a in arrays], [const(*s) for s in shapes], [sds(*s) for s in shapes], prefetch=1, after=after,
    )(info, *arrays)


def stack_body(info, w, *refs):
    *parts, o = refs
    D = o.shape[1]
    sp, rest, up = parts[0], parts[1:-1], parts[-1]
    o[...] = jnp.zeros_like(o)
    for k in range(2):
        o[k : k + 1, :] = jnp.where(info[ID] == k, sp[...], 0.0) * w[0]
    for k, r in enumerate(rest):
        o[2 + k : 3 + k, :] = r[...] * w[0]
    for k in range(up.shape[1] // D):
        o[2 + len(rest) + k : 3 + len(rest) + k, :] = up[:, k * D : (k + 1) * D] * w[0]


def stack(info, weight, parts, after=()):
    D = parts[0].shape[1]
    rows = 1 + sum(p.shape[1] // D for p in parts)
    rows += -rows % 8
    return call(
        stack_body, "stack", (1,), [const(*p.shape) for p in parts], const(rows, D), sds(rows, D), prefetch=2, after=after,
    )(info, weight, *parts)


def flat(chunks):
    return jnp.concatenate(list(chunks), axis=1)


def local(
    tokens, cotangent, lengths, species_ids, species_table, ln1_gain, ln1_bias, w_qkv, q_bias, v_bias,
    w_out, out_bias, ln2_gain, ln2_bias, w_up, up_bias, w_down, down_bias, *, dp_size,
):
    D = tokens.shape[2]
    hd = D // HEADS
    scale = hd ** (-0.5)
    FF = w_up.shape[1]
    tok = tokens[0]
    cot = cotangent[0]
    paired = dp_size == 16
    dp = lax.axis_index("dp")
    x = lax.axis_index("species")
    info = jnp.stack([lengths[0], species_ids[0], dp % 2, (dp // 2) % 2, (dp // 4) % 2, dp // 8, x]).astype(jnp.int32)
    length_float = lengths[0].astype(F32)

    exchange = lambda a, bit: lax.ppermute(a, "dp", [(i, i ^ bit) for i in range(16)])
    gather = lambda a, *bits: [exchange(a, bit) for bit in bits]
    qkv, n1t = qkv_proj(info, tok, species_table, ln1_gain, ln1_bias, w_qkv, q_bias, v_bias)
    hops = []
    if paired:
        count = jnp.full((8, LANES), length_float)
        count = count + sum(tie(c, n1t) for c in gather(count, 1, 2, 3))
        hops = [count]
    att, att_f32, nl = attn_fwd(info, qkv, scale, hd, after=hops)
    if paired:
        count = count + sum(tie(c, nl) for c in gather(count, 4, 8, 12))
        hops = [count]
    back = lambda first, count, after: attn_bwd(info, qkv, att_f32, ga, nl, first, count, scale, hd, after=after)
    if paired:
        nb = D // 3
        scatter = lambda a: lax.psum_scatter(a, "dp", scatter_dimension=0, tiled=True)
        mid, n2g, gf, act, gp, part, down_part = ffn_a(
            info, length_float.reshape(1), tok, species_table, att, w_out, out_bias, ln2_gain, ln2_bias, w_up, up_bias, cot, after=hops
        )
        down = scatter(part)
        share_weight = 1.0 / (2.0 * count[0, 0])
        weight = (length_float * share_weight).reshape(1)
        gu, up_other, up_own, up_part = ffn_b(info, weight, gf, w_down, gp, n2g, after=[part])
        up = Sum("up", (up_other, up_own))
        ga, gm, mixed, gb, attt, ln2g_part, ln2b_part, ob_part = ffn_c(
            gu, act, w_up, w_down, gf, mid, att, ln2_gain, w_out, down_bias, after=[up_part]
        )
        up.start(ob_part)
        gq0 = back(0, 5, [up.send])
        first = Sum("first", wide_grad(info, weight, [n1t, n1t, attt], [[(gq0, 0)], [(gq0, 1)], [gb]], nb, ORDERS["first"], after=[gq0]))
        up.advance(first.own)
        gq1 = back(5, 1, [first.own, up.send])
        first.start(gq1)
        up.advance(first.send)
        down = tie(down, up.send) * share_weight
        down_other = to_stream(down)
        gt, ln1g_part, ln1b_part, sp_part, qb_part, vb_part = back1(
            info, [gq0, gq1], w_qkv, tok, species_table, ln1_gain, gm, after=[first.send, up.send, down]
        )
        up.advance(sp_part)
        n = D // dp_size
        last = Sum("last", last_grad(
            info, weight, n1t, [(gq0, 4), (gq1, 0)],
            [sp_part, ln1g_part, ln1b_part, qb_part, vb_part, ob_part, ln2g_part, ln2b_part, down_part, up_part],
            nb, ORDERS["last"], after=[up.send],
        ))
        first.advance(last.own)
        last.start(first.send)
        up.advance(last.send)
        first.advance(up.send)
        last.advance(first.send)
        g_down = down + tie(down_other, last.send)
        last.advance(g_down)
        first.advance(last.send)
        last.advance(first.send)
        up_pair = up.finish()
        up_pair = (up_pair[0], tie(up_pair[1], last.send))
        (g_up,) = join(info, [up_pair], [(0, g, 0, g * nb) for g in range(FF // nb)], [(n, FF)])
        first.advance(g_up)
        last.advance(first.send)
    else:
        weight = (length_float / (2.0 * lax.psum(length_float, "dp"))).reshape(1)
        mid, n2t, act, actt, gp, gf, attt, down_part = mid1(
            info, tok, species_table, att, w_out, out_bias, ln2_gain, ln2_bias, w_up, up_bias, cot
        )
        gu, up_part = mid2(gf, w_down, gp)
        gm, gb, ga, ln2g_part, ln2b_part, ob_part = back2(info, gu, w_up, mid, ln2_gain, cot, w_out)
        gqs = [back(0, D // LANES, ())]
        gt, ln1g_part, ln1b_part, sp_part, qb_part, vb_part = back1(info, gqs, w_qkv, tok, species_table, ln1_gain, gm)
        mixed = mixed_out(act, w_down, mid, down_bias)
        small = stack(info, weight, [sp_part, ln1g_part, ln1b_part, qb_part, vb_part, ob_part, ln2g_part, ln2b_part, down_part, up_part])
        small = lax.psum(lax.psum(small, "dp"), "species")
    n = D // dp_size
    if not paired:
        share = lambda r: lax.dynamic_slice_in_dim(small[r], dp * n, n)
        species = lax.dynamic_slice_in_dim(small[:2], dp * n, n, axis=1)
        up_share = lax.dynamic_slice_in_dim(small[10 : 10 + FF // D].reshape(-1), dp * (FF // dp_size), FF // dp_size)
    if paired:
        moves = [(0, 3 * h + t, 0, t * D + h * nb) for t in range(3) for h in range(2)]
        moves += [(1, t, 0, t * D + 2 * nb) for t in range(3)] + [(1, 3, 2, None)] + [(0, 6 + t, 1, t * nb) for t in range(3)]
        g_qkv, g_out, species, *vectors, up_share = join(
            info, [first.finish(), last.finish()], moves, [(n, 3 * D), (n, D), (2, n)] + [(n,)] * 8 + [(FF // D, n)]
        )
        share = lambda r: vectors[r - 2]
        up_share = up_share.reshape(-1)
    else:
        def total(part):
            return lax.psum(lax.psum_scatter(part, "dp", scatter_dimension=0, tiled=True), "species")

        g_down = total(wgrad(weight, actt, gf))
        g_up = total(wgrad(weight, n2t, gu))
        g_out = total(wgrad(weight, attt, gb))
        g_qkv = total(wgrad(weight, n1t, flat(gqs[0])))
    return (
        mixed[None], gt[None], species, share(2), share(3), g_qkv, share(4), share(5), g_out, share(6),
        share(7), share(8), g_up, up_share, g_down, share(9),
    )


def solution(mesh):
    cells = P(("species", "dp"), None, None)
    scalars = P(("species", "dp"))
    in_specs = (cells, cells, scalars, scalars) + (P(),) * 14
    v, m = P("dp"), P("dp", None)
    out_specs = (cells, cells, P(None, "dp"), v, v, m, v, v, m, v, v, v, m, v, m, v)
    return jax.shard_map(
        partial(local, dp_size=mesh.shape["dp"]), mesh=mesh, in_specs=in_specs, out_specs=out_specs, check_vma=False
    )
```

```python
from functools import partial

import jax
import jax.numpy as jnp
from jax import lax
from jax.experimental import pallas as pl
from jax.experimental.pallas import tpu as pltpu
from jax.sharding import PartitionSpec as P

HEADS = 12
F32 = jnp.float32
BF = jnp.bfloat16
LOG2E = 1.4426950408889634
MIB = 1 << 20
LANES = 128


def nt(a, b):
    return lax.dot_general(a, b, (((1,), (1,)), ((), ())), preferred_element_type=F32)


def nn(a, b):
    return lax.dot_general(a, b, (((1,), (0,)), ((), ())), preferred_element_type=F32)


def tie(a, *after):
    return lax.optimization_barrier((a, *after))[0] if after else a


def call(body, name, grid, ins, outs, shapes, scratch=(), prefetch=0, mib=56, after=(), us=0.05):
    f = pl.pallas_call(
        body,
        grid_spec=pltpu.PrefetchScalarGridSpec(
            num_scalar_prefetch=prefetch, grid=grid, in_specs=ins, out_specs=outs, scratch_shapes=list(scratch)
        ),
        out_shape=shapes,
        compiler_params=pltpu.CompilerParams(vmem_limit_bytes=mib * MIB),
        cost_estimate=pl.CostEstimate(flops=1000, bytes_accessed=int(us * 3.2e6), transcendentals=0),
        name=name,
    )
    return lambda first, *rest: f(tie(first, *after), *rest)


def const(*shape):
    return pl.BlockSpec(shape, lambda *a: (0,) * len(shape))


def sds(*shape, dt=F32):
    return jax.ShapeDtypeStruct(shape, dt)


def normed(x):
    c = x - jnp.mean(x, axis=-1, keepdims=True)
    r = lax.rsqrt(jnp.mean(c * c, axis=-1, keepdims=True) + 1e-5)
    return c * r, r


def norm_back(g, n, r, gain):
    e = g * gain
    return r * (e - jnp.mean(e, axis=-1, keepdims=True) - n * jnp.mean(e * n, axis=-1, keepdims=True))


def colsum(x):
    return jnp.sum(x, axis=0, keepdims=True)


def rows_of(rb, n):
    return pl.BlockSpec((rb, n), lambda i, *_: (i, 0))


def cols_of(n, rb):
    return pl.BlockSpec((n, rb), lambda i, *_: (0, i))


LEN, ID, CORE, Y, ZL, ZH, X = range(7)


def vec(ref):
    return ref[...].astype(F32)[None, :]


def species_row(info, table):
    rows = table[...].astype(F32)
    return jnp.where(info[ID] == 0, rows[0:1], rows[1:2])


def qkv_body(info, tok, tab, g, b, w, qb, vb, qkv, n1t):
    n, _ = normed(tok[...].astype(F32) + species_row(info, tab))
    nb = (n * vec(g) + vec(b)).astype(BF)
    n1t[...] = nb.T
    bias = jnp.concatenate([vec(qb), jnp.zeros((1, tok.shape[1]), F32), vec(vb)], axis=1)
    qkv[...] = (nn(nb, w[...]) + bias).astype(BF)


def qkv_proj(info, tok, tab, g, b, w, qb, vb, rb=256):
    S, D = tok.shape
    N = w.shape[1]
    return call(
        qkv_body, "qkv_proj", (S // rb,),
        [rows_of(rb, D), const(2, D), const(D), const(D), const(D, N), const(D), const(D)],
        [rows_of(rb, N), cols_of(D, rb)],
        [sds(S, N, dt=BF), sds(D, S, dt=BF)], prefetch=1,
    )(info, tok, tab, g, b, w, qb, vb)


def split2(x):
    hi = x.astype(BF)
    return hi, (x - hi.astype(F32)).astype(BF)


def split3(x):
    a = x.astype(BF).astype(F32)
    r = x - a
    b = r.astype(BF).astype(F32)
    return a, b, r - b


def attn_fwd_body(ln, q_ref, k_ref, v_ref, o_ref, of_ref, nl_ref, *, scale, qb, hd):
    S = q_ref.shape[0]
    lane = lax.broadcasted_iota(jnp.int32, (1, LANES), 1)
    row = lax.broadcasted_iota(jnp.int32, (S, 1), 0)
    mask = jnp.where(row < ln[0], 0.0, -1e30).astype(F32)
    kk = k_ref[...]
    kf = kk.astype(F32)
    vf = v_ref[...].astype(F32)
    hi, lo = split2(q_ref[...].astype(F32) * (scale * LOG2E))
    hi = hi.astype(F32)
    lo = lo.astype(F32)
    qa, ka, va = [], [], []
    for h in range(2):
        own = (lane // hd) == h
        aux = lane == (1 - h) * hd
        k2 = jnp.where(own, kf, jnp.where(aux, mask, 0.0)).astype(BF)
        ka.append(jnp.concatenate([kk, k2], axis=1))
        q1 = jnp.where(own, hi, 0.0).astype(BF)
        q2 = jnp.where(own, lo, jnp.where(aux, 1.0, 0.0)).astype(BF)
        qa.append(jnp.concatenate([q1, q2], axis=1))
        va.append(jnp.where(own, vf, 1.0).astype(BF))
    for b in range(S // qb):
        sl = slice(b * qb, (b + 1) * qb)
        outs, nls = [], []
        for h in range(2):
            s = nt(qa[h][sl], ka[h])
            m = jnp.max(s, axis=1, keepdims=True)
            p = jnp.exp2(s - m).astype(BF)
            o = nn(p, va[h])
            outs.append(o / pltpu.roll(o, hd, 1))
            nls.append(-(m + jnp.log2(o)))
        o = jnp.where(lane < hd, outs[0], outs[1])
        of_ref[sl, :] = o
        o_ref[sl, :] = o.astype(BF)
        nl_ref[sl, :] = jnp.where(lane < hd, nls[1], nls[0])


def attn_fwd(ln, qkv, scale, hd, qb=512, after=()):
    S, D = qkv.shape[0], qkv.shape[1] // 3
    n = D // LANES
    qb = min(qb, S)
    cb = lambda off: pl.BlockSpec((S, LANES), lambda p, l: (0, off + p))
    return call(
        partial(attn_fwd_body, scale=scale, qb=qb, hd=hd), "attn_fwd", (n,),
        [cb(0), cb(n), cb(2 * n)], [cb(0), cb(0), cb(0)],
        [sds(S, D, dt=BF), sds(S, D), sds(S, D)], prefetch=1, after=after,
    )(ln, qkv, qkv, qkv)


def attn_bwd_body(ln, q_ref, k_ref, v_ref, o_ref, do_ref, nl_ref, g_ref, dqt_ref, kt_ref, ka_ref, va_ref, *, scale, kb, hd):
    S = q_ref.shape[0]
    n = ln[0]
    lane = lax.broadcasted_iota(jnp.int32, (1, LANES), 1)
    row = lax.broadcasted_iota(jnp.int32, (S, 1), 0)
    mask = jnp.where(row < n, 0.0, -1e30).astype(F32)
    kk = k_ref[...]
    kf = kk.astype(F32)
    vf = v_ref[...].astype(F32)
    dof = do_ref[...].astype(F32)
    qf = q_ref[...].astype(F32)
    hi, lo = split2(qf * (scale * LOG2E))
    hi = hi.astype(F32)
    lo = lo.astype(F32)
    n0, n1, n2 = split3(nl_ref[...])
    do_o = dof * o_ref[...]
    kt_ref[...] = kf.T.astype(BF)
    qa, qo, da, do_own = [], [], [], []
    for h in range(2):
        own = (lane // hd) == h
        base = (1 - h) * hd
        three = (lane > base) & (lane < base + 4)
        pick = lambda a, b, c: jnp.where(lane == base + 1, a, jnp.where(lane == base + 2, b, jnp.where(lane == base + 3, c, 0.0)))
        ka_ref[h, :, 0:LANES] = kk
        ka_ref[h, :, LANES:] = jnp.where(own, kf, jnp.where(lane == base, mask, jnp.where(three, 1.0, 0.0))).astype(BF)
        va_ref[h] = jnp.where(own, vf, jnp.where(three, 1.0, 0.0)).astype(BF)
        q1 = jnp.where(own, hi, 0.0).astype(BF)
        q2 = jnp.where(own, lo, jnp.where(lane == base, 1.0, pick(n0, n1, n2))).astype(BF)
        qa.append(jnp.concatenate([q1, q2], axis=1))
        qo.append(jnp.where(own, qf, 0.0).astype(BF))
        delta = -jnp.sum(jnp.where(own, do_o, 0.0), axis=1, keepdims=True)
        do_own.append(jnp.where(own, dof, 0.0).astype(BF))
        da.append(jnp.where(own, dof, pick(*split3(delta))).astype(BF))
    for b in range(S // kb):
        sl = slice(b * kb, (b + 1) * kb)

        @pl.when(b * kb < n)
        def _():
            dv = dk = None
            for h in range(2):
                p = jnp.exp2(nt(ka_ref[h, sl, :], qa[h]))
                ds = (p * nt(va_ref[h, sl, :], da[h])).astype(BF)
                dvh = nn(p.astype(BF), do_own[h])
                dkh = nn(ds, qo[h])
                dv = dvh if h == 0 else dv + dvh
                dk = dkh if h == 0 else dk + dkh
                dqt = nn(kt_ref[h * hd : (h + 1) * hd, sl], ds)
                if b == 0:
                    dqt_ref[h * hd : (h + 1) * hd, :] = dqt
                else:
                    dqt_ref[h * hd : (h + 1) * hd, :] += dqt
            g_ref[1, sl, :] = (dk * scale).astype(BF)
            g_ref[2, sl, :] = dv.astype(BF)

        @pl.when(b * kb >= n)
        def _():
            g_ref[1, sl, :] = jnp.zeros((kb, LANES), BF)
            g_ref[2, sl, :] = jnp.zeros((kb, LANES), BF)

    g_ref[0] = (dqt_ref[...].T * scale).astype(BF)


def attn_bwd(ln, qkv, o, do, nl, first, count, scale, hd, kb=1024, after=()):
    S, D = qkv.shape[0], qkv.shape[1] // 3
    n = D // LANES
    kb = min(kb, S)
    cb = lambda off: pl.BlockSpec((S, LANES), lambda p, l: (0, off + first + p))
    return call(
        partial(attn_bwd_body, scale=scale, kb=kb, hd=hd), "attn_bwd", (count,),
        [cb(0), cb(n), cb(2 * n), cb(0), cb(0), cb(0)],
        pl.BlockSpec((3, S, LANES), lambda p, l: (0, 0, p)),
        sds(3, S, count * LANES, dt=BF),
        scratch=[pltpu.VMEM((LANES, S), F32), pltpu.VMEM((LANES, S), BF), pltpu.VMEM((2, S, 2 * LANES), BF), pltpu.VMEM((2, S, LANES), BF)],
        prefetch=1, after=after, us=9 if count == 1 else 0.05,
    )(ln, qkv, qkv, qkv, o, do, nl)


def mid1_body(info, tok, tab, att, wo, ob, g2, b2, wu, ub, cot, mid_o, n2t, act_o, actt, gp_o, gf_o, attt, dbs, *, fb):
    i = pl.program_id(0)
    rb = tok.shape[0]
    FF = wu.shape[1]
    a = att[...]
    attt[...] = a.T
    mid = tok[...].astype(F32) + species_row(info, tab) + nn(a, wo[...]) + vec(ob)
    mid_o[...] = mid
    n, _ = normed(mid)
    n2 = (n * vec(g2) + vec(b2)).astype(BF)
    n2t[...] = n2.T
    row = i * rb + lax.broadcasted_iota(jnp.int32, (rb, 1), 0)
    gf = jnp.where(row < info[LEN], cot[...].astype(F32), 0.0)
    gf_o[...] = gf.astype(BF)

    @pl.when(i == 0)
    def _():
        dbs[...] = jnp.zeros_like(dbs)

    dbs[...] += colsum(gf)
    C = 0.7978845608
    C2 = C * 0.044715
    bias = vec(ub)
    for j in range(FF // fb):
        sl = slice(j * fb, (j + 1) * fb)
        u = nn(n2, wu[:, sl]) + bias[:, sl]
        cu = C2 * (u * u)
        h = 0.5 * jnp.tanh(u * (cu + C)) + 0.5
        act = u * h
        ab = act.astype(BF)
        act_o[:, sl] = ab
        actt[sl, :] = ab.T
        gp_o[:, sl] = (h + act * (1.0 - h) * (6.0 * cu + 2.0 * C)).astype(BF)


def mid1(info, tok, tab, att, wo, ob, g2, b2, wu, ub, cot, rb=256, fb=768):
    S, D = tok.shape
    FF = wu.shape[1]
    r = partial(rows_of, rb)
    t = lambda n: cols_of(n, rb)
    return call(
        partial(mid1_body, fb=fb), "mid1", (S // rb,),
        [r(D), const(2, D), r(D), const(D, D), const(D), const(D), const(D), const(D, FF), const(FF), r(D)],
        [r(D), t(D), r(FF), t(FF), r(FF), r(D), t(D), const(1, D)],
        [sds(S, D), sds(D, S, dt=BF), sds(S, FF, dt=BF), sds(FF, S, dt=BF), sds(S, FF, dt=BF), sds(S, D, dt=BF), sds(D, S, dt=BF), sds(1, D)],
        prefetch=1,
    )(info, tok, tab, att, wo, ob, g2, b2, wu, ub, cot)


def mid2_body(gf, wd, gp, gu_o, ubs):
    gu = (nt(gf[...], wd[...]) * gp[...].astype(F32)).astype(BF)
    gu_o[...] = gu
    ubs[...] = colsum(gu.astype(F32))


def mid2(gf, wd, gp, nb=512, after=()):
    S, D = gf.shape
    FF = wd.shape[0]
    t = lambda n: pl.BlockSpec((n, nb), lambda j: (0, j))
    return call(
        mid2_body, "mid2", (FF // nb,),
        [const(S, D), pl.BlockSpec((nb, D), lambda j: (j, 0)), t(S)],
        [t(S), t(1)], [sds(S, FF, dt=BF), sds(1, FF)], after=after,
    )(gf, wd, gp)


def back2_body(ln, gu, wu, mid, g2, cot, wo, gm_o, gb_o, ga_o, gs, bs, obs):
    i = pl.program_id(0)
    rb = mid.shape[0]
    gn = nt(gu[...], wu[...])
    n, r = normed(mid[...])
    row = i * rb + lax.broadcasted_iota(jnp.int32, (rb, 1), 0)
    gf = jnp.where(row < ln[0], cot[...].astype(F32), 0.0)
    gm = gf + norm_back(gn, n, r, vec(g2))
    gm_o[...] = gm
    gb = gm.astype(BF)
    gb_o[...] = gb
    ga_o[...] = nt(gb, wo[...]).astype(BF)

    @pl.when(i == 0)
    def _():
        for s in (gs, bs, obs):
            s[...] = jnp.zeros_like(s)

    gs[...] += colsum(gn * n)
    bs[...] += colsum(gn)
    obs[...] += colsum(gb.astype(F32))


def back2(ln, gu, wu, mid, g2, cot, wo, rb=256, after=()):
    S, D = mid.shape
    FF = wu.shape[1]
    r = partial(rows_of, rb)
    return call(
        back2_body, "back2", (S // rb,),
        [r(FF), const(D, FF), r(D), const(D), r(D), const(D, D)],
        [r(D), r(D), r(D), const(1, D), const(1, D), const(1, D)],
        [sds(S, D), sds(S, D, dt=BF), sds(S, D, dt=BF), sds(1, D), sds(1, D), sds(1, D)],
        prefetch=1, after=after,
    )(ln, gu, wu, mid, g2, cot, wo)


def back1_body(info, *refs):
    *gq, w, tok, tab, g1, gm, gt_o, gs, bs, ss, qs, vs = refs
    i = pl.program_id(0)
    D = tok.shape[1]
    gn = None
    for t in range(3):
        whole = jnp.concatenate([g[t] for g in gq], axis=1)
        part = nt(whole, w[:, t * D : (t + 1) * D])
        gn = part if gn is None else gn + part
    n, r = normed(tok[...].astype(F32) + species_row(info, tab))
    g = gm[...] + norm_back(gn, n, r, vec(g1))
    gt_o[...] = g.astype(BF)

    @pl.when(i == 0)
    def _():
        for s in (gs, bs, ss, qs, vs):
            s[...] = jnp.zeros_like(s)

    gs[...] += colsum(gn * n)
    bs[...] += colsum(gn)
    ss[...] += colsum(g)
    qs[...] += colsum(jnp.concatenate([g[0] for g in gq], axis=1).astype(F32))
    vs[...] += colsum(jnp.concatenate([g[2] for g in gq], axis=1).astype(F32))


def back1(info, gq, w, tok, tab, g1, gm, rb=256, after=()):
    S, D = tok.shape
    r = partial(rows_of, rb)
    return call(
        back1_body, "back1", (S // rb,),
        [pl.BlockSpec((3, rb, g.shape[2]), lambda i, n: (0, i, 0)) for g in gq] + [const(D, 3 * D), r(D), const(2, D), const(D), r(D)],
        [r(D)] + [const(1, D)] * 5,
        [sds(S, D, dt=BF)] + [sds(1, D)] * 5, prefetch=1, after=after, us=11,
    )(info, *gq, w, tok, tab, g1, gm)


def mixed_body(act, wd, mid, db, o):
    o[...] = (mid[...] + nn(act[...], wd[...]) + vec(db)).astype(BF)


def mixed_out(act, wd, mid, db, first=0, count=4, rb=256, after=()):
    D = mid.shape[1]
    FF = wd.shape[0]
    r = lambda n: pl.BlockSpec((rb, n), lambda i: (first + i, 0))
    return call(
        mixed_body, "mixed_out", (count,),
        [r(FF), const(FF, D), r(D), const(D)], rows_of(rb, D), sds(count * rb, D, dt=BF), after=after,
    )(act, wd, mid, db)


def wgrad_body(w, a, b, o):
    o[...] = nn(a[...], b[...]) * w[0]


def wgrad(weight, at, b, nb=768, after=()):
    M, S = at.shape
    N = b.shape[1]
    mb = min(M, 768)
    return call(
        wgrad_body, "wgrad", (M // mb, N // nb),
        [pl.BlockSpec((mb, S), lambda i, j, w: (i, 0)), pl.BlockSpec((S, nb), lambda i, j, w: (0, j))],
        pl.BlockSpec((mb, nb), lambda i, j, w: (i, j)), sds(M, N),
        prefetch=1, after=after,
    )(weight, at, b)


NUMBER = {"y": Y, "zl": ZL, "zh": ZH, "x": X}
STEP = {"y": 2, "zl": 4, "zh": 8, "x": 16}
YX = (("y", "zl", "zh", "x"), ("x", "y", "zl", "zh"))
ZX = (("zl", "x", "y", "zh"), ("x", "zl", "y", "zh"))
YXZ = (("y", "x", "zl", "zh"), ("x", "y", "zh", "zl"))
XYZ = (("y", "x", "zl", "zh"), ("x", "y", "zl", "zh"))
ORDERS = {"up": YXZ, "first": YX, "last": XYZ}


def places(info, core, p, half, orders):
    far = 1 - info[X] if half else info[X]
    bit = {"y": (p >> 2) & 1, "zl": (p >> 1) & 1, "zh": p & 1, "x": far}
    at = [sum(bit[a] * (8 >> k) for k, a in enumerate(order)) for order in orders]
    return jnp.where(core == 0, at[0], at[1])


def wide_body(info, w, *refs, counts, steps, orders):
    n = sum(counts)
    many_lhs = len(counts)
    lefts, rhs, (other, own, held) = refs[:many_lhs], refs[many_lhs : many_lhs + n], refs[many_lhs + n :]
    j = pl.program_id(0)
    R = lefts[0].shape[2]
    nb = other.shape[-1]
    cores = (1 - info[CORE], info[CORE])

    def bring(lhs):
        rel = lambda a, k: 1 - info[a] if k else info[a]
        for i, core in enumerate(cores):
            for p in range(8):
                block = rel(ZH, p & 1) * 4 + rel(ZL, (p >> 1) & 1) * 2 + rel(Y, (p >> 2) & 1)
                held[(i * 8 + p) * R : (i * 8 + p + 1) * R, :] = lhs[block, core]

    at, lo = 0, 0
    for left, many, count in zip(lefts, counts, steps):
        parts = rhs[at : at + many]

        def run(parts=parts, left=left, many=many):
            bring(left)
            for t in range(3):
                if len(parts[0].shape) == 3:
                    b = [r[t] for r in parts]
                    b = b[0] if many == 1 else jnp.concatenate(b, axis=1)
                else:
                    b = parts[0][:, t * (parts[0].shape[1] // 3) : (t + 1) * (parts[0].shape[1] // 3)]
                G = b.shape[1] // nb
                res = nn(held[...], b) * w[0]
                for h in range(G):
                    part = res[:, h * nb : (h + 1) * nb].reshape(2, 8, 2, R // 2, nb)
                    for i, (core, out) in enumerate(zip(cores, (other, own))):
                        for p in range(8):
                            for half in range(2):
                                out[places(info, core, p, half, orders), t * G + h] = part[i, p, half]

        pl.when((j >= lo) & (j < lo + count))(run)
        at, lo = at + many, lo + count


def wide_grad(info, weight, lhs, rhs, nb, orders, after=()):
    S = lhs[0].shape[1]
    R = lhs[0].shape[0] // 16
    specs, arrays = [], []
    for b in (b for group in rhs for b in group):
        b, k = b if isinstance(b, tuple) else (b, None)
        arrays.append(b)
        specs.append(const(*b.shape) if k is None else pl.BlockSpec((3, S, nb), lambda *_, k=k: (0, 0, k)))
    return call(
        partial(wide_body, counts=[len(g) for g in rhs], steps=[1] * len(rhs), orders=orders), "wide_grad", (len(rhs),),
        [const(8, 2, R, S) for _ in lhs] + specs,
        [pl.BlockSpec((16, 3, R // 2, nb), lambda j, *_: (0, j, 0, 0))] * 2,
        [sds(16, 3 * len(rhs), R // 2, nb)] * 2,
        scratch=[pltpu.VMEM((16 * R, S), BF)], prefetch=2, after=after, us=10,
    )(info, weight, *[a.reshape(8, 2, R, S) for a in lhs], *arrays)


def last_body(info, w, lhs, *refs, n, orders):
    rhs, parts = refs[:n], refs[n:-5]
    other, own, held, rows, turned = refs[-5:]
    R = lhs.shape[2]
    nb = other.shape[-1]
    cores = (1 - info[CORE], info[CORE])
    rel = lambda a, k: 1 - info[a] if k else info[a]
    for i, core in enumerate(cores):
        for p in range(8):
            block = rel(ZH, p & 1) * 4 + rel(ZL, (p >> 1) & 1) * 2 + rel(Y, (p >> 2) & 1)
            held[(i * 8 + p) * R : (i * 8 + p + 1) * R, :] = lhs[block, core]
    for t in range(3):
        res = nn(held[...], jnp.concatenate([r[t] for r in rhs], axis=1)) * w[0]
        part = res.reshape(2, 8, 2, R // 2, nb)
        for i, (core, out) in enumerate(zip(cores, (other, own))):
            for p in range(8):
                for half in range(2):
                    out[places(info, core, p, half, orders), t] = part[i, p, half]
    sp, *rest, up = parts
    rows[...] = jnp.zeros_like(rows)
    for k in range(2):
        rows[k : k + 1, :] = jnp.where(info[ID] == k, sp[...], 0.0) * w[0]
    at = 2
    for r in rest:
        rows[at : at + 1, :] = r[...] * w[0]
        at += 1
    D = rows.shape[1]
    many = up.shape[0]
    for k in range(many):
        rows[at + k : at + k + 1, :] = up[k] * w[0]
    turned[...] = rows[...].T
    blank = jnp.zeros((R // 2, nb - LANES), F32)
    lane = lax.broadcasted_iota(jnp.int32, (1, LANES), 1)
    span = many * R
    for core, out in zip(cores, (other, own)):
        for p in range(8):
            block = rel(ZH, p & 1) * 8 + rel(ZL, (p >> 1) & 1) * 4 + rel(Y, (p >> 2) & 1) * 2 + core
            row, start = block * span // D, block * span % D
            for half in range(2):
                place = places(info, core, p, half, orders)
                here = pl.ds(pl.multiple_of(block * R + half * (R // 2), 8), R // 2)
                value = jnp.where(lane < at, turned[here, :], 0.0)
                for k in range(many):
                    there = pl.ds(pl.multiple_of(start + k * R + half * (R // 2), 8), R // 2)
                    column = jnp.sum(jnp.where(lane == at + row, turned[there, :], 0.0), axis=1, keepdims=True)
                    value = jnp.where(lane == at + k, column, value)
                out[place, 3, :, :LANES] = value
                out[place, 3, :, LANES:] = blank


def last_grad(info, weight, lhs, rhs, parts, nb, orders, after=()):
    D, S = lhs.shape
    R = D // 16
    units = const(16, 4, R // 2, nb)
    lanes = [pl.BlockSpec((3, S, LANES), lambda *_, k=k: (0, 0, k)) for _, k in rhs]
    return call(
        partial(last_body, n=len(rhs), orders=orders), "last_grad", (1,),
        [const(8, 2, R, S)] + lanes + [const(*b.shape) for b in parts], [units, units], [sds(16, 4, R // 2, nb)] * 2,
        scratch=[pltpu.VMEM((D, S), BF), pltpu.VMEM((LANES, D), F32), pltpu.VMEM((D, LANES), F32)],
        prefetch=2, after=after,
    )(info, weight, lhs.reshape(8, 2, R, S), *[b for b, _ in rhs], *parts)


def scatter_units(info, res, other, own, orders):
    nb = other.shape[-1]
    R = res.shape[0] // 16
    cores = (1 - info[CORE], info[CORE])
    for g in range(res.shape[1] // nb):
        part = res[:, g * nb : (g + 1) * nb].reshape(2, 8, 2, R // 2, nb)
        for i, (core, out) in enumerate(zip(cores, (other, own))):
            for p in range(8):
                for half in range(2):
                    out[places(info, core, p, half, orders), g] = part[i, p, half]


def gather_blocks(info, natural, held):
    R = natural.shape[1]
    rel = lambda a, k: 1 - info[a] if k else info[a]
    for i, core in enumerate((1 - info[CORE], info[CORE])):
        for p in range(8):
            block = rel(ZH, p & 1) * 8 + rel(ZL, (p >> 1) & 1) * 4 + rel(Y, (p >> 2) & 1) * 2 + core
            held[(i * 8 + p) * R : (i * 8 + p + 1) * R, :] = natural[block]


def ffn_a_body(
    info, w, tok, tab, att, wo, ob, g2, b2, wu, ub, cot,
    mid_o, n2g, gf_o, act_o, gp_o, wd_o, dbs,
    n2_s, nat_s, actt_s, ub_s, *, rb,
):
    j = pl.program_id(0)
    S, D = tok.shape
    fb = wu.shape[1]
    R = nat_s.shape[1]
    blocks = [slice(i, i + rb) for i in range(0, S, rb)]

    @pl.when(j == 0)
    def _():
        sp = species_row(info, tab)
        total = None
        for r in blocks:
            mid = tok[r, :].astype(F32) + sp + nn(att[r, :], wo[...]) + vec(ob)
            mid_o[r, :] = mid
            n, _ = normed(mid)
            n2 = (n * vec(g2) + vec(b2)).astype(BF)
            n2_s[r, :] = n2
            nat_s[:, :, r] = n2.T.reshape(16, R, rb)
            row = r.start + lax.broadcasted_iota(jnp.int32, (rb, 1), 0)
            gf = jnp.where(row < info[LEN], cot[r, :].astype(F32), 0.0)
            gf_o[r, :] = gf.astype(BF)
            total = colsum(gf) if total is None else total + colsum(gf)
        dbs[...] = total
        gather_blocks(info, nat_s, n2g)
        bias = vec(ub)
        for c in range(ub_s.shape[0]):
            ub_s[c] = bias[:, c * fb : (c + 1) * fb]

    C = 0.7978845608
    C2 = C * 0.044715
    bias = ub_s[j]
    for r in blocks:
        u = nn(n2_s[r, :], wu[...]) + bias
        cu = C2 * (u * u)
        h = 0.5 * jnp.tanh(u * (cu + C)) + 0.5
        act = u * h
        ab = act.astype(BF)
        act_o[r, :] = ab
        actt_s[:, r] = ab.T
        gp_o[r, :] = (h + act * (1.0 - h) * (6.0 * cu + 2.0 * C)).astype(BF)
    wd_o[...] = nn(actt_s[...], gf_o[...]) * w[0]


def single(*shape):
    return pl.BlockSpec(shape, lambda *a: (0,) * len(shape), pipeline_mode=pl.Buffered(1))


def ffn_a(info, weight, tok, tab, att, wo, ob, g2, b2, wu, ub, cot, rb=256, after=()):
    S, D = tok.shape
    FF = wu.shape[1]
    n = FF // D
    cols = lambda m: pl.BlockSpec((m, D), lambda j, *_: (0, j))
    return call(
        partial(ffn_a_body, rb=rb), "ffn_a", (n,),
        [
            single(S, D), const(2, D), single(S, D), single(D, D), const(D), const(D), const(D),
            cols(D), const(FF), single(S, D),
        ],
        [single(S, D), single(D, S), single(S, D), cols(S), cols(S), pl.BlockSpec((D, D), lambda j, *_: (j, 0)), const(1, D)],
        [sds(S, D), sds(D, S, dt=BF), sds(S, D, dt=BF), sds(S, FF, dt=BF), sds(S, FF, dt=BF), sds(FF, D), sds(1, D)],
        scratch=[pltpu.VMEM((S, D), BF), pltpu.VMEM((16, D // 16, S), BF), pltpu.VMEM((D, S), BF), pltpu.VMEM((n, 1, D), F32)],
        prefetch=2, after=after,
    )(info, weight, tok, tab, att, wo, ob, g2, b2, wu, ub, cot)


def ffn_b_body(info, w, gf, wd, gp, n2g, gu, other, own, ubs, *, rb):
    S = gf.shape[0]
    total = None
    for i in range(0, S, rb):
        r = slice(i, i + rb)
        g = (nt(gf[r, :], wd[...]) * gp[r, :].astype(F32)).astype(BF)
        gu[r, :] = g
        here = colsum(g.astype(F32))
        total = here if total is None else total + here
    ubs[0] = total
    scatter_units(info, nn(n2g[...], gu[...]) * w[0], other, own, ORDERS["up"])


def ffn_b(info, weight, gf, wd, gp, n2g, rb=256, after=()):
    S, D = gf.shape
    FF = wd.shape[0]
    n = FF // D
    R, nb = D // 16, D // 3
    units = pl.BlockSpec((16, 3, R // 2, nb), lambda j, *_: (0, j, 0, 0))
    cols = pl.BlockSpec((S, D), lambda j, *_: (0, j))
    return call(
        partial(ffn_b_body, rb=rb), "ffn_b", (n,),
        [single(S, D), pl.BlockSpec((D, D), lambda j, *_: (j, 0)), cols, single(D, S)],
        [cols, units, units, pl.BlockSpec((1, 1, D), lambda j, *_: (j, 0, 0))],
        [sds(S, FF, dt=BF), sds(16, 3 * n, R // 2, nb), sds(16, 3 * n, R // 2, nb), sds(n, 1, D)],
        prefetch=2, after=after,
    )(info, weight, gf, wd, gp, n2g)


def ffn_c_body(gu, wu, gf, mid_i, att, g2, wo, ga_o, gm_o, gb_o, attt, gs, bs, obs, gn_s, *, rb):
    j = pl.program_id(0)
    last = pl.num_programs(0) - 1
    S = gf.shape[0]
    blocks = [slice(i, i + rb) for i in range(0, S, rb)]

    @pl.when(j == 0)
    def _():
        for r in blocks:
            gn_s[r, :] = nt(gu[r, :], wu[...])
        attt[...] = att[...].T

    @pl.when((j > 0) & (j < last))
    def _():
        for r in blocks:
            gn_s[r, :] += nt(gu[r, :], wu[...])

    @pl.when(j == last)
    def _():
        sums = None
        for r in blocks:
            gn = gn_s[r, :] + nt(gu[r, :], wu[...])
            n, rs = normed(mid_i[r, :])
            gm = gf[r, :].astype(F32) + norm_back(gn, n, rs, vec(g2))
            gm_o[r, :] = gm
            gb = gm.astype(BF)
            gb_o[r, :] = gb
            ga_o[r, :] = nt(gb, wo[...]).astype(BF)
            here = [colsum(gn * n), colsum(gn), colsum(gb.astype(F32))]
            sums = here if sums is None else [a + b for a, b in zip(sums, here)]
        gs[...], bs[...], obs[...] = sums


def ffn_c(gu, wu, gf, mid, att, g2, wo, rb=256, after=()):
    S, D = gf.shape
    FF = wu.shape[1]
    cols = lambda m: pl.BlockSpec((m, D), lambda j: (0, j))
    return call(
        partial(ffn_c_body, rb=rb), "ffn_c", (FF // D,),
        [cols(S), cols(D), single(S, D), single(S, D), single(S, D), const(D), single(D, D)],
        [single(S, D), single(S, D), single(S, D), single(D, S), const(1, D), const(1, D), const(1, D)],
        [sds(S, D, dt=BF), sds(S, D), sds(S, D, dt=BF), sds(D, S, dt=BF), sds(1, D), sds(1, D), sds(1, D)],
        scratch=[pltpu.VMEM((S, D), F32)], after=after,
    )(gu, wu, gf, mid, att, g2, wo)


def to_core(a):
    return lax.ppermute(a, "dp", [(i, i ^ 1) for i in range(16)])


def to_stream(a):
    return lax.ppermute(a, "species", [(0, 1), (1, 0)])


class Sum:
    def __init__(self, name, parts):
        other, own = parts
        self.orders = ORDERS[name]
        self.own, self.got = own, to_core(other)
        self.step = 0

    def start(self, *after):
        n = self.own.shape[0] // 2
        got = tie(self.got, *after)
        self.send = self.own[n:] + got[n:]
        self.keep = [self.own[:n], got[:n]]
        return self.send

    def advance(self, *after):
        bits = [STEP[order[self.step]] for order in self.orders]
        got = lax.ppermute(self.send, ("species", "dp"), [(i, i ^ bits[i & 1]) for i in range(32)])
        got = tie(got, *after)
        self.step += 1
        n = got.shape[0] // 2
        terms = self.keep + [got]
        add = lambda lo, hi: sum((t[lo:hi] for t in terms[1:]), terms[0][lo:hi])
        if n:
            self.send, self.keep = add(n, 2 * n), [add(0, n)]
        else:
            self.send = add(0, 1)
            self.keep = [self.send]
        return self.send

    def finish(self):
        while self.step < 4:
            self.advance()
        unit = self.send[0]
        return unit, to_stream(unit)


def join_body(info, *refs, n, moves):
    pairs = [(refs[2 * i], refs[2 * i + 1]) for i in range(n)]
    outs = refs[2 * n :]
    up = info[X] == 1
    for i, g, o, c in moves:
        a, b = pairs[i][0][g], pairs[i][1][g]
        U, nb = a.shape
        if c is None:
            both = [a[:, :LANES], b[:, :LANES]]
            low, high = jnp.where(up, both[1], both[0]), jnp.where(up, both[0], both[1])
            rows = jnp.concatenate([low, high], axis=0).T
            outs[o][...] = rows[:2]
            for k in range(8):
                outs[o + 1 + k][...] = rows[2 + k]
            outs[o + 9][...] = rows[10 : 10 + outs[o + 9].shape[0]]
            continue
        outs[o][:U, c : c + nb] = jnp.where(up, b, a)
        outs[o][U:, c : c + nb] = jnp.where(up, a, b)


def join(info, pairs, moves, shapes, after=()):
    arrays = [a if a.ndim == 3 else a[None] for p in pairs for a in p]
    return call(
        partial(join_body, n=len(pairs), moves=moves), "join", (1,),
        [const(*a.shape) for a in arrays], [const(*s) for s in shapes], [sds(*s) for s in shapes], prefetch=1, after=after,
    )(info, *arrays)


def stack_body(info, w, *refs):
    *parts, o = refs
    D = o.shape[1]
    sp, rest, up = parts[0], parts[1:-1], parts[-1]
    o[...] = jnp.zeros_like(o)
    for k in range(2):
        o[k : k + 1, :] = jnp.where(info[ID] == k, sp[...], 0.0) * w[0]
    for k, r in enumerate(rest):
        o[2 + k : 3 + k, :] = r[...] * w[0]
    for k in range(up.shape[1] // D):
        o[2 + len(rest) + k : 3 + len(rest) + k, :] = up[:, k * D : (k + 1) * D] * w[0]


def stack(info, weight, parts, after=()):
    D = parts[0].shape[1]
    rows = 1 + sum(p.shape[1] // D for p in parts)
    rows += -rows % 8
    return call(
        stack_body, "stack", (1,), [const(*p.shape) for p in parts], const(rows, D), sds(rows, D), prefetch=2, after=after,
    )(info, weight, *parts)


def flat(chunks):
    return jnp.concatenate(list(chunks), axis=1)


def local(
    tokens, cotangent, lengths, species_ids, species_table, ln1_gain, ln1_bias, w_qkv, q_bias, v_bias,
    w_out, out_bias, ln2_gain, ln2_bias, w_up, up_bias, w_down, down_bias, *, dp_size,
):
    D = tokens.shape[2]
    hd = D // HEADS
    scale = hd ** (-0.5)
    FF = w_up.shape[1]
    tok = tokens[0]
    cot = cotangent[0]
    paired = dp_size == 16
    dp = lax.axis_index("dp")
    x = lax.axis_index("species")
    info = jnp.stack([lengths[0], species_ids[0], dp % 2, (dp // 2) % 2, (dp // 4) % 2, dp // 8, x]).astype(jnp.int32)
    length_float = lengths[0].astype(F32)

    exchange = lambda a, bit: lax.ppermute(a, "dp", [(i, i ^ bit) for i in range(16)])
    gather = lambda a, *bits: [exchange(a, bit) for bit in bits]
    qkv, n1t = qkv_proj(info, tok, species_table, ln1_gain, ln1_bias, w_qkv, q_bias, v_bias)
    hops = []
    if paired:
        count = jnp.full((8, LANES), length_float)
        count = count + sum(tie(c, n1t) for c in gather(count, 1, 2, 3))
        hops = [count]
    att, att_f32, nl = attn_fwd(info, qkv, scale, hd, after=hops)
    if paired:
        count = count + sum(tie(c, nl) for c in gather(count, 4, 8, 12))
        hops = [count]
    back = lambda first, count, after: attn_bwd(info, qkv, att_f32, ga, nl, first, count, scale, hd, after=after)
    if paired:
        nb = D // 3
        scatter = lambda a: lax.psum_scatter(a, "dp", scatter_dimension=0, tiled=True)
        mid, n2g, gf, act, gp, part, down_part = ffn_a(
            info, length_float.reshape(1), tok, species_table, att, w_out, out_bias, ln2_gain, ln2_bias, w_up, up_bias, cot, after=hops
        )
        down = scatter(part)
        share_weight = 1.0 / (2.0 * count[0, 0])
        weight = (length_float * share_weight).reshape(1)
        gu, up_other, up_own, up_part = ffn_b(info, weight, gf, w_down, gp, n2g, after=[part])
        up = Sum("up", (up_other, up_own))
        ga, gm, gb, attt, ln2g_part, ln2b_part, ob_part = ffn_c(gu, w_up, gf, mid, att, ln2_gain, w_out, after=[up_part])
        up.start(ob_part)
        gq0 = back(0, 5, [up.send])
        first = Sum("first", wide_grad(info, weight, [n1t, n1t, attt], [[(gq0, 0)], [(gq0, 1)], [gb]], nb, ORDERS["first"], after=[gq0]))
        up.advance(first.own)
        gq1 = back(5, 1, [first.own, up.send])
        first.start(gq1)
        up.advance(first.send)
        gt, ln1g_part, ln1b_part, sp_part, qb_part, vb_part = back1(
            info, [gq0, gq1], w_qkv, tok, species_table, ln1_gain, gm, after=[first.send, up.send]
        )
        up.advance(sp_part)
        down = tie(down, up.send) * share_weight
        down_other = to_stream(down)
        n = D // dp_size
        last = Sum("last", last_grad(
            info, weight, n1t, [(gq0, 4), (gq1, 0)],
            [sp_part, ln1g_part, ln1b_part, qb_part, vb_part, ob_part, ln2g_part, ln2b_part, down_part, up_part],
            nb, ORDERS["last"], after=[up.send, down],
        ))
        first.advance(last.own)
        last.start(first.send)
        mixed = mixed_out(act, w_down, mid, down_bias, after=[last.send])
        up.advance(mixed)
        first.advance(up.send)
        last.advance(first.send)
        g_down = down + tie(down_other, last.send)
        last.advance(g_down)
        first.advance(last.send)
        last.advance(first.send)
        up_pair = up.finish()
        up_pair = (up_pair[0], tie(up_pair[1], last.send))
        (g_up,) = join(info, [up_pair], [(0, g, 0, g * nb) for g in range(FF // nb)], [(n, FF)])
        first.advance(g_up)
        last.advance(first.send)
    else:
        weight = (length_float / (2.0 * lax.psum(length_float, "dp"))).reshape(1)
        mid, n2t, act, actt, gp, gf, attt, down_part = mid1(
            info, tok, species_table, att, w_out, out_bias, ln2_gain, ln2_bias, w_up, up_bias, cot
        )
        gu, up_part = mid2(gf, w_down, gp)
        gm, gb, ga, ln2g_part, ln2b_part, ob_part = back2(info, gu, w_up, mid, ln2_gain, cot, w_out)
        gqs = [back(0, D // LANES, ())]
        gt, ln1g_part, ln1b_part, sp_part, qb_part, vb_part = back1(info, gqs, w_qkv, tok, species_table, ln1_gain, gm)
        mixed = mixed_out(act, w_down, mid, down_bias)
        small = stack(info, weight, [sp_part, ln1g_part, ln1b_part, qb_part, vb_part, ob_part, ln2g_part, ln2b_part, down_part, up_part])
        small = lax.psum(lax.psum(small, "dp"), "species")
    n = D // dp_size
    if not paired:
        share = lambda r: lax.dynamic_slice_in_dim(small[r], dp * n, n)
        species = lax.dynamic_slice_in_dim(small[:2], dp * n, n, axis=1)
        up_share = lax.dynamic_slice_in_dim(small[10 : 10 + FF // D].reshape(-1), dp * (FF // dp_size), FF // dp_size)
    if paired:
        moves = [(0, 3 * h + t, 0, t * D + h * nb) for t in range(3) for h in range(2)]
        moves += [(1, t, 0, t * D + 2 * nb) for t in range(3)] + [(1, 3, 2, None)] + [(0, 6 + t, 1, t * nb) for t in range(3)]
        g_qkv, g_out, species, *vectors, up_share = join(
            info, [first.finish(), last.finish()], moves, [(n, 3 * D), (n, D), (2, n)] + [(n,)] * 8 + [(FF // D, n)]
        )
        share = lambda r: vectors[r - 2]
        up_share = up_share.reshape(-1)
    else:
        def total(part):
            return lax.psum(lax.psum_scatter(part, "dp", scatter_dimension=0, tiled=True), "species")

        g_down = total(wgrad(weight, actt, gf))
        g_up = total(wgrad(weight, n2t, gu))
        g_out = total(wgrad(weight, attt, gb))
        g_qkv = total(wgrad(weight, n1t, flat(gqs[0])))
    return (
        mixed[None], gt[None], species, share(2), share(3), g_qkv, share(4), share(5), g_out, share(6),
        share(7), share(8), g_up, up_share, g_down, share(9),
    )


def solution(mesh):
    cells = P(("species", "dp"), None, None)
    scalars = P(("species", "dp"))
    in_specs = (cells, cells, scalars, scalars) + (P(),) * 14
    v, m = P("dp"), P("dp", None)
    out_specs = (cells, cells, P(None, "dp"), v, v, m, v, v, m, v, v, v, m, v, m, v)
    return jax.shard_map(
        partial(local, dp_size=mesh.shape["dp"]), mesh=mesh, in_specs=in_specs, out_specs=out_specs, check_vma=False
    )
```
